32 devices in a mesh: dp: 8 (over y, x, core), tensor: 4 (over z).
Axes of the slice: x: 2, y: 2, z: 4, core: 2. Of those that a mesh axis runs over, the one named last changes fastest.
Arguments:
- stream: bfloat16 [8192, 1536], P('dp'), may hold values from -6 to 6
- out_grad: bfloat16 [8192, 1536], P('dp'), may hold values from -6 to 6
- seq_lengths: int32 [8, 4], replicated, may hold values from 0 to 1024, as said below
- anchor: int32 [8192], P('dp'), may hold values from 0 to 8191, as said below
- norm_gain: float32 [1536], replicated, may hold values from 0.5 to 1.5
- w_z: bfloat16 [1536, 3072], P(None, 'tensor'), may hold values from -0.15625 to 0.15625
- w_x: bfloat16 [1536, 3072], P(None, 'tensor'), may hold values from -0.15625 to 0.15625
- w_bc: bfloat16 [1536, 256], replicated, may hold values from -0.15625 to 0.15625
- w_dt: bfloat16 [1536, 48], P(None, 'tensor'), may hold values from -0.15625 to 0.15625
- conv_x_w: float32 [4, 3072], P(None, 'tensor'), may hold values from -3 to 3
- conv_x_b: float32 [3072], P('tensor'), may hold values from -0.5 to 0.5
- conv_bc_w: float32 [4, 256], replicated, may hold values from -3 to 3
- conv_bc_b: float32 [256], replicated, may hold values from -0.5 to 0.5
- dt_bias: float32 [48], P('tensor'), may hold values from -10 to -3
- a_log: float32 [48], P('tensor'), may hold values from -1 to 2
- d_skip: float32 [48], P('tensor'), may hold values from 0.5 to 1.5
- gated_gain: float32 [3072], P('tensor'), may hold values from 0.5 to 1.5
- w_out: bfloat16 [3072, 1536], P('tensor'), may hold values from -0.109375 to 0.109375
Outputs:
- out_stream: bfloat16 [8192, 1536], P('dp', 'tensor')
- in_grad: bfloat16 [8192, 1536], P('dp', 'tensor')
- grad_norm_gain: float32 [1536], P('tensor')
- grad_w_z: float32 [1536, 3072], P('dp', 'tensor')
- grad_w_x: float32 [1536, 3072], P('dp', 'tensor')
- grad_w_bc: float32 [1536, 256], P('dp')
- grad_w_dt: float32 [1536, 48], P('dp', 'tensor')
- grad_conv_x_w: float32 [4, 3072], P(None, 'tensor')
- grad_conv_x_b: float32 [3072], P('tensor')
- grad_conv_bc_w: float32 [4, 256], replicated
- grad_conv_bc_b: float32 [256], replicated
- grad_dt_bias: float32 [48], P('tensor')
- grad_a_log: float32 [48], P('tensor')
- grad_d_skip: float32 [48], P('tensor')
- grad_gated_gain: float32 [3072], P('tensor')
- grad_w_out: float32 [3072, 1536], P('tensor', 'dp')
- rms_stats: float32 [3], replicated
The draws below stay inside these ranges and needn't reach their ends.
Inputs may be any that keep to these rules, and one draw needn't show every extreme that they name: `seq_lengths`: row g gives the lengths of the sequences packed in order from slot 0 of group g; zero entries are empty; a row sums to at most 1024 and the slots after its sum are padding; in every draw one row holds a single sequence of 1024 tokens. anchor is a permutation of 0 .. 8191; the 1024 slots of each group take exactly 128 tokens from each block of 1024 consecutive input positions.
All inputs are finite; a program needn't handle non-finite values.
Results may differ from the reference program's by a relative error of at most 0.018.
Values may be sent and summed in bfloat16 or wider, within the bound.
No kernel may reach another device: no remote copies, remote signals or barrier semaphores. Data moves between devices by JAX's collectives and lax.ppermute only.
A program may use at most 192 MiB of HBM per device.

```python
import jax
import jax.numpy as jnp
from jax import lax

D = 1536
INNER = 3072
HEADS = 48
HEADDIM = 64
STATE = 128
CONV = 4
SPAN = 256
TOK_DEV = 1024
SLOTS = 4
TOKENS = 8192
N_DP = 8
N_TENSOR = 4


def draw_seq_lengths(key, part):
    key_full, key_jitter, key_cuts = jax.random.split(key, 3)
    full_group = jax.random.randint(key_full, (), 0, N_DP)
    groups = jnp.arange(N_DP, dtype=jnp.int32)
    base_total = TOK_DEV // 3 + (TOK_DEV - TOK_DEV // 3) * groups // max(N_DP - 1, 1)
    jitter = jax.random.randint(key_jitter, (N_DP,), 1, TOK_DEV // 16 + 1)
    totals = base_total - jitter
    cut_points = jax.random.randint(key_cuts, (N_DP, SLOTS - 1), 0, totals[:, None] + 1)
    cut_points = jnp.sort(cut_points, axis=1)
    cut_edges = jnp.concatenate([jnp.zeros((N_DP, 1), jnp.int32), cut_points.astype(jnp.int32), totals[:, None].astype(jnp.int32)], axis=1)
    lengths = cut_edges[:, 1:] - cut_edges[:, :-1]
    full_row = jnp.zeros((SLOTS,), jnp.int32).at[0].set(TOK_DEV)
    lengths = jnp.where((groups == full_group)[:, None], full_row[None, :], lengths)
    return lengths.astype(jnp.int32)


def shuffle(one_key):
    return jax.random.permutation(one_key, TOK_DEV)


def draw_anchor(key, part):
    key_slots, key_rows = jax.random.split(key)
    per_peer = TOK_DEV // N_DP
    slot_perm = jax.vmap(shuffle)(jax.random.split(key_slots, N_DP)).astype(jnp.int32)
    row_perm = jax.vmap(shuffle)(jax.random.split(key_rows, N_DP)).astype(jnp.int32)
    source = slot_perm // per_peer
    rank_in = slot_perm % per_peer
    dest_group = jnp.arange(N_DP, dtype=jnp.int32)[:, None]
    local_row = row_perm[source, dest_group * per_peer + rank_in]
    return (source * TOK_DEV + local_row).reshape(-1).astype(jnp.int32)


def shard_levels(stream_key, dims, cuts, smallest, largest):
    factor_of, own = 1.0, jax.random.fold_in(stream_key, 6)
    for position, parts in cuts:
        steps = jnp.exp(jax.random.uniform(jax.random.fold_in(own, position), (parts,), jnp.float32, smallest / len(cuts), largest / len(cuts)))
        factor_of = factor_of * jnp.repeat(steps, dims[position] // parts).reshape([-1 if axis == position else 1 for axis in range(len(dims))])
    return factor_of


def gaussian(own_key, extent, width, bound, cuts=(), kind=jnp.bfloat16):
    loudness = shard_levels(own_key, extent, cuts, -0.22, 0.18) if cuts else 1.0
    entries = jax.random.normal(own_key, extent, jnp.float32) * width * loudness
    return jnp.minimum(jnp.maximum(entries, -bound), bound).astype(kind)


def setup_inputs(seed: int = 0) -> dict:
    key_of = jax.random.split(jax.random.key(seed), 19)
    return {
        "stream": gaussian(key_of[0], (TOKENS, D), 1.0, 6.0, ((0, 8),)),
        "out_grad": gaussian(key_of[1], (TOKENS, D), 1.0, 6.0, ((0, 8),)),
        "seq_lengths": draw_seq_lengths(jax.random.fold_in(key_of[18], 71), 0),
        "anchor": draw_anchor(jax.random.fold_in(key_of[18], 71), 0),
        "norm_gain": jnp.clip(1.0 + 0.1 * jax.random.normal(key_of[4], (D,), jnp.float32), 0.5, 1.5),
        "w_z": gaussian(key_of[5], (D, INNER), D ** -0.5, 0.15625, ((1, 4),)),
        "w_x": gaussian(key_of[6], (D, INNER), D ** -0.5, 0.15625, ((1, 4),)),
        "w_bc": gaussian(key_of[7], (D, 2 * STATE), D ** -0.5, 0.15625),
        "w_dt": gaussian(key_of[8], (D, HEADS), D ** -0.5, 0.15625, ((1, 4),)),
        "conv_x_w": gaussian(key_of[9], (CONV, INNER), CONV ** -0.5, 3.0, ((1, 4),), jnp.float32),
        "conv_x_b": jnp.clip(jax.random.uniform(key_of[10], (INNER,), jnp.float32, -0.5, 0.5) * shard_levels(key_of[10], (INNER,), ((0, 4),), -0.4, 0.0), -0.5, 0.5),
        "conv_bc_w": gaussian(key_of[11], (CONV, 2 * STATE), CONV ** -0.5, 3.0, (), jnp.float32),
        "conv_bc_b": jnp.clip(jax.random.uniform(key_of[12], (2 * STATE,), jnp.float32, -0.5, 0.5), -0.5, 0.5),
        "dt_bias": jnp.clip(-10.0 + 7.0 * jax.random.uniform(key_of[13], (HEADS,), jnp.float32) ** shard_levels(key_of[13], (HEADS,), ((0, 4),), -0.2, 0.2), -10.0, -3.0),
        "a_log": jnp.clip(-1.0 + 3.0 * jax.random.uniform(key_of[14], (HEADS,), jnp.float32) ** shard_levels(key_of[14], (HEADS,), ((0, 4),), -0.2, 0.2), -1.0, 2.0),
        "d_skip": jnp.clip(0.5 + 1.0 * jax.random.uniform(key_of[15], (HEADS,), jnp.float32) ** shard_levels(key_of[15], (HEADS,), ((0, 4),), -0.2, 0.2), 0.5, 1.5),
        "gated_gain": jnp.clip(1.0 + 0.1 * jax.random.normal(key_of[16], (INNER,), jnp.float32), 0.5, 1.5),
        "w_out": gaussian(key_of[17], (INNER, D), INNER ** -0.5, 0.109375, ((0, 4),)),
    }


EPSILON = 1e-05
HIGHEST = lax.Precision.HIGHEST

@jax.custom_vjp
def low(v):
    return lax.optimization_barrier(v.astype(jnp.bfloat16)).astype(jnp.float32)

@jax.custom_vjp
def low_back(v):
    return v

def low_keep(v):
    return (low(v), None)

def low_pass(kept, grad):
    return (grad,)

def back_keep(v):
    return (v, None)

def back_low(kept, grad):
    return (low(grad),)
low.defvjp(low_keep, low_pass)
low_back.defvjp(back_keep, back_low)

def product(left, right):
    return jnp.dot(left, right, precision=HIGHEST, preferred_element_type=jnp.float32)

def layout(my_lengths):
    seq_ends = jnp.cumsum(my_lengths, dtype=jnp.int32)
    positions = jnp.arange(TOK_DEV, dtype=jnp.int32)
    segment = lax.optimization_barrier(jnp.sum((seq_ends[None, :] <= positions[:, None]).astype(jnp.int32), axis=1, dtype=jnp.int32))
    valid_rows = (positions < seq_ends[-1]).astype(jnp.float32)
    return (segment, valid_rows)

def causal_conv(values, weight, conv_bias, segment):
    tap_count = weight.shape[0]
    conv_sum = conv_bias[None, :] + weight[tap_count - 1][None, :] * values
    for offset_back in range(1, tap_count):
        earlier = jnp.pad(values, ((offset_back, 0), (0, 0)))[:-offset_back]
        before = jnp.pad(segment, (offset_back, 0), constant_values=-1)[:-offset_back]
        same_seg = (before == segment).astype(jnp.float32)
        conv_sum = conv_sum + weight[tap_count - 1 - offset_back][None, :] * earlier * same_seg[:, None]
    return jax.nn.silu(conv_sum)

def state_scan(weighted, log_rates, b_rows, c_rows, segment, block_len):
    tok_len, head_count, head_size = weighted.shape
    block_count = tok_len // block_len
    state_size = b_rows.shape[1]
    blocks_u = weighted.reshape(block_count, block_len, head_count, head_size)
    cumulated = jnp.cumsum(log_rates.reshape(block_count, block_len, head_count), axis=1).transpose(0, 2, 1)
    seg_blocks = segment.reshape(block_count, block_len)
    seg_prior = jnp.concatenate([jnp.full((1,), -1, jnp.int32), seg_blocks[:-1, -1]])
    b_blocks = b_rows.reshape(block_count, block_len, state_size)
    c_blocks = c_rows.reshape(block_count, block_len, state_size)
    scores = jnp.einsum('cin,cjn->cij', c_blocks, b_blocks, precision=HIGHEST)
    within = jnp.arange(block_len, dtype=jnp.int32)
    same_seg = (seg_blocks[:, :, None] == seg_blocks[:, None, :]) & (within[:, None] >= within[None, :])[None]
    log_gaps = cumulated[:, :, :, None] - cumulated[:, :, None, :]
    decay_mat = jnp.where(same_seg[:, None], jnp.exp(jnp.where(same_seg[:, None], log_gaps, 0.0)), 0.0)
    intra_out = jnp.einsum('chij,cjhp->cihp', decay_mat * scores[:, None], blocks_u, precision=HIGHEST)
    last_cum = cumulated[:, :, -1:]
    tail_decay = jnp.exp(last_cum - cumulated) * (seg_blocks == seg_blocks[:, -1:])[:, None, :].astype(jnp.float32)
    states = jnp.einsum('chj,cjn,cjhp->chpn', tail_decay, b_blocks, blocks_u, precision=HIGHEST)
    carry_keep = jnp.exp(last_cum[:, :, 0]) * (seg_blocks[:, -1] == seg_prior)[:, None].astype(jnp.float32)

    def carry_step(carried, step_item):
        new_states, factor = step_item
        return (new_states + factor[:, None, None] * carried, carried)
    zero_state = jnp.zeros((head_count, head_size, state_size), jnp.float32)
    _, entering = lax.scan(carry_step, zero_state, (states, carry_keep))
    head_decay = jnp.exp(cumulated) * (seg_blocks == seg_prior[:, None])[:, None, :].astype(jnp.float32)
    inter_out = jnp.einsum('cin,chpn,chi->cihp', c_blocks, entering, head_decay, precision=HIGHEST)
    return (intra_out + inter_out).reshape(tok_len, head_count * head_size)

def block(x_in, segment, valid_rows, params):
    norm_gain, w_z, w_x, w_bc, w_dt, conv_x_w, conv_x_b, conv_bc_w, conv_bc_b, dt_bias, a_log, d_skip, gated_gain, w_out = params
    tok_len = x_in.shape[0]
    inverse_root_input = lax.rsqrt(lax.optimization_barrier(jnp.mean(x_in * x_in, axis=1, keepdims=True)) + EPSILON)
    normed = low(x_in * inverse_root_input * norm_gain[None, :])
    inner_part = INNER // N_TENSOR
    heads_part = HEADS // N_TENSOR
    z_parts = []
    x_parts = []
    dt_parts = []
    for share in range(N_TENSOR):
        copy_in = low_back(normed)
        inner_cols = slice(share * inner_part, (share + 1) * inner_part)
        head_cols = slice(share * heads_part, (share + 1) * heads_part)
        z_parts.append(low_back(product(copy_in, w_z[:, inner_cols])))
        x_parts.append(low_back(product(copy_in, w_x[:, inner_cols])))
        dt_parts.append(low_back(product(copy_in, w_dt[:, head_cols])))
    z_proj = jnp.concatenate(z_parts, axis=1)
    x_proj = jnp.concatenate(x_parts, axis=1)
    dt_proj = jnp.concatenate(dt_parts, axis=1)
    bc_proj = low_back(product(normed, w_bc))
    bc_conv = causal_conv(bc_proj, conv_bc_w, conv_bc_b, segment)
    conv_out = causal_conv(x_proj, conv_x_w, conv_x_b, segment)
    step_dt = jax.nn.softplus(dt_proj + dt_bias[None, :])
    decay_rates = -jnp.exp(a_log)
    weighted = conv_out.reshape(tok_len, HEADS, HEADDIM) * step_dt[:, :, None]
    ssm_out = state_scan(weighted, step_dt * decay_rates[None, :], bc_conv[:, :STATE], bc_conv[:, STATE:], segment, SPAN)
    ssm_out = ssm_out + jnp.repeat(d_skip, HEADDIM)[None, :] * conv_out
    gated_out = ssm_out * jax.nn.silu(z_proj)
    rstd_gate = lax.rsqrt(lax.optimization_barrier(jnp.mean(gated_out * gated_out, axis=1, keepdims=True)) + EPSILON)
    mixed_in = low(gated_out * rstd_gate * gated_gain[None, :])
    mix_sum = jnp.zeros((tok_len, D), jnp.float32)
    for share in range(N_TENSOR):
        inner_cols = slice(share * inner_part, (share + 1) * inner_part)
        mix_sum = mix_sum + low(product(mixed_in[:, inner_cols], w_out[inner_cols, :]))
    mix_sum = low_back(mix_sum)
    return (x_in + valid_rows[:, None] * mix_sum, mix_sum)

def reference(stream, out_grad, seq_lengths, anchor, norm_gain, w_z, w_x, w_bc, w_dt, conv_x_w, conv_x_b, conv_bc_w, conv_bc_b, dt_bias, a_log, d_skip, gated_gain, w_out):
    params = tuple((member.astype(jnp.float32) for member in (norm_gain, w_z, w_x, w_bc, w_dt, conv_x_w, conv_x_b, conv_bc_w, conv_bc_b, dt_bias, a_log, d_skip, gated_gain, w_out)))
    segments, valids = jax.vmap(layout)(seq_lengths)
    inverse = jnp.argsort(anchor).astype(jnp.int32)
    stream32 = stream.astype(jnp.float32)

    def forward(stream_in, weights):
        dealt = stream_in[anchor].reshape(N_DP, TOK_DEV, D)

        def group_step(carried, group_item):
            x_group, seg_group, valid_group = group_item
            out_group, mix_group = jax.checkpoint(block)(x_group, seg_group, valid_group, weights)
            return (carried, (out_group, mix_group))
        _, (outs_dealt, mixes) = lax.scan(group_step, jnp.zeros((), jnp.float32), (dealt, segments, valids))
        return (outs_dealt.reshape(TOKENS, D)[inverse], mixes)
    out_full, backward, mixes = jax.vjp(forward, stream32, params, has_aux=True)
    in_grad32, param_grads = backward(out_grad.astype(jnp.float32))
    out_stream = out_full.astype(jnp.bfloat16)
    in_grad = in_grad32.astype(jnp.bfloat16)
    dealt_x = stream32[anchor].reshape(N_DP, TOK_DEV, D)
    dealt_out = out_stream.astype(jnp.float32)[anchor].reshape(N_DP, TOK_DEV, D)
    row_weight = valids[:, :, None]
    square_sums = jnp.stack([jnp.sum(row_weight * dealt_x * dealt_x), jnp.sum(row_weight * mixes * mixes), jnp.sum(row_weight * dealt_out * dealt_out)])
    valid_count = jnp.sum(seq_lengths).astype(jnp.float32) * D
    rms_stats = jnp.sqrt(square_sums / valid_count)
    return (out_stream, in_grad, param_grads[0], param_grads[1], param_grads[2], param_grads[3], param_grads[4], param_grads[5], param_grads[6], param_grads[7], param_grads[8], param_grads[9], param_grads[10], param_grads[11], param_grads[12], param_grads[13], rms_stats)
```

```python
import functools

import jax
import jax.numpy as jnp
from jax import lax
from jax.experimental import pallas as pl
from jax.experimental.pallas import tpu as pltpu
from jax.sharding import PartitionSpec as P

SPAN = 256
EPSILON = 1e-05
LANES = 128
NEVER = -1e30
BF = jnp.bfloat16
F32 = jnp.float32
I32 = jnp.int32
MIB = 1 << 20


def dot(a, b):
    return jnp.dot(a, b, preferred_element_type=F32)


def dot_t(a, b):
    return lax.dot_general(a, b, (((1,), (1,)), ((), ())), preferred_element_type=F32)


def iota(shape, dim):
    return lax.broadcasted_iota(I32, shape, dim)


def split2(v):
    hi = v.astype(BF)
    return hi, (v - hi.astype(F32)).astype(BF)


def split3(v):
    hi = v.astype(BF)
    rest = v - hi.astype(F32)
    mid = rest.astype(BF)
    return hi, mid, (rest - mid.astype(F32)).astype(BF)


def params(mib=56, **more):
    return pltpu.CompilerParams(vmem_limit_bytes=mib * MIB, **more)


def whole(shape):
    rank = len(shape)
    return pl.BlockSpec(shape, lambda *_: (0,) * rank)


def index_kernel(per, src_ref, pos_row_ref, pos_col_ref, req_ref):
    n = src_ref.shape[1]
    rows = src_ref[...]
    cols = rows.T
    src_row, loc_row = rows[0:1], rows[1:2]
    src_col = cols[:, 0:1]
    member = (src_col == iota((n, LANES), 1).astype(F32)).astype(F32)
    member_t = (src_row == iota((LANES, n), 0).astype(F32)).astype(F32)
    before = (iota((n, n), 1) < iota((n, n), 0)).astype(F32).astype(BF)
    before_t = (iota((n, n), 0) < iota((n, n), 1)).astype(F32).astype(BF)
    rank = jnp.sum(dot(before, member.astype(BF)) * member, axis=1, keepdims=True)
    rank_t = jnp.sum(dot(member_t.astype(BF), before_t) * member_t, axis=0, keepdims=True)
    place = (src_col * per + rank).astype(I32)
    pos_col_ref[...] = place
    pos_row_ref[...] = (src_row * per + rank_t).astype(I32)
    onehot = (place == iota((n, n), 1)).astype(F32).astype(BF)
    high = jnp.floor(loc_row * (1.0 / 32.0))
    low = loc_row - high * 32.0
    pair = jnp.where(iota((8, n), 0) == 0, high, low).astype(BF)
    found = dot(pair, onehot)
    req_ref[...] = (found[0:1] * 32.0 + found[1:2]).astype(I32)


def find_places(anchor, n, per):
    src = (anchor // n).astype(F32)
    loc = (anchor % n).astype(F32)
    rows = jnp.concatenate([src[None], loc[None], jnp.zeros((6, n), F32)])
    return pl.pallas_call(
        functools.partial(index_kernel, per),
        out_shape=(
            jax.ShapeDtypeStruct((1, n), I32),
            jax.ShapeDtypeStruct((n, 1), I32),
            jax.ShapeDtypeStruct((1, n), I32),
        ),
        compiler_params=params(),
        name="places",
    )(rows)


def pick_kernel(idx_ref, data_ref, out_ref, hot_ref):
    n = idx_ref.shape[1]

    @pl.when(pl.program_id(0) == 0)
    def _():
        col = jnp.broadcast_to(idx_ref[...].astype(F32), (8, n)).T[:, 0:1].astype(I32)
        hot_ref[...] = (col == iota((n, n), 1)).astype(F32).astype(BF)

    out_ref[...] = dot(hot_ref[...], data_ref[...]).astype(BF)


def put_kernel(idx_ref, data_ref, out_ref, hot_ref):
    n = idx_ref.shape[1]

    @pl.when(pl.program_id(0) == 0)
    def _():
        hot_ref[...] = (idx_ref[...] == iota((n, n), 0)).astype(F32).astype(BF)

    out_ref[...] = dot(hot_ref[...], data_ref[...]).astype(BF)


def put_add_kernel(idx_ref, data_ref, base_ref, out_ref, hot_ref):
    n = idx_ref.shape[1]

    @pl.when(pl.program_id(0) == 0)
    def _():
        hot_ref[...] = (idx_ref[...] == iota((n, n), 0)).astype(F32).astype(BF)

    out_ref[...] = (base_ref[...].astype(F32) + dot(hot_ref[...], data_ref[...])).astype(BF)


def move_rows(kernel, idx, *data, name):
    n, width = data[0].shape
    tile = next((t for t in (384, 256) if width % t == 0), width)
    spec = pl.BlockSpec((n, tile), lambda i: (0, i))
    return pl.pallas_call(
        kernel,
        grid=(width // tile,),
        in_specs=[whole((1, n))] + [spec] * len(data),
        out_specs=spec,
        out_shape=jax.ShapeDtypeStruct((n, width), BF),
        scratch_shapes=[pltpu.VMEM((n, n), BF)],
        compiler_params=params(),
        cost_estimate=pl.CostEstimate(flops=2 * n * n * width, bytes_accessed=4 * n * width, transcendentals=0),
        name=name,
    )(idx, *data)


def seg_of(ends, place):
    seg = jnp.zeros(place.shape, I32)
    for end in ends:
        seg = seg + (place >= end).astype(I32)
    return jnp.where(place < 0, -1, seg)


def seg_scalar(ends, place):
    seg = jnp.int32(0)
    for end in ends:
        seg = seg + (place >= end).astype(I32)
    return jnp.where(place < 0, jnp.int32(-1), seg)


def softplus(v):
    e = jnp.exp(-jnp.abs(v))
    w = 1.0 + e
    one = w == 1.0
    log1p = jnp.where(one, e, jnp.log(w) * (e / jnp.where(one, 1.0, w - 1.0)))
    return jnp.maximum(v, 0.0) + log1p


def widen(parts, head_size, width):
    rows = parts[0].shape[0]
    spread = (iota((2 * LANES, width), 0) % LANES == iota((2 * LANES, width), 1) // head_size)
    spread = spread.astype(F32).astype(BF)
    stacked = jnp.concatenate([jnp.concatenate(split2(p), axis=1) for p in parts], axis=0)
    out = dot(stacked, spread)
    return [out[k * rows : (k + 1) * rows] for k in range(len(parts))]


def head_sums(v, head_size, split):
    rows, width = v.shape
    gather = (iota((width, LANES), 0) // head_size == iota((width, LANES), 1)).astype(F32).astype(BF)
    pieces = split(v)
    out = dot(jnp.concatenate(pieces, axis=0), gather)
    return sum(out[k * rows : (k + 1) * rows] for k in range(len(pieces)))


def fixed_sum(mask, v):
    out = dot(mask, jnp.concatenate(split3(v), axis=1))
    w = v.shape[1]
    return out[:, :w] + out[:, w : 2 * w] + out[:, 2 * w :]


def decays(ends, base, span, dt, rates):
    place = base + iota((span, 1), 0)
    seg_c = seg_of(ends, place)
    low = (iota((span, span), 0) >= iota((span, span), 1)).astype(F32).astype(BF)
    cum = fixed_sum(low, dt * rates)
    last = cum[span - 1 : span]
    seg_before = seg_scalar(ends, base - 1)
    seg_last = seg_scalar(ends, base + span - 1)
    head_decay = jnp.where(seg_c == seg_before, jnp.exp(cum), 0.0)
    tail_decay = jnp.where(seg_c == seg_last, jnp.exp(last - cum), 0.0)
    return cum, head_decay, tail_decay, seg_c, seg_last


def half_masks(group):
    lane = iota((1, LANES), 1)
    return [(lane // (LANES // group) == k).astype(F32) for k in range(group)]


def fwd_kernel(
    sizes, where_ref, gotx_ref, pos_ref, gain_ref, wz_ref, wx_ref, wbc_ref, wdt_ref, cxw_ref, cxb_ref,
    cbw_ref, cbb_ref, dtb_ref, rate_ref, skip_ref, ggain_ref, wout_ref,
    xd_ref, ht_ref, rin_ref, z_ref, xs_ref, px_ref, y_ref, bcv_ref, pbc_ref, dtr_ref, g_ref, stat_ref,
    state_out_ref, mix_ref,
    xext, bext, state,
):
    head_size, shares, slots = sizes
    span = pos_ref.shape[0]
    n = gotx_ref.shape[0]
    inner = wz_ref.shape[1]
    width = gotx_ref.shape[1]
    state_size = wbc_ref.shape[1] // 2
    taps = cxw_ref.shape[0]
    group = LANES // head_size
    step = pl.program_id(0)
    base = step * span
    ends = [where_ref[k] for k in range(slots)]
    tensor = where_ref[slots]

    @pl.when(step == 0)
    def _():
        xext[0:8] = jnp.zeros((8, inner), F32)
        bext[0:8] = jnp.zeros((8, 2 * state_size), F32)
        state[...] = jnp.zeros_like(state)

    onehot = (pos_ref[...] == iota((span, n), 1)).astype(F32).astype(BF)
    x = dot(onehot, gotx_ref[...])
    xd_ref[...] = x.astype(BF)
    r_in = lax.rsqrt(jnp.sum(x * x, axis=1, keepdims=True) * (1.0 / width) + EPSILON)
    rin_ref[...] = r_in
    h = (x * r_in * gain_ref[...]).astype(BF)
    ht_ref[...] = h.T
    z = dot(h, wz_ref[...])
    z_ref[...] = z
    xs = dot(h, wx_ref[...])
    bc = dot(h, wbc_ref[...])
    dtr = dot(h, wdt_ref[...])
    dtr_ref[...] = dtr
    xs_ref[...] = xs.astype(BF)
    bcv_ref[...] = bc.astype(BF)

    place = base + iota((span, 1), 0)
    seg_here = seg_of(ends, place)
    xext[8 : 8 + span] = xs
    bext[8 : 8 + span] = bc
    px = cxb_ref[...] + cxw_ref[taps - 1 : taps] * xs
    pbc = cbb_ref[...] + cbw_ref[taps - 1 : taps] * bc
    for k in range(1, taps):
        same = (seg_of(ends, place - k) == seg_here).astype(F32)
        px = px + cxw_ref[taps - 1 - k : taps - k] * (xext[8 - k : 8 - k + span] * same)
        pbc = pbc + cbw_ref[taps - 1 - k : taps - k] * (bext[8 - k : 8 - k + span] * same)
    xext[0:8] = xs[span - 8 :]
    bext[0:8] = bc[span - 8 :]
    px_ref[...] = px
    pbc_ref[...] = pbc
    u = px * jax.nn.sigmoid(px)
    bcc = pbc * jax.nn.sigmoid(pbc)
    b_rows = bcc[:, :state_size].astype(BF)
    c_rows = bcc[:, state_size:].astype(BF)

    dt = softplus(dtr + dtb_ref[...])
    cum, head_decay, tail_decay, seg_c, _ = decays(ends, base, span, dt, rate_ref[...])
    cum_t = cum.T
    dt_w, head_w, tail_w = widen([dt, head_decay, tail_decay], head_size, inner)
    udt = u * dt_w
    seg_r = seg_of(ends, base + iota((1, span), 1))
    counts = (seg_c == seg_r) & (iota((span, span), 0) >= iota((span, span), 1))
    never = jnp.where(counts, 0.0, NEVER)
    scores = dot_t(c_rows, b_rows)
    entering = state[...]
    state_out_ref[0] = entering
    masks = half_masks(group)
    pieces = []
    for tile in range(inner // LANES):
        lanes = slice(tile * LANES, (tile + 1) * LANES)
        block = udt[:, lanes]
        total = None
        for k in range(group):
            head = tile * group + k
            decay = jnp.exp(cum[:, head : head + 1] - cum_t[head : head + 1, :] + never)
            term = dot((decay * scores).astype(BF), (block * masks[k]).astype(BF))
            total = term if total is None else total + term
        pieces.append(total)
    y = jnp.concatenate(pieces, axis=1)
    y = y + dot(c_rows, entering.astype(BF)) * head_w
    y = y + skip_ref[...] * u
    y_ref[...] = y
    b_t = bcc[:, :state_size].T.astype(BF)
    state[...] = head_w[span - 1 : span] * entering + dot(b_t, (udt * tail_w).astype(BF))
    gated = y * (z * jax.nn.sigmoid(z))
    squares = jnp.sum(gated * gated, axis=1, keepdims=True)
    stat_ref[0] = jnp.broadcast_to(squares, (span, LANES)).T[0:8]
    g = (gated * ggain_ref[...]).astype(BF)
    g_ref[...] = g
    mix = dot(g, wout_ref[...]).astype(BF)
    cols = width // shares
    for j in range(shares):
        mix_ref[tensor ^ j] = mix[:, j * cols : (j + 1) * cols]


def run_fwd(where, sizes, gotx, pos, vectors, weights):
    head_size, shares, slots = sizes
    n, width = gotx.shape
    gain, cxw, cxb, cbw, cbb, dtb, rate, skip, ggain = vectors
    w_z, w_x, w_bc, w_dt, w_out = weights
    inner = w_z.shape[1]
    two = w_bc.shape[1]
    span = SPAN
    steps = n // span

    def rows(cols):
        return pl.BlockSpec((span, cols), lambda i, *_: (i, 0))

    ops = [gotx, pos, gain, w_z, w_x, w_bc, w_dt, cxw, cxb, cbw, cbb, dtb, rate, skip, ggain, w_out]
    specs = [whole(o.shape) for o in ops]
    specs[1] = rows(1)
    cols = width // shares
    outs = [
        ((n, width), BF, rows(width)),
        ((width, n), BF, pl.BlockSpec((width, span), lambda i, *_: (0, i))),
        ((n, 1), F32, rows(1)),
        ((n, inner), F32, rows(inner)),
        ((n, inner), BF, rows(inner)),
        ((n, inner), F32, rows(inner)),
        ((n, inner), F32, rows(inner)),
        ((n, two), BF, rows(two)),
        ((n, two), F32, rows(two)),
        ((n, LANES), F32, rows(LANES)),
        ((n, inner), BF, rows(inner)),
        ((steps, 8, span), F32, pl.BlockSpec((1, 8, span), lambda i, *_: (i, 0, 0))),
        ((steps, two // 2, inner), F32, pl.BlockSpec((1, two // 2, inner), lambda i, *_: (i, 0, 0))),
        ((shares, n, cols), BF, pl.BlockSpec((shares, span, cols), lambda i, *_: (0, i, 0))),
    ]
    return pl.pallas_call(
        functools.partial(fwd_kernel, sizes),
        grid_spec=pltpu.PrefetchScalarGridSpec(
            num_scalar_prefetch=1,
            grid=(steps,),
            in_specs=specs,
            out_specs=[o[2] for o in outs],
            scratch_shapes=[
                pltpu.VMEM((span + 8, inner), F32),
                pltpu.VMEM((span + 8, two), F32),
                pltpu.VMEM((two // 2, inner), F32),
            ],
        ),
        out_shape=[jax.ShapeDtypeStruct(o[0], o[1]) for o in outs],
        compiler_params=params(),
        cost_estimate=pl.CostEstimate(flops=2 * n * width * (4 * inner), bytes_accessed=40 * MIB, transcendentals=0),
        name="forward",
    )(where, *ops)


def dots_kernel(slots, where_ref, pos_ref, dyn_ref, g_ref, stat_ref, out_ref, stat_out_ref):
    span = pos_ref.shape[0]
    n = dyn_ref.shape[0]
    base = pl.program_id(0) * span
    onehot = (pos_ref[...] == iota((span, n), 1)) & (base + iota((span, 1), 0) < where_ref[slots - 1])
    dyn = dot(onehot.astype(F32).astype(BF), dyn_ref[...])
    out_ref[...] = dyn.astype(BF)
    inner_dot = jnp.sum(dyn * g_ref[...].astype(F32), axis=1, keepdims=True)
    as_row = jnp.broadcast_to(inner_dot, (span, LANES)).T[0:8]
    stat_out_ref[0] = jnp.where(iota((8, span), 0) == 0, stat_ref[0], as_row)


def run_dots(where, slots, pos, got_dyn, g, stat):
    n, inner = got_dyn.shape
    span = SPAN
    rows = pl.BlockSpec((span, inner), lambda i, *_: (i, 0))
    stats = pl.BlockSpec((1, 8, span), lambda i, *_: (i, 0, 0))
    return pl.pallas_call(
        functools.partial(dots_kernel, slots),
        grid_spec=pltpu.PrefetchScalarGridSpec(
            num_scalar_prefetch=1,
            grid=(n // span,),
            in_specs=[pl.BlockSpec((span, 1), lambda i, *_: (i, 0)), whole((n, inner)), rows, stats],
            out_specs=[rows, stats],
        ),
        out_shape=[jax.ShapeDtypeStruct((n, inner), BF), jax.ShapeDtypeStruct(stat.shape, F32)],
        compiler_params=params(),
        cost_estimate=pl.CostEstimate(flops=2 * n * n * inner, bytes_accessed=6 * MIB, transcendentals=0),
        name="row_dots",
    )(where, pos, got_dyn, g, stat)


def bwd_kernel(
    sizes, where_ref, stat_ref, dyn_ref, z_ref, xs_ref, px_ref, y_ref, bcv_ref, pbc_ref, dtr_ref, xd_ref,
    rin_ref, state_ref, gain_ref, wz_ref, wx_ref, wbc_ref, wdt_ref, cxw_ref, cbw_ref, dtb_ref, rate_ref,
    skip_ref, ggain_ref,
    back_ref, dz_ref, late_ref, yn_ref, dots_ref, accx_ref, accb_ref, acch_ref, accd_ref,
    xext, bext, dstate, across,
):
    head_size, shares, slots = sizes
    span, inner = z_ref.shape
    width = xd_ref.shape[1]
    two = pbc_ref.shape[1]
    state_size = two // 2
    taps = cxw_ref.shape[0]
    group = LANES // head_size
    units = inner * shares
    steps = pl.num_programs(0)
    step = pl.program_id(0)
    base = (steps - 1 - step) * span
    ends = [where_ref[k] for k in range(slots)]
    tensor = where_ref[slots]

    @pl.when(step == 0)
    def _():
        xext[span : span + 8] = jnp.zeros((8, inner), F32)
        bext[span : span + 8] = jnp.zeros((8, two), F32)
        dstate[...] = jnp.zeros_like(dstate)
        across[...] = jnp.zeros_like(across)
        accx_ref[...] = jnp.zeros_like(accx_ref)
        accb_ref[...] = jnp.zeros_like(accb_ref)
        acch_ref[...] = jnp.zeros_like(acch_ref)
        accd_ref[...] = jnp.zeros_like(accd_ref)

    def add_row(ref, row, value):
        ref[row : row + 1] += jnp.sum(value, axis=0, keepdims=True)

    place = base + iota((span, 1), 0)
    stat_cols = stat_ref[0].T
    r_g = lax.rsqrt(stat_cols[:, 0:1] * (1.0 / units) + EPSILON)
    row_dot = stat_cols[:, 1:2] * (1.0 / units)
    z = z_ref[...]
    y = y_ref[...]
    dyn = dyn_ref[...].astype(F32)
    sig_z = jax.nn.sigmoid(z)
    silu_z = z * sig_z
    gated = y * silu_z
    normed = gated * r_g
    d_gated = r_g * (dyn * ggain_ref[...]) - normed * (r_g * r_g * row_dot)
    d_y = d_gated * silu_z
    dz = (d_gated * y * (sig_z * (1.0 + z * (1.0 - sig_z)))).astype(BF)
    dz_ref[...] = dz
    valid = (place < ends[slots - 1]).astype(F32)
    yn_ref[...] = (normed * ggain_ref[...] * valid).astype(BF)
    add_row(accx_ref, taps + 2, dyn * normed)

    px = px_ref[...]
    sig_x = jax.nn.sigmoid(px)
    u = px * sig_x
    pbc = pbc_ref[...]
    sig_bc = jax.nn.sigmoid(pbc)
    bcc = pbc * sig_bc
    b_rows = bcc[:, :state_size].astype(BF)
    c_rows = bcc[:, state_size:].astype(BF)
    add_row(accx_ref, taps + 1, u * d_y)

    pre = dtr_ref[...] + dtb_ref[...]
    dt = softplus(pre)
    rates = rate_ref[...]
    cum, head_decay, tail_decay, seg_c, seg_last = decays(ends, base, span, dt, rates)
    cum_t = cum.T
    dt_w, head_w, tail_w = widen([dt, head_decay, tail_decay], head_size, inner)
    udt = u * dt_w
    seg_r = seg_of(ends, base + iota((1, span), 1))
    counts = (seg_c == seg_r) & (iota((span, span), 1) >= iota((span, span), 0))
    never = jnp.where(counts, 0.0, NEVER)
    scores = dot_t(b_rows, c_rows)
    d_scores = jnp.zeros((span, span), F32)
    masks = half_masks(group)
    pieces = []
    for tile in range(inner // LANES):
        lanes = slice(tile * LANES, (tile + 1) * LANES)
        udt_block = udt[:, lanes]
        dy_block = d_y[:, lanes]
        dy_low = dy_block.astype(BF)
        total = None
        for k in range(group):
            head = tile * group + k
            decay = jnp.exp(cum_t[head : head + 1, :] - cum[:, head : head + 1] + never)
            d_scores = d_scores + decay * dot_t((udt_block * masks[k]).astype(BF), dy_low)
            term = dot((decay * scores).astype(BF), (dy_block * masks[k]).astype(BF))
            total = term if total is None else total + term
        pieces.append(total)
    in_block = jnp.concatenate(pieces, axis=1)
    d_state = dstate[...]
    d_state_low = d_state.astype(BF)
    entering = state_ref[0]
    entering_low = entering.astype(BF)
    at_end = dot(b_rows, d_state_low)
    at_start = dot(c_rows, entering_low)
    d_udt = in_block + at_end * tail_w
    from_start = (d_y * head_w).astype(BF)
    to_end = (udt * tail_w).astype(BF)
    d_c = dot(d_scores.T.astype(BF), b_rows) + dot_t(from_start, entering_low)
    d_b = dot(d_scores.astype(BF), c_rows) + dot_t(to_end, d_state_low)
    y_block = y - skip_ref[...] * u - at_start * head_w
    balance = d_y.astype(BF).astype(F32) * y_block - udt.astype(BF).astype(F32) * in_block
    balance = balance + from_start.astype(F32) * at_start - to_end.astype(F32) * at_end
    v_part = head_sums(u * d_udt, head_size, split2)
    mask_low = counts.astype(F32).astype(BF)
    d_la = fixed_sum(mask_low, head_sums(balance, head_size, split3))
    d_la = d_la + jnp.where(seg_c == seg_last, across[0:1], 0.0)
    d_dt = v_part + rates * d_la
    d_pre = d_dt * jax.nn.sigmoid(pre)
    add_row(acch_ref, 0, d_la * dt * rates)
    add_row(acch_ref, 1, d_pre)

    c_t = bcc[:, state_size:].T.astype(BF)
    d_enter = dot(c_t, from_start) + head_w[span - 1 : span] * d_state
    dstate[...] = d_enter
    crossing = jnp.sum(d_enter.astype(BF).astype(F32) * entering, axis=0, keepdims=True)
    across[...] = head_sums(jnp.broadcast_to(crossing, (8, inner)), head_size, split3)

    d_u = skip_ref[...] * d_y + dt_w * d_udt
    d_px = d_u * (sig_x * (1.0 + px * (1.0 - sig_x)))
    d_pbc = jnp.concatenate([d_b, d_c], axis=1) * (sig_bc * (1.0 + pbc * (1.0 - sig_bc)))
    xext[0:span] = d_px
    bext[0:span] = d_pbc
    seg_here = seg_of(ends, place)
    xs = xs_ref[...].astype(F32)
    bcv = bcv_ref[...].astype(F32)
    d_xs = cxw_ref[taps - 1 : taps] * d_px
    d_bc = cbw_ref[taps - 1 : taps] * d_pbc
    add_row(accx_ref, taps, d_px)
    add_row(accb_ref, taps, d_pbc)
    add_row(accx_ref, taps - 1, d_px * xs)
    add_row(accb_ref, taps - 1, d_pbc * bcv)
    for k in range(1, taps):
        later = place + k
        same = ((seg_of(ends, later) == seg_here) & (later < steps * span)).astype(F32)
        tap = taps - 1 - k
        xk = xext[k : k + span] * same
        bk = bext[k : k + span] * same
        d_xs = d_xs + cxw_ref[tap : tap + 1] * xk
        d_bc = d_bc + cbw_ref[tap : tap + 1] * bk
        add_row(accx_ref, tap, xk * xs)
        add_row(accb_ref, tap, bk * bcv)
    xext[span : span + 8] = d_px[0:8]
    bext[span : span + 8] = d_pbc[0:8]
    dx_low = d_xs.astype(BF)
    dbc_low = d_bc.astype(BF)
    ddt_low = d_pre.astype(BF)
    late_ref[:, 0:inner] = dx_low
    late_ref[:, inner : inner + two] = dbc_low
    late_ref[:, inner + two : inner + two + LANES] = ddt_low
    back = dot_t(dz, wz_ref[...]) + dot_t(dx_low, wx_ref[...])
    back = back + dot_t(ddt_low, wdt_ref[...]) + dot_t(dbc_low, wbc_ref[...])
    x_hat = xd_ref[...].astype(F32) * rin_ref[...]
    shared = back * x_hat
    add_row(accd_ref, 0, shared)
    inner_dot = jnp.sum(shared * gain_ref[...], axis=1, keepdims=True)
    dots_ref[0] = jnp.broadcast_to(inner_dot, (span, LANES)).T[0:8]
    low = back.astype(BF)
    cols = width // shares
    for j in range(shares):
        back_ref[tensor ^ j] = low[:, j * cols : (j + 1) * cols]


def run_bwd(where, sizes, stat, dyn, kept, vectors, weights):
    head_size, shares, slots = sizes
    z, xs, px, y, bcv, pbc, dtr, xd, rin, states = kept
    gain, cxw, cbw, dtb, rate, skip, ggain = vectors
    w_z, w_x, w_bc, w_dt = weights
    n, inner = z.shape
    width = xd.shape[1]
    two = pbc.shape[1]
    span = SPAN
    steps = n // span
    cols = width // shares

    def rows(c):
        return pl.BlockSpec((span, c), lambda i, *_: (steps - 1 - i, 0))

    stats = pl.BlockSpec((1, 8, span), lambda i, *_: (steps - 1 - i, 0, 0))
    ops = [stat, dyn, z, xs, px, y, bcv, pbc, dtr, xd, rin, states]
    specs = [stats, *(rows(o.shape[1]) for o in ops[1:11])]
    specs.append(pl.BlockSpec((1, two // 2, inner), lambda i, *_: (steps - 1 - i, 0, 0)))
    fixed = [gain, w_z, w_x, w_bc, w_dt, cxw, cbw, dtb, rate, skip, ggain]
    outs = [
        ((shares, n, cols), BF, pl.BlockSpec((shares, span, cols), lambda i, *_: (0, steps - 1 - i, 0))),
        ((n, inner), BF, rows(inner)),
        ((n, inner + two + LANES), BF, rows(inner + two + LANES)),
        ((n, inner), BF, rows(inner)),
        ((steps, 8, span), F32, stats),
        ((8, inner), F32, whole((8, inner))),
        ((8, two), F32, whole((8, two))),
        ((8, LANES), F32, whole((8, LANES))),
        ((8, width), F32, whole((8, width))),
    ]
    return pl.pallas_call(
        functools.partial(bwd_kernel, sizes),
        grid_spec=pltpu.PrefetchScalarGridSpec(
            num_scalar_prefetch=1,
            grid=(steps,),
            in_specs=specs + [whole(o.shape) for o in fixed],
            out_specs=[o[2] for o in outs],
            scratch_shapes=[
                pltpu.VMEM((span + 8, inner), F32),
                pltpu.VMEM((span + 8, two), F32),
                pltpu.VMEM((two // 2, inner), F32),
                pltpu.VMEM((8, LANES), F32),
            ],
        ),
        out_shape=[jax.ShapeDtypeStruct(o[0], o[1]) for o in outs],
        compiler_params=params(),
        cost_estimate=pl.CostEstimate(flops=2 * n * width * (4 * inner), bytes_accessed=40 * MIB, transcendentals=0),
        name="backward",
    )(where, *ops, *fixed)


def outer_kernel(groups, where_ref, left_ref, right_ref, out_ref):
    width, n = left_ref.shape
    rows = width // groups
    low = dot(left_ref[...], right_ref[...]).astype(BF)
    for i in range(groups):
        out_ref[where_ref[0] ^ i] = low[i * rows : (i + 1) * rows]


def outer(me, groups, left_t, right, first, count):
    width, n = left_t.shape
    tile = next(t for t in (256, 128) if count % t == 0 and first % t == 0)
    rows = width // groups
    return pl.pallas_call(
        functools.partial(outer_kernel, groups),
        grid_spec=pltpu.PrefetchScalarGridSpec(
            num_scalar_prefetch=1,
            grid=(count // tile,),
            in_specs=[
                whole((width, n)),
                pl.BlockSpec((n, tile), lambda i, *_: (0, first // tile + i)),
            ],
            out_specs=pl.BlockSpec((groups, rows, tile), lambda i, *_: (0, 0, i)),
        ),
        out_shape=jax.ShapeDtypeStruct((groups, rows, count), BF),
        compiler_params=params(),
        cost_estimate=pl.CostEstimate(flops=2 * n * width * count, bytes_accessed=8 * MIB, transcendentals=0),
        name="outer",
    )(me, left_t, right)


def swap(v, axis, bit):
    size = lax.axis_size(axis)
    return lax.ppermute(v, axis, [(i, i ^ (1 << bit)) for i in range(size)])


def bits_of(axis):
    return lax.axis_size(axis).bit_length() - 1


def halve(v, axis, order):
    count = len(order)
    shape = v.shape[1:]
    v = v.reshape((2,) * count + shape)
    left = list(range(count - 1, -1, -1))
    for at, bit in enumerate(order):
        dim = left.index(bit)
        sent = lax.index_in_dim(v, 1, dim, keepdims=False)
        kept = lax.index_in_dim(v, 0, dim, keepdims=False)
        left.pop(dim)
        got = swap(sent, axis, bit)
        v = kept.astype(F32) + got.astype(F32)
        if at < count - 1:
            v = v.astype(BF)
    return v.reshape(shape)


def sum_all(v, axis):
    for bit in range(bits_of(axis)):
        v = v + swap(v, axis, bit)
    return v


def exchange(v, axis):
    groups = lax.axis_size(axis)
    rows = v.shape[0]
    parts = v.reshape((groups, rows // groups) + v.shape[1:])
    return lax.all_to_all(parts, axis, split_axis=0, concat_axis=0, tiled=True).reshape(v.shape)


def pad_lanes(v):
    return jnp.pad(v, [(0, 0)] * (v.ndim - 1) + [(0, LANES - v.shape[-1])])


def local(
    stream, out_grad, seq_lengths, anchor, norm_gain, w_z, w_x, w_bc, w_dt, conv_x_w, conv_x_b, conv_bc_w,
    conv_bc_b, dt_bias, a_log, d_skip, gated_gain, w_out,
):
    groups = lax.axis_size("dp")
    shares = lax.axis_size("tensor")
    me = lax.axis_index("dp")
    tensor = lax.axis_index("tensor")
    n, width = stream.shape
    per = n // groups
    cols = width // shares
    first_col = tensor * cols
    inner = w_z.shape[1]
    heads = w_dt.shape[1]
    head_size = inner // heads
    two = w_bc.shape[1]
    slots = seq_lengths.shape[1]
    taps = conv_x_w.shape[0]
    sizes = (head_size, shares, slots)

    my_lengths = lax.dynamic_index_in_dim(seq_lengths, me, 0, keepdims=False)
    ends = [my_lengths[0]]
    for k in range(1, slots):
        ends.append(ends[-1] + my_lengths[k])
    where = jnp.stack([*ends, tensor]).astype(I32)
    me_arr = jnp.stack([me, me]).astype(I32)

    pos_row, pos_col, requests = find_places(anchor, n, per)
    wanted = lax.all_to_all(
        requests.reshape(groups, per), "dp", split_axis=0, concat_axis=0, tiled=True
    ).reshape(1, n)
    x_send = move_rows(pick_kernel, wanted, stream, name="pick_x")
    got_x = exchange(x_send, "dp")
    d_yn_src = jnp.einsum("td,id->ti", out_grad, w_out, preferred_element_type=F32).astype(BF)
    got_dyn = exchange(move_rows(pick_kernel, wanted, d_yn_src, name="pick_dyn"), "dp")

    gain = norm_gain[None]
    w_dt_pad = pad_lanes(w_dt)
    dtb = pad_lanes(dt_bias[None])
    rate = pad_lanes(-jnp.exp(a_log)[None])
    skip = jnp.repeat(d_skip, head_size)[None]
    ggain = gated_gain[None]
    vectors = (gain, conv_x_w, conv_x_b[None], conv_bc_w, conv_bc_b[None], dtb, rate, skip, ggain)
    (xd, h_t, rin, z, xs, px, y, bcv, pbc, dtr, g, stat, states, mix_parts) = run_fwd(
        where, sizes, got_x, pos_col, vectors, (w_z, w_x, w_bc, w_dt_pad, w_out)
    )
    dyn, stat = run_dots(where, slots, pos_col, got_dyn, g, stat)
    stat = sum_all(stat, "tensor")

    kept = (z, xs, px, y, bcv, pbc, dtr, xd, rin, states)
    back_parts, dz, late, yn, in_dots, acc_x, acc_b, acc_h, acc_d = run_bwd(
        where, sizes, stat, dyn, kept, (gain, conv_x_w, conv_bc_w, dtb, rate, skip, ggain), (w_z, w_x, w_bc, w_dt_pad)
    )
    tensor_order = list(range(bits_of("tensor")))
    dp_bits = bits_of("dp")
    order_a = list(range(dp_bits))
    order_b = order_a[:1] + order_a[1:][::-1]

    seq_place = jnp.arange(n, dtype=I32)
    valid = (seq_place < ends[-1]).astype(F32)[:, None]
    r_g = lax.rsqrt(stat[:, 0, :].reshape(n, 1) * (1.0 / (inner * shares)) + EPSILON)
    mix = halve(mix_parts, "tensor", tensor_order) * r_g
    x_cols = lax.dynamic_slice_in_dim(xd, first_col, cols, 1).astype(F32)
    out_cols = (x_cols + valid * mix).astype(BF)
    out_float = out_cols.astype(F32)
    squares = jnp.stack(
        [jnp.sum(valid * x_cols * x_cols), jnp.sum(valid * mix * mix), jnp.sum(valid * out_float * out_float)]
    )
    out_back = exchange(move_rows(put_kernel, pos_row, out_cols, name="put_out"), "dp")
    out_final = move_rows(put_kernel, wanted, out_back, name="place_out")

    yn_src = move_rows(
        put_kernel, wanted, exchange(move_rows(put_kernel, pos_row, yn, name="put_yn"), "dp"), name="place_yn"
    )
    g_z = halve(outer(me_arr, groups, h_t, dz, 0, inner), "dp", order_a)
    g_out = halve(outer(me_arr, groups, out_grad.T, yn_src, 0, inner), "dp", order_b)

    in_dots = sum_all(in_dots, "tensor")[:, 0, :].reshape(n, 1)
    d_h = halve(back_parts, "tensor", tensor_order)
    gain_cols = lax.dynamic_slice_in_dim(norm_gain, first_col, cols, 0)
    x_hat = x_cols * rin
    dx_cols = (rin * (d_h * gain_cols[None] - x_hat * (in_dots * (1.0 / width)))).astype(BF)
    dx_back = exchange(move_rows(put_kernel, pos_row, dx_cols, name="put_dx"), "dp")
    dy_cols = lax.dynamic_slice_in_dim(out_grad, first_col, cols, 1)
    dx_final = move_rows(put_add_kernel, wanted, dx_back, dy_cols, name="place_dx")

    split = inner - LANES
    g_late_a = halve(outer(me_arr, groups, h_t, late, 0, split), "dp", order_a)
    g_late_b = halve(outer(me_arr, groups, h_t, late, split, LANES + two + LANES), "dp", order_b)
    g_x = jnp.concatenate([g_late_a, g_late_b[:, :LANES]], axis=1)
    g_bc = sum_all(g_late_b[:, LANES : LANES + two], "tensor")
    g_dt = g_late_b[:, LANES + two : LANES + two + heads]

    parts = [acc_x, acc_h, acc_b[: taps + 1], acc_d[0:1], squares]
    flat = [p.reshape(-1) for p in parts]
    lens = [f.shape[0] for f in flat]
    total = sum(lens)
    packed = jnp.pad(jnp.concatenate(flat), (0, -total % 1024)).reshape(-1, LANES)
    packed = sum_all(packed, "dp").reshape(-1)
    own_len = lens[0] + lens[1]
    both = jnp.pad(packed[own_len:], (0, own_len % 1024)).reshape(-1, LANES)
    both = sum_all(both, "tensor").reshape(-1)
    s_x = packed[: lens[0]].reshape(acc_x.shape)
    s_h = packed[lens[0] : own_len].reshape(acc_h.shape)
    s_b = both[: lens[2]].reshape(taps + 1, two)
    s_d = both[lens[2] : lens[2] + lens[3]]
    s_sq = both[lens[2] + lens[3] : lens[2] + lens[3] + lens[4]]
    g_gain = lax.dynamic_slice_in_dim(s_d, first_col, cols, 0)
    rms = jnp.sqrt(s_sq / (jnp.sum(seq_lengths).astype(F32) * width))
    g_skip = jnp.sum(s_x[taps + 1].reshape(heads, head_size), axis=1)
    return (
        out_final, dx_final, g_gain, g_z, g_x, g_bc, g_dt, s_x[:taps], s_x[taps], s_b[:taps], s_b[taps],
        s_h[1, :heads], s_h[0, :heads], g_skip, s_x[taps + 2], g_out.T, rms,
    )


def solution(mesh):
    in_specs = (
        P("dp", None), P("dp", None), P(), P("dp"), P(), P(None, "tensor"), P(None, "tensor"), P(),
        P(None, "tensor"), P(None, "tensor"), P("tensor"), P(), P(), P("tensor"), P("tensor"), P("tensor"),
        P("tensor"), P("tensor", None),
    )
    out_specs = (
        P("dp", "tensor"), P("dp", "tensor"), P("tensor"), P("dp", "tensor"), P("dp", "tensor"), P("dp", None),
        P("dp", "tensor"), P(None, "tensor"), P("tensor"), P(), P(), P("tensor"), P("tensor"), P("tensor"),
        P("tensor"), P("tensor", "dp"), P(),
    )
    return jax.shard_map(local, mesh=mesh, in_specs=in_specs, out_specs=out_specs, check_vma=False)
```

```python
import functools

import jax
import jax.numpy as jnp
from jax import lax
from jax.experimental import pallas as pl
from jax.experimental.pallas import tpu as pltpu
from jax.sharding import PartitionSpec as P

SPAN = 256
EPSILON = 1e-05
LANES = 128
NEVER = -1e30
BF = jnp.bfloat16
F32 = jnp.float32
I32 = jnp.int32
MIB = 1 << 20
EXTRA = 16
FORWARD = ((0, 2), (2, 4))
BACKWARD = ((2, 4), (0, 2))


def dot(a, b):
    return jnp.dot(a, b, preferred_element_type=F32)


def dot_t(a, b):
    return lax.dot_general(a, b, (((1,), (1,)), ((), ())), preferred_element_type=F32)


def iota(shape, dim):
    return lax.broadcasted_iota(I32, shape, dim)


def split2(v):
    hi = v.astype(BF)
    return hi, (v - hi.astype(F32)).astype(BF)


def split3(v):
    hi = v.astype(BF)
    rest = v - hi.astype(F32)
    mid = rest.astype(BF)
    return hi, mid, (rest - mid.astype(F32)).astype(BF)


def params(mib=56, **more):
    return pltpu.CompilerParams(vmem_limit_bytes=mib * MIB, **more)


def whole(shape):
    rank = len(shape)
    return pl.BlockSpec(shape, lambda *_: (0,) * rank)


def call(kernel, ins, in_specs, outs, name, grid=(1,), scalars=(), deps=(), scratch=(), flops=0, keep=(), mib=56):
    n_scalars, n_in, n_extra = len(scalars), len(ins), len(keep) + len(deps)

    def body(*refs):
        kernel(*refs[: n_scalars + n_in], *refs[n_scalars + n_in + n_extra :])

    extra = [a for _, a in keep] + list(deps)
    first = n_scalars + n_in
    moved = sum(a.size * a.dtype.itemsize for a in ins) + sum(
        functools.reduce(lambda p, q: p * q, o[0]) * 2 for o in outs
    )
    return pl.pallas_call(
        body,
        grid_spec=pltpu.PrefetchScalarGridSpec(
            num_scalar_prefetch=n_scalars,
            grid=grid,
            in_specs=[*in_specs, *(pl.BlockSpec(memory_space=pl.ANY) for _ in extra)],
            out_specs=[o[2] for o in outs],
            scratch_shapes=list(scratch),
        ),
        out_shape=[jax.ShapeDtypeStruct(o[0], o[1]) for o in outs],
        input_output_aliases={first + k: at for k, (at, _) in enumerate(keep)},
        compiler_params=params(mib),
        cost_estimate=pl.CostEstimate(flops=flops, bytes_accessed=moved, transcendentals=0),
        name=name,
    )(*scalars, *ins, *extra)


def index_kernel(per, src_ref, pos_row_ref, pos_col_ref, req_ref):
    n = src_ref.shape[1]
    rows = src_ref[...]
    cols = rows.T
    src_row, loc_row = rows[0:1], rows[1:2]
    src_col = cols[:, 0:1]
    member = (src_col == iota((n, LANES), 1).astype(F32)).astype(F32)
    member_t = (src_row == iota((LANES, n), 0).astype(F32)).astype(F32)
    before = (iota((n, n), 1) < iota((n, n), 0)).astype(F32).astype(BF)
    before_t = (iota((n, n), 0) < iota((n, n), 1)).astype(F32).astype(BF)
    rank = jnp.sum(dot(before, member.astype(BF)) * member, axis=1, keepdims=True)
    rank_t = jnp.sum(dot(member_t.astype(BF), before_t) * member_t, axis=0, keepdims=True)
    place = (src_col * per + rank).astype(I32)
    pos_col_ref[...] = place
    pos_row_ref[...] = (src_row * per + rank_t).astype(I32)
    onehot = (place == iota((n, n), 1)).astype(F32).astype(BF)
    high = jnp.floor(loc_row * (1.0 / 32.0))
    low = loc_row - high * 32.0
    pair = jnp.where(iota((8, n), 0) == 0, high, low).astype(BF)
    found = dot(pair, onehot)
    req_ref[...] = (found[0:1] * 32.0 + found[1:2]).astype(I32)


def find_places(anchor, n, per):
    src = (anchor // n).astype(F32)
    loc = (anchor % n).astype(F32)
    rows = jnp.concatenate([src[None], loc[None], jnp.zeros((6, n), F32)])
    return pl.pallas_call(
        functools.partial(index_kernel, per),
        out_shape=(
            jax.ShapeDtypeStruct((1, n), I32),
            jax.ShapeDtypeStruct((n, 1), I32),
            jax.ShapeDtypeStruct((1, n), I32),
        ),
        compiler_params=params(),
        name="places",
    )(rows)


def pick_kernel(idx_ref, data_ref, out_ref, hot_ref):
    n = idx_ref.shape[1]

    @pl.when(pl.program_id(0) == 0)
    def _():
        col = jnp.broadcast_to(idx_ref[...].astype(F32), (8, n)).T[:, 0:1].astype(I32)
        hot_ref[...] = (col == iota((n, n), 1)).astype(F32).astype(BF)

    out_ref[...] = dot(hot_ref[...], data_ref[...]).astype(BF)


def put_kernel(idx_ref, data_ref, out_ref, hot_ref):
    n = idx_ref.shape[1]

    @pl.when(pl.program_id(0) == 0)
    def _():
        hot_ref[...] = (idx_ref[...] == iota((n, n), 0)).astype(F32).astype(BF)

    out_ref[...] = dot(hot_ref[...], data_ref[...]).astype(BF)


def put_add_kernel(idx_ref, data_ref, base_ref, out_ref, hot_ref):
    n = idx_ref.shape[1]

    @pl.when(pl.program_id(0) == 0)
    def _():
        hot_ref[...] = (idx_ref[...] == iota((n, n), 0)).astype(F32).astype(BF)

    out_ref[...] = (base_ref[...].astype(F32) + dot(hot_ref[...], data_ref[...])).astype(BF)


def move_rows(kernel, idx, *data, name, deps=()):
    n, width = data[0].shape
    tile = next((t for t in (384, 256) if width % t == 0), width)
    spec = pl.BlockSpec((n, tile), lambda i, *_: (0, i))
    return call(
        kernel,
        [idx, *data],
        [whole((1, n))] + [spec] * len(data),
        [((n, width), BF, spec)],
        name,
        grid=(width // tile,),
        deps=deps,
        scratch=[pltpu.VMEM((n, n), BF)],
        flops=2 * n * n * width,
    )[0]


def row_ends(ids_ref, lengths_ref):
    me = ids_ref[0]
    ends = [lengths_ref[me, 0]]
    for k in range(1, lengths_ref.shape[1]):
        ends.append(ends[-1] + lengths_ref[me, k])
    return ends


def seg_of(ends, place):
    seg = jnp.zeros(place.shape, I32)
    for end in ends:
        seg = seg + (place >= end).astype(I32)
    return jnp.where(place < 0, -1, seg)


def seg_scalar(ends, place):
    seg = jnp.int32(0)
    for end in ends:
        seg = seg + (place >= end).astype(I32)
    return jnp.where(place < 0, jnp.int32(-1), seg)


def softplus(v):
    e = jnp.exp(-jnp.abs(v))
    w = 1.0 + e
    one = w == 1.0
    log1p = jnp.where(one, e, jnp.log(w) * (e / jnp.where(one, 1.0, w - 1.0)))
    return jnp.maximum(v, 0.0) + log1p


def widen(parts, head_size, width):
    rows = parts[0].shape[0]
    spread = (iota((2 * LANES, width), 0) % LANES == iota((2 * LANES, width), 1) // head_size)
    spread = spread.astype(F32).astype(BF)
    stacked = jnp.concatenate([jnp.concatenate(split2(p), axis=1) for p in parts], axis=0)
    out = dot(stacked, spread)
    return [out[k * rows : (k + 1) * rows] for k in range(len(parts))]


def head_sums(v, head_size, split):
    rows, width = v.shape
    gather = (iota((width, LANES), 0) // head_size == iota((width, LANES), 1)).astype(F32).astype(BF)
    pieces = split(v)
    out = dot(jnp.concatenate(pieces, axis=0), gather)
    return sum(out[k * rows : (k + 1) * rows] for k in range(len(pieces)))


def fixed_sum(mask, v):
    out = dot(mask, jnp.concatenate(split3(v), axis=1))
    w = v.shape[1]
    return out[:, :w] + out[:, w : 2 * w] + out[:, 2 * w :]


def decays(ends, base, span, dt, rates):
    place = base + iota((span, 1), 0)
    seg_c = seg_of(ends, place)
    low = (iota((span, span), 0) >= iota((span, span), 1)).astype(F32).astype(BF)
    cum = fixed_sum(low, dt * rates)
    last = cum[span - 1 : span]
    seg_before = seg_scalar(ends, base - 1)
    seg_last = seg_scalar(ends, base + span - 1)
    head_decay = jnp.where(seg_c == seg_before, jnp.exp(cum), 0.0)
    tail_decay = jnp.where(seg_c == seg_last, jnp.exp(last - cum), 0.0)
    return cum, head_decay, tail_decay, seg_c, seg_last


def half_masks(group):
    lane = iota((1, LANES), 1)
    return [(lane // (LANES // group) == k).astype(F32) for k in range(group)]


def hand_out(send_ref, keep_ref, me, pieces):
    for j, piece in enumerate(pieces):
        place = me ^ j

        @pl.when(place % 2 == 1)
        def _(piece=piece, place=place):
            send_ref[place // 2, 0 : piece.shape[0]] = piece

        @pl.when(place % 2 == 0)
        def _(piece=piece, place=place):
            keep_ref[place // 2, 0 : piece.shape[0]] = piece


def fwd_kernel(
    sizes, first, ids_ref, lengths_ref, gotx_ref, pos_ref, gain_ref, wz_ref, wx_ref, wbc_ref, wdt_ref, vx_ref, vb_ref,
    vh_ref, wout_ref, *refs,
):
    head_size, shares = sizes
    if first:
        xtail_in, btail_in, state_in, *refs = refs
    (
        xd_ref, ht_ref, rin_ref, z_ref, xs_ref, px_ref, y_ref, bcv_ref, pbc_ref, dtr_ref, g_ref, stat_ref,
        state_out_ref, send_ref, keep_ref, xtail_ref, btail_ref, state,
        xext, bext,
    ) = refs
    span = pos_ref.shape[0]
    n = gotx_ref.shape[0]
    inner = wz_ref.shape[1]
    width = gotx_ref.shape[1]
    state_size = wbc_ref.shape[1] // 2
    taps = vb_ref.shape[0] - 1
    group = LANES // head_size
    step = pl.program_id(0)
    base = (first + step) * span
    ends = row_ends(ids_ref, lengths_ref)
    cxw_ref, cbw_ref = vx_ref, vb_ref
    bias_x, skip, ggain = (vx_ref[taps + k : taps + k + 1] for k in range(3))

    @pl.when(step == 0)
    def _():
        xext[0:8] = xtail_in[...] if first else jnp.zeros((8, inner), F32)
        bext[0:8] = btail_in[...] if first else jnp.zeros((8, 2 * state_size), F32)
        state[...] = state_in[...] if first else jnp.zeros_like(state)

    onehot = (pos_ref[...] == iota((span, n), 1)).astype(F32).astype(BF)
    x = dot(onehot, gotx_ref[...])
    xd_ref[...] = x.astype(BF)
    r_in = lax.rsqrt(jnp.sum(x * x, axis=1, keepdims=True) * (1.0 / width) + EPSILON)
    rin_ref[...] = r_in
    h = (x * r_in * gain_ref[...]).astype(BF)
    ht_ref[...] = h.T
    z = dot(h, wz_ref[...])
    z_ref[...] = z
    xs = dot(h, wx_ref[...])
    bc = dot(h, wbc_ref[...])
    dtr = dot(h, wdt_ref[...])
    dtr_ref[...] = dtr
    xs_ref[...] = xs.astype(BF)
    bcv_ref[...] = bc.astype(BF)

    place = base + iota((span, 1), 0)
    seg_here = seg_of(ends, place)
    xext[8 : 8 + span] = xs
    bext[8 : 8 + span] = bc
    px = bias_x + cxw_ref[taps - 1 : taps] * xs
    pbc = vb_ref[taps : taps + 1] + cbw_ref[taps - 1 : taps] * bc
    for k in range(1, taps):
        same = (seg_of(ends, place - k) == seg_here).astype(F32)
        px = px + cxw_ref[taps - 1 - k : taps - k] * (xext[8 - k : 8 - k + span] * same)
        pbc = pbc + cbw_ref[taps - 1 - k : taps - k] * (bext[8 - k : 8 - k + span] * same)
    xext[0:8] = xs[span - 8 :]
    bext[0:8] = bc[span - 8 :]
    xtail_ref[...] = xs[span - 8 :]
    btail_ref[...] = bc[span - 8 :]
    px_ref[...] = px
    pbc_ref[...] = pbc
    u = px * jax.nn.sigmoid(px)
    bcc = pbc * jax.nn.sigmoid(pbc)
    b_rows = bcc[:, :state_size].astype(BF)
    c_rows = bcc[:, state_size:].astype(BF)

    dt = softplus(dtr + vh_ref[0:1])
    cum, head_decay, tail_decay, seg_c, _ = decays(ends, base, span, dt, vh_ref[1:2])
    cum_t = cum.T
    dt_w, head_w, tail_w = widen([dt, head_decay, tail_decay], head_size, inner)
    udt = u * dt_w
    seg_r = seg_of(ends, base + iota((1, span), 1))
    counts = (seg_c == seg_r) & (iota((span, span), 0) >= iota((span, span), 1))
    never = jnp.where(counts, 0.0, NEVER)
    scores = dot_t(c_rows, b_rows)
    entering = state[...]
    state_out_ref[0] = entering
    masks = half_masks(group)
    pieces = []
    for tile in range(inner // LANES):
        lanes = slice(tile * LANES, (tile + 1) * LANES)
        block = udt[:, lanes]
        total = None
        for k in range(group):
            head = tile * group + k
            decay = jnp.exp(cum[:, head : head + 1] - cum_t[head : head + 1, :] + never)
            term = dot((decay * scores).astype(BF), (block * masks[k]).astype(BF))
            total = term if total is None else total + term
        pieces.append(total)
    y = jnp.concatenate(pieces, axis=1)
    y = y + dot(c_rows, entering.astype(BF)) * head_w
    y = y + skip * u
    y_ref[...] = y
    b_t = bcc[:, :state_size].T.astype(BF)
    state[...] = head_w[span - 1 : span] * entering + dot(b_t, (udt * tail_w).astype(BF))
    gated = y * (z * jax.nn.sigmoid(z))
    squares = jnp.sum(gated * gated, axis=1, keepdims=True)
    stat_ref[0] = jnp.broadcast_to(squares, (span, LANES)).T[0:8]
    g = (gated * ggain).astype(BF)
    g_ref[...] = g
    mix = dot(g, wout_ref[...]).astype(BF)
    cols = width // shares
    hand_out(send_ref, keep_ref, ids_ref[1], [mix[:, j * cols : (j + 1) * cols] for j in range(shares)])


def run_fwd(part, scalars, sizes, got_x, pos, vectors, weights, before, deps):
    head_size, shares = sizes
    n, width = got_x.shape
    gain, vx, vb, vh = vectors
    w_z, w_x, w_bc, w_dt, w_out = weights
    inner = w_z.shape[1]
    two = w_bc.shape[1]
    span = SPAN
    first, last = part
    steps = last - first
    blocks = n // span

    def rows(c):
        return pl.BlockSpec((span, c), lambda i, *_: (first + i, 0))

    def by_block(a, c):
        return pl.BlockSpec((1, a, c), lambda i, *_: (first + i, 0, 0))

    ops = [got_x, pos, gain, w_z, w_x, w_bc, w_dt, vx, vb, vh, w_out]
    specs = [whole(o.shape) for o in ops]
    specs[1] = rows(1)
    cols = width // shares
    part_spec = pl.BlockSpec((shares // 2, span, cols), lambda i, *_: (0, i, 0))
    outs = [
        ((n, width), BF, rows(width)),
        ((width, n), BF, pl.BlockSpec((width, span), lambda i, *_: (0, first + i))),
        ((n, 1), F32, rows(1)),
        ((n, inner), F32, rows(inner)),
        ((n, inner), BF, rows(inner)),
        ((n, inner), F32, rows(inner)),
        ((n, inner), F32, rows(inner)),
        ((n, two), BF, rows(two)),
        ((n, two), F32, rows(two)),
        ((n, LANES), F32, rows(LANES)),
        ((n, inner), BF, rows(inner)),
        ((blocks, 8, span), F32, by_block(8, span)),
        ((blocks, two // 2, inner), F32, by_block(two // 2, inner)),
        ((shares // 2, steps * span, cols), BF, part_spec),
        ((shares // 2, steps * span, cols), BF, part_spec),
        ((8, inner), F32, whole((8, inner))),
        ((8, two), F32, whole((8, two))),
        ((two // 2, inner), F32, whole((two // 2, inner))),
    ]
    keep = []
    if before is not None:
        carry = list(before[15:18])
        ops += carry
        specs += [whole(o.shape) for o in carry]
        keep = list(enumerate(before[:13]))
    return call(
        functools.partial(fwd_kernel, sizes, first), ops, specs, outs, f"forward_{first}", grid=(steps,),
        scalars=scalars, deps=deps, keep=keep, flops=2 * steps * span * width * 5 * inner,
        scratch=[pltpu.VMEM((span + 8, inner), F32), pltpu.VMEM((span + 8, two), F32)],
    )


def dots_kernel(ids_ref, lengths_ref, pos_ref, dyn_ref, g_ref, stat_ref, out_ref, stat_out_ref):
    span = pos_ref.shape[0]
    n = dyn_ref.shape[0]
    base = pl.program_id(0) * span
    full = row_ends(ids_ref, lengths_ref)[-1]
    onehot = (pos_ref[...] == iota((span, n), 1)) & (base + iota((span, 1), 0) < full)
    dyn = dot(onehot.astype(F32).astype(BF), dyn_ref[...])
    out_ref[...] = dyn.astype(BF)
    inner_dot = jnp.sum(dyn * g_ref[...].astype(F32), axis=1, keepdims=True)
    as_row = jnp.broadcast_to(inner_dot, (span, LANES)).T[0:8]
    stat_out_ref[0] = jnp.where(iota((8, span), 0) == 0, stat_ref[0], as_row)


def run_dots(scalars, pos, got_dyn, g, stat, deps):
    n, inner = got_dyn.shape
    span = SPAN
    rows = pl.BlockSpec((span, inner), lambda i, *_: (i, 0))
    stats = pl.BlockSpec((1, 8, span), lambda i, *_: (i, 0, 0))
    return call(
        dots_kernel, [pos, got_dyn, g, stat],
        [pl.BlockSpec((span, 1), lambda i, *_: (i, 0)), whole((n, inner)), rows, stats],
        [((n, inner), BF, rows), (stat.shape, F32, stats)], "row_dots", grid=(n // span,), scalars=scalars, deps=deps,
        flops=2 * n * n * inner,
    )


def bwd_kernel(
    sizes, last, blocks, ids_ref, lengths_ref, stat_ref, dyn_ref, z_ref, xs_ref, px_ref, y_ref, bcv_ref, pbc_ref,
    dtr_ref, xd_ref, rin_ref, state_ref, gain_ref, wz_ref, wx_ref, wbc_ref, wdt_ref, vx_ref, vb_ref, vh_ref, *refs,
):
    head_size, shares = sizes
    newest = last == blocks
    if not newest:
        before, refs = refs[:8], refs[8:]
    (
        cols_ref, send_ref, keep_ref, *carry, xext, bext, extra,
    ) = refs
    xhead_ref, bhead_ref, dstate, across, accx_ref, accb_ref, acch_ref, accd_ref = carry
    span, inner = z_ref.shape
    width = xd_ref.shape[1]
    two = pbc_ref.shape[1]
    early = cols_ref.shape[1] - 2 * inner
    state_size = two // 2
    taps = vb_ref.shape[0] - 1
    group = LANES // head_size
    units = inner * shares
    step = pl.program_id(0)
    base = (last - 1 - step) * span
    ends = row_ends(ids_ref, lengths_ref)
    tensor = ids_ref[1]
    cxw_ref, cbw_ref = vx_ref, vb_ref
    skip, ggain = vx_ref[taps + 1 : taps + 2], vx_ref[taps + 2 : taps + 3]

    @pl.when(step == 0)
    def _():
        for k, ref in enumerate(carry):
            ref[...] = jnp.zeros_like(ref) if newest else before[k][...]
        extra[...] = jnp.zeros_like(extra)

    xext[span : span + 8] = xhead_ref[...]
    bext[span : span + 8] = bhead_ref[...]

    def add_row(ref, row, value):
        ref[row : row + 1] += jnp.sum(value, axis=0, keepdims=True)

    place = base + iota((span, 1), 0)
    stat_cols = stat_ref[0].T
    r_g = lax.rsqrt(stat_cols[:, 0:1] * (1.0 / units) + EPSILON)
    row_dot = stat_cols[:, 1:2] * (1.0 / units)
    z = z_ref[...]
    y = y_ref[...]
    dyn = dyn_ref[...].astype(F32)
    sig_z = jax.nn.sigmoid(z)
    silu_z = z * sig_z
    gated = y * silu_z
    normed = gated * r_g
    d_gated = r_g * (dyn * ggain) - normed * (r_g * r_g * row_dot)
    d_y = d_gated * silu_z
    dz = (d_gated * y * (sig_z * (1.0 + z * (1.0 - sig_z)))).astype(BF)
    cols_ref[:, early : early + inner] = dz
    add_row(accx_ref, taps + 2, dyn * normed)

    px = px_ref[...]
    sig_x = jax.nn.sigmoid(px)
    u = px * sig_x
    pbc = pbc_ref[...]
    sig_bc = jax.nn.sigmoid(pbc)
    bcc = pbc * sig_bc
    b_rows = bcc[:, :state_size].astype(BF)
    c_rows = bcc[:, state_size:].astype(BF)
    add_row(accx_ref, taps + 1, u * d_y)

    pre = dtr_ref[...] + vh_ref[0:1]
    dt = softplus(pre)
    rates = vh_ref[1:2]
    cum, head_decay, tail_decay, seg_c, seg_last = decays(ends, base, span, dt, rates)
    cum_t = cum.T
    dt_w, head_w, tail_w = widen([dt, head_decay, tail_decay], head_size, inner)
    udt = u * dt_w
    seg_r = seg_of(ends, base + iota((1, span), 1))
    counts = (seg_c == seg_r) & (iota((span, span), 1) >= iota((span, span), 0))
    never = jnp.where(counts, 0.0, NEVER)
    scores = dot_t(b_rows, c_rows)
    d_scores = jnp.zeros((span, span), F32)
    masks = half_masks(group)
    pieces = []
    for tile in range(inner // LANES):
        lanes = slice(tile * LANES, (tile + 1) * LANES)
        udt_block = udt[:, lanes]
        dy_block = d_y[:, lanes]
        dy_low = dy_block.astype(BF)
        total = None
        for k in range(group):
            head = tile * group + k
            decay = jnp.exp(cum_t[head : head + 1, :] - cum[:, head : head + 1] + never)
            d_scores = d_scores + decay * dot_t((udt_block * masks[k]).astype(BF), dy_low)
            term = dot((decay * scores).astype(BF), (dy_block * masks[k]).astype(BF))
            total = term if total is None else total + term
        pieces.append(total)
    in_block = jnp.concatenate(pieces, axis=1)
    d_state = dstate[...]
    d_state_low = d_state.astype(BF)
    entering = state_ref[0]
    entering_low = entering.astype(BF)
    at_end = dot(b_rows, d_state_low)
    at_start = dot(c_rows, entering_low)
    d_udt = in_block + at_end * tail_w
    from_start = (d_y * head_w).astype(BF)
    to_end = (udt * tail_w).astype(BF)
    d_c = dot(d_scores.T.astype(BF), b_rows) + dot_t(from_start, entering_low)
    d_b = dot(d_scores.astype(BF), c_rows) + dot_t(to_end, d_state_low)
    y_block = y - skip * u - at_start * head_w
    balance = d_y.astype(BF).astype(F32) * y_block - udt.astype(BF).astype(F32) * in_block
    balance = balance + from_start.astype(F32) * at_start - to_end.astype(F32) * at_end
    v_part = head_sums(u * d_udt, head_size, split2)
    mask_low = counts.astype(F32).astype(BF)
    d_la = fixed_sum(mask_low, head_sums(balance, head_size, split3))
    d_la = d_la + jnp.where(seg_c == seg_last, across[0:1], 0.0)
    d_dt = v_part + rates * d_la
    d_pre = d_dt * jax.nn.sigmoid(pre)
    add_row(acch_ref, 0, d_la * dt * rates)
    add_row(acch_ref, 1, d_pre)

    c_t = bcc[:, state_size:].T.astype(BF)
    d_enter = dot(c_t, from_start) + head_w[span - 1 : span] * d_state
    dstate[...] = d_enter
    crossing = jnp.sum(d_enter.astype(BF).astype(F32) * entering, axis=0, keepdims=True)
    across[...] = head_sums(jnp.broadcast_to(crossing, (8, inner)), head_size, split3)

    d_u = skip * d_y + dt_w * d_udt
    d_px = d_u * (sig_x * (1.0 + px * (1.0 - sig_x)))
    d_pbc = jnp.concatenate([d_b, d_c], axis=1) * (sig_bc * (1.0 + pbc * (1.0 - sig_bc)))
    xext[0:span] = d_px
    bext[0:span] = d_pbc
    seg_here = seg_of(ends, place)
    xs = xs_ref[...].astype(F32)
    bcv = bcv_ref[...].astype(F32)
    d_xs = cxw_ref[taps - 1 : taps] * d_px
    d_bc = cbw_ref[taps - 1 : taps] * d_pbc
    add_row(accx_ref, taps, d_px)
    add_row(accb_ref, taps, d_pbc)
    add_row(accx_ref, taps - 1, d_px * xs)
    add_row(accb_ref, taps - 1, d_pbc * bcv)
    for k in range(1, taps):
        later = place + k
        same = ((seg_of(ends, later) == seg_here) & (later < blocks * span)).astype(F32)
        tap = taps - 1 - k
        xk = xext[k : k + span] * same
        bk = bext[k : k + span] * same
        d_xs = d_xs + cxw_ref[tap : tap + 1] * xk
        d_bc = d_bc + cbw_ref[tap : tap + 1] * bk
        add_row(accx_ref, tap, xk * xs)
        add_row(accb_ref, tap, bk * bcv)
    xhead_ref[...] = d_px[0:8]
    bhead_ref[...] = d_pbc[0:8]
    dx_low = d_xs.astype(BF)
    dbc_low = d_bc.astype(BF)
    ddt_low = d_pre.astype(BF)
    cols_ref[:, 0:two] = dbc_low
    cols_ref[:, two : two + LANES] = ddt_low
    cols_ref[:, early + inner : early + 2 * inner] = dx_low
    for at in range(two + LANES, early, LANES):
        cols_ref[:, at : at + LANES] = jnp.zeros((span, LANES), BF)
    back = dot_t(dz, wz_ref[...]) + dot_t(dx_low, wx_ref[...])
    back = back + dot_t(ddt_low, wdt_ref[...]) + dot_t(dbc_low, wbc_ref[...])
    x_hat = xd_ref[...].astype(F32) * rin_ref[...]
    shared = back * x_hat
    add_row(accd_ref, 0, shared)
    inner_dot = jnp.sum(shared * gain_ref[...], axis=1, keepdims=True)
    low = back.astype(BF)
    cols = width // shares
    row = jnp.broadcast_to(inner_dot, (span, LANES)).T[0:1]
    for k in range(span // LANES):
        extra[k : k + 1] = row[:, k * LANES : (k + 1) * LANES]
    hand_out(send_ref, keep_ref, tensor, [low[:, j * cols : (j + 1) * cols] for j in range(shares)])
    more = extra[...].astype(BF)
    for part in range(shares // 2):
        send_ref[part, span : span + EXTRA, 0:LANES] = more
        keep_ref[part, span : span + EXTRA, 0:LANES] = more


def run_bwd(part, scalars, sizes, stat, dyn, kept, vectors, weights, before, deps):
    head_size, shares = sizes
    z, xs, px, y, bcv, pbc, dtr, xd, rin, states = kept
    w_z, w_x, w_bc, w_dt = weights
    n, inner = z.shape
    width = xd.shape[1]
    two = pbc.shape[1]
    span = SPAN
    first, last = part
    steps = last - first
    blocks = n // span
    cols = width // shares

    def rows(c):
        return pl.BlockSpec((span, c), lambda i, *_: (last - 1 - i, 0))

    def by_block(a, c):
        return pl.BlockSpec((1, a, c), lambda i, *_: (last - 1 - i, 0, 0))

    ops = [stat, dyn, z, xs, px, y, bcv, pbc, dtr, xd, rin, states]
    specs = [by_block(8, span), *(rows(o.shape[1]) for o in ops[1:11]), by_block(two // 2, inner)]
    fixed = [vectors[0], w_z, w_x, w_bc, w_dt, *vectors[1:]]
    part_spec = pl.BlockSpec((shares // 2, span + EXTRA, cols), lambda i, *_: (0, steps - 1 - i, 0))
    wide = -(-(2 * inner + two + LANES) // (2 * LANES)) * (2 * LANES)
    sums = [(8, inner), (8, two), (two // 2, inner), (8, LANES), (8, inner), (8, two), (8, LANES), (8, width)]
    outs = [
        ((n, wide), BF, rows(wide)),
        ((shares // 2, steps * (span + EXTRA), cols), BF, part_spec),
        ((shares // 2, steps * (span + EXTRA), cols), BF, part_spec),
        *((c, F32, whole(c)) for c in sums),
    ]
    keep = []
    if before is not None:
        fixed += before[3:]
        keep = list(enumerate(before[:1]))
    return call(
        functools.partial(bwd_kernel, sizes, last, blocks), ops + fixed, specs + [whole(o.shape) for o in fixed], outs,
        f"backward_{first}", grid=(steps,), scalars=scalars, deps=deps, keep=keep,
        flops=2 * steps * span * width * 6 * inner,
        scratch=[pltpu.VMEM((span + 8, inner), F32), pltpu.VMEM((span + 8, two), F32), pltpu.VMEM((EXTRA, LANES), F32)],
    )


def outer_kernel(groups, ids_ref, left_ref, right_ref, send_ref, keep_ref):
    each = groups // pl.num_programs(0)
    rows = left_ref.shape[0] // each
    low = dot(left_ref[...], right_ref[...]).astype(BF)
    at = pl.program_id(0) * each
    for i in range(each):
        place = ids_ref[0] ^ (at + i)

        @pl.when(place % 2 == 1)
        def _(i=i, place=place):
            send_ref[place // 2] = low[i * rows : (i + 1) * rows]

        @pl.when(place % 2 == 0)
        def _(i=i, place=place):
            keep_ref[place // 2] = low[i * rows : (i + 1) * rows]


def outer(ids, groups, left_t, right, first, count, deps=()):
    width, n = left_t.shape
    steps = 4
    rows = width // groups
    out = ((groups // 2, rows, count), BF, whole((groups // 2, rows, count)))
    return call(
        functools.partial(outer_kernel, groups), [left_t, right],
        [pl.BlockSpec((width // steps, n), lambda i, *_: (i, 0)), pl.BlockSpec((n, count), lambda *_: (0, first // count))],
        [out, out], "outer",
        grid=(steps,), scalars=[ids], deps=deps, flops=2 * n * width * count,
    )


def put_yn_kernel(units, ids_ref, lengths_ref, pos_ref, stat_ref, data_ref, out_ref, hot_ref, scale_ref):
    n = pos_ref.shape[1]
    blocks, _, span = stat_ref.shape

    @pl.when(pl.program_id(0) == 0)
    def _():
        hot_ref[...] = (pos_ref[...] == iota((n, n), 0)).astype(F32).astype(BF)
        full = row_ends(ids_ref, lengths_ref)[-1]
        for k in range(blocks):
            squares = stat_ref[k].T[:, 0:1]
            valid = k * span + iota((span, 1), 0) < full
            scale = lax.rsqrt(squares * (1.0 / units) + EPSILON)
            scale_ref[k * span : (k + 1) * span] = jnp.where(valid, scale, 0.0)

    yn = (data_ref[...].astype(F32) * scale_ref[...]).astype(BF)
    out_ref[...] = dot(hot_ref[...], yn).astype(BF)


def put_yn(scalars, units, pos, stat, g, deps):
    n, width = g.shape
    tile = next((t for t in (384, 256) if width % t == 0), width)
    spec = pl.BlockSpec((n, tile), lambda i, *_: (0, i))
    return call(
        functools.partial(put_yn_kernel, units), [pos, stat, g], [whole(pos.shape), whole(stat.shape), spec],
        [((n, width), BF, spec)], "put_yn", grid=(width // tile,), scalars=scalars, deps=deps,
        scratch=[pltpu.VMEM((n, n), BF), pltpu.VMEM((n, 1), F32)], flops=2 * n * n * width,
    )[0]


def add_up(refs, counts):
    pieces, at = [], 0
    for count in counts:
        total = refs[at][0].astype(F32)
        for ref in refs[at + 1 : at + count]:
            total = total + ref[0].astype(F32)
        pieces.append(total)
        at += count
    return jnp.concatenate(pieces, axis=0)


def send_out_kernel(units, counts, ids_ref, lengths_ref, pos_ref, stat_ref, x_ref, *refs):
    *terms, out_ref, sq_ref = refs
    n = pos_ref.shape[1]
    blocks, _, span = stat_ref.shape
    mix = add_up(terms, counts)
    squares = jnp.concatenate([stat_ref[k].T[:, 0:1] for k in range(blocks)], axis=0)
    valid = (iota((n, 1), 0) < row_ends(ids_ref, lengths_ref)[-1]).astype(F32)
    mix = mix * (lax.rsqrt(squares * (1.0 / units) + EPSILON) * valid)
    x = x_ref[...].astype(F32)
    out = (x + mix).astype(BF)
    full = out.astype(F32)
    onehot = (pos_ref[...] == iota((n, n), 0)).astype(F32).astype(BF)
    out_ref[...] = dot(onehot, out).astype(BF)
    sq_ref[...] = jnp.zeros_like(sq_ref)
    for k, v in enumerate((x * x * valid, mix * mix, full * full * valid)):
        sq_ref[k : k + 1] = jnp.sum(v, axis=0, keepdims=True)


def send_dx_kernel(width, span, counts, pos_ref, x_ref, rin_ref, gain_ref, *refs):
    *terms, out_ref = refs
    n = pos_ref.shape[1]
    total = add_up(terms, counts)
    each = span + EXTRA
    d_h, dots = [], []
    for k in range(n // span):
        d_h.append(total[k * each : k * each + span])
        rows = total[k * each + span : k * each + span + 8, 0:LANES].T
        dots += [rows[:, i : i + 1] for i in range(span // LANES)]
    d_h, dots = jnp.concatenate(d_h, axis=0), jnp.concatenate(dots, axis=0)
    r_in = rin_ref[...]
    x_hat = x_ref[...].astype(F32) * r_in
    dx = (r_in * (d_h * gain_ref[...] - x_hat * (dots * (1.0 / width)))).astype(BF)
    onehot = (pos_ref[...] == iota((n, n), 0)).astype(F32).astype(BF)
    out_ref[...] = dot(onehot, dx).astype(BF)


def term_ops(groups_of_terms):
    ops = [t for terms in groups_of_terms for t in terms]
    specs = [pl.BlockSpec((1,) + o.shape[1:], lambda *_: (0, 0, 0)) for o in ops]
    return ops, specs, [len(terms) for terms in groups_of_terms]


def swap(v, axis, bit):
    size = lax.axis_size(axis)
    return lax.ppermute(v, axis, [(i, i ^ (1 << bit)) for i in range(size)])


def bits_of(axis):
    return lax.axis_size(axis).bit_length() - 1


class Halving:
    def __init__(self, send, keep, axis, order):
        self.axis, self.order = axis, order
        self.left = list(range(len(order) - 1, 0, -1))
        shape = (2,) * len(self.left) + keep.shape[1:]
        self.terms = [keep.reshape(shape)]
        self.sent = send.reshape(shape)
        self.flat = [keep]
        self.at = 0

    def step(self):
        got = swap(self.sent, self.axis, self.order[self.at])
        self.terms.append(got)
        self.flat.append(got.reshape((-1,) + got.shape[len(self.left) :]))
        self.at += 1
        if self.left:
            dim = self.left.index(self.order[self.at])
            self.left.pop(dim)
            odd = [lax.index_in_dim(t, 1, dim, keepdims=False).astype(F32) for t in self.terms]
            self.sent = sum(odd[1:], odd[0]).astype(BF)
            self.terms = [lax.index_in_dim(t, 0, dim, keepdims=False) for t in self.terms]
        else:
            self.sent = None
        return self.sent

    def finish(self):
        while self.sent is not None:
            self.step()
        return self

    def total(self):
        self.finish()
        wide = [t.astype(F32) for t in self.terms]
        return sum(wide[1:], wide[0])


def sum_all(v, axis, after=()):
    if after:
        v = lax.optimization_barrier((v, *after))[0]
    for bit in range(bits_of(axis)):
        v = v + swap(v, axis, bit)
    return v


def exchange(v, axis):
    groups = lax.axis_size(axis)
    rows = v.shape[0]
    parts = v.reshape((groups, rows // groups) + v.shape[1:])
    return lax.all_to_all(parts, axis, split_axis=0, concat_axis=0, tiled=True).reshape(v.shape)


def pad_lanes(v):
    return jnp.pad(v, [(0, 0)] * (v.ndim - 1) + [(0, LANES - v.shape[-1])])


def local(
    stream, out_grad, seq_lengths, anchor, norm_gain, w_z, w_x, w_bc, w_dt, conv_x_w, conv_x_b, conv_bc_w,
    conv_bc_b, dt_bias, a_log, d_skip, gated_gain, w_out,
):
    groups = lax.axis_size("dp")
    shares = lax.axis_size("tensor")
    me = lax.axis_index("dp")
    tensor = lax.axis_index("tensor")
    n, width = stream.shape
    per = n // groups
    cols = width // shares
    first_col = tensor * cols
    inner = w_z.shape[1]
    heads = w_dt.shape[1]
    head_size = inner // heads
    two = w_bc.shape[1]
    taps = conv_x_w.shape[0]
    sizes = (head_size, shares)
    units = inner * shares
    ids = jnp.stack([me, tensor]).astype(I32)
    scalars = [ids, seq_lengths]
    tensor_order = list(range(bits_of("tensor")))
    dp_bits = bits_of("dp")
    order_a = list(range(dp_bits))
    order_b = order_a[:1] + order_a[1:][::-1]

    pos_row, pos_col, requests = find_places(anchor, n, per)
    wanted = lax.all_to_all(
        requests.reshape(groups, per), "dp", split_axis=0, concat_axis=0, tiled=True
    ).reshape(1, n)
    got_x = exchange(move_rows(pick_kernel, wanted, stream, name="pick_x"), "dp")
    gain = norm_gain[None]
    vx = jnp.concatenate([conv_x_w, conv_x_b[None], jnp.repeat(d_skip, head_size)[None], gated_gain[None]])
    vb = jnp.concatenate([conv_bc_w, conv_bc_b[None]])
    vh = pad_lanes(jnp.stack([dt_bias, -jnp.exp(a_log)]))
    w_dt_pad = pad_lanes(w_dt)
    dy_t = out_grad.T
    gain_cols = lax.dynamic_slice_in_dim(norm_gain, first_col, cols, 0)[None]
    dy_cols = lax.dynamic_slice_in_dim(out_grad, first_col, cols, 1)
    d_yn_src = jnp.einsum("td,id->ti", out_grad, w_out, preferred_element_type=F32).astype(BF)
    dyn_send = move_rows(
        pick_kernel, wanted, d_yn_src, name="pick_dyn", deps=[gain, vx, vb, vh, w_dt_pad, dy_t, gain_cols, dy_cols]
    )
    got_dyn = exchange(dyn_send, "dp")

    vectors = (gain, vx, vb, vh)
    first, second = FORWARD
    weights = (w_z, w_x, w_bc, w_dt_pad)
    got = run_fwd(first, scalars, sizes, got_x, pos_col, vectors, (*weights, w_out), None, [dyn_send])
    mix_1 = Halving(got[13], got[14], "tensor", tensor_order)
    got = run_fwd(second, scalars, sizes, got_x, pos_col, vectors, (*weights, w_out), got, [])
    mix_2 = Halving(got[13], got[14], "tensor", tensor_order)
    (xd, h_t, rin, z, xs, px, y, bcv, pbc, dtr, g, stat, states) = got[:13]
    x_cols = lax.dynamic_slice_in_dim(xd, first_col, cols, 1)
    dyn, stat = run_dots(scalars, pos_col, got_dyn, g, stat, [mix_1.step()])
    stat = sum_all(stat, "tensor")
    mix_2.sent, stat = lax.optimization_barrier((mix_2.sent, stat))

    kept = (z, xs, px, y, bcv, pbc, dtr, xd, rin, states)
    yn_send = put_yn(scalars, units, pos_row, stat, g, [x_cols])
    yn_back = exchange(yn_send, "dp")
    mix_1.finish()
    got = run_bwd(BACKWARD[0], scalars, sizes, stat, dyn, kept, vectors, weights, None, [yn_send])
    back_1 = Halving(got[1], got[2], "tensor", tensor_order)
    yn_src = move_rows(put_kernel, wanted, yn_back, name="place_yn", deps=[got[1], mix_2.step(), mix_1.terms[-1]])
    h_out = Halving(*outer(ids, groups, dy_t, yn_src, 0, inner), "dp", order_b)
    mix_2.finish()
    got = run_bwd(BACKWARD[1], scalars, sizes, stat, dyn, kept, vectors, weights, got, [h_out.sent])
    back_2 = Halving(got[1], got[2], "tensor", tensor_order)
    grad_cols = got[0]
    acc_x, acc_b, acc_h, acc_d = got[7:]

    ops, specs, counts = term_ops([mix_1.flat, mix_2.flat])
    ops = [pos_row, stat, x_cols, *ops]
    out_send, squares = call(
        functools.partial(send_out_kernel, units, counts), ops, [*(whole(o.shape) for o in ops[:3]), *specs],
        [((n, cols), BF, whole((n, cols))), ((8, cols), F32, whole((8, cols)))], "send_out", scalars=scalars,
        flops=2 * n * n * cols, deps=[back_2.sent, back_1.step(), h_out.step()],
    )
    back_1.finish()
    out_back = exchange(out_send, "dp")
    flat = [acc_x, acc_h, acc_b[: taps + 1], acc_d[0], jnp.sum(squares, axis=1)]
    flat = [f.reshape(-1) for f in flat]
    lens = [f.shape[0] for f in flat]
    small = jnp.pad(jnp.concatenate(flat), (0, -sum(lens) % 1024)).reshape(-1, LANES)
    half = grad_cols.shape[1] // 2
    h_a = Halving(*outer(ids, groups, h_t, grad_cols, 0, half, [out_send]), "dp", order_a)
    h_b = Halving(*outer(ids, groups, h_t, grad_cols, half, half, [h_a.sent]), "dp", order_b)
    waits = [h_b.sent, h_a.step(), h_out.step(), back_2.step(), back_1.terms[-1]]
    out_final = move_rows(put_kernel, wanted, out_back, name="place_out", deps=[w for w in waits if w is not None])
    back_2.finish()

    back_ops, back_specs, back_counts = term_ops([back_2.flat, back_1.flat])
    ops = [pos_row, x_cols, rin, gain_cols]
    waits = [out_final, h_b.step(), h_out.finish().terms[-1]]
    dx_send = call(
        functools.partial(send_dx_kernel, width, SPAN, back_counts), [*ops, *back_ops],
        [*(whole(o.shape) for o in ops), *back_specs],
        [((n, cols), BF, whole((n, cols)))], "send_dx", flops=2 * n * n * cols, deps=waits,
    )[0]
    dx_back = exchange(dx_send, "dp")
    small = sum_all(small, "dp", [dx_send])
    dx_final = move_rows(put_add_kernel, wanted, dx_back, dy_cols, name="place_dx", deps=[h_a.step()])

    g_out = h_out.total()
    g_a = h_a.total()
    g_b = h_b.total()
    early = 2 * half - 2 * inner
    g_bc = sum_all(g_a[:, :two], "tensor")
    g_dt = g_a[:, two : two + heads]
    g_z = jnp.concatenate([g_a[:, early:], g_b[:, : early + inner - half]], axis=1)
    g_x = g_b[:, early + inner - half :]

    own = lens[0] + lens[1]
    s_x = small.reshape(-1)[: lens[0]].reshape(acc_x.shape)
    s_h = small.reshape(-1)[lens[0] : own].reshape(acc_h.shape)
    both = sum_all(small[own // LANES :], "tensor").reshape(-1)
    s_b = both[: lens[2]].reshape(taps + 1, two)
    s_d = both[lens[2] : lens[2] + lens[3]]
    s_sq = both[lens[2] + lens[3] : lens[2] + lens[3] + 3]
    g_gain = lax.dynamic_slice_in_dim(s_d, first_col, cols, 0)
    rms = jnp.sqrt(s_sq / (jnp.sum(seq_lengths).astype(F32) * width))
    g_skip = jnp.sum(s_x[taps + 1].reshape(heads, head_size), axis=1)
    return (
        out_final, dx_final, g_gain, g_z, g_x, g_bc, g_dt, s_x[:taps], s_x[taps], s_b[:taps], s_b[taps],
        s_h[1, :heads], s_h[0, :heads], g_skip, s_x[taps + 2], g_out.T, rms,
    )


def solution(mesh):
    in_specs = (
        P("dp", None), P("dp", None), P(), P("dp"), P(), P(None, "tensor"), P(None, "tensor"), P(),
        P(None, "tensor"), P(None, "tensor"), P("tensor"), P(), P(), P("tensor"), P("tensor"), P("tensor"),
        P("tensor"), P("tensor", None),
    )
    out_specs = (
        P("dp", "tensor"), P("dp", "tensor"), P("tensor"), P("dp", "tensor"), P("dp", "tensor"), P("dp", None),
        P("dp", "tensor"), P(None, "tensor"), P("tensor"), P(), P(), P("tensor"), P("tensor"), P("tensor"),
        P("tensor"), P("tensor", "dp"), P(),
    )
    return jax.shard_map(local, mesh=mesh, in_specs=in_specs, out_specs=out_specs, check_vma=False)
```

```python
import copy
import functools

import jax
import jax.numpy as jnp
from jax import lax
from jax.experimental import pallas as pl
from jax.experimental.pallas import tpu as pltpu
from jax.sharding import PartitionSpec as P

SPAN = 256
EPSILON = 1e-05
LANES = 128
NEVER = -1e30
BF = jnp.bfloat16
F32 = jnp.float32
I32 = jnp.int32
MIB = 1 << 20
EXTRA = 16
FORWARD = ((0, 2), (2, 4))
BACKWARD = ((2, 4), (0, 2))


def dot(a, b):
    return jnp.dot(a, b, preferred_element_type=F32)


def dot_t(a, b):
    return lax.dot_general(a, b, (((1,), (1,)), ((), ())), preferred_element_type=F32)


def iota(shape, dim):
    return lax.broadcasted_iota(I32, shape, dim)


def split2(v):
    hi = v.astype(BF)
    return hi, (v - hi.astype(F32)).astype(BF)


def split3(v):
    hi = v.astype(BF)
    rest = v - hi.astype(F32)
    mid = rest.astype(BF)
    return hi, mid, (rest - mid.astype(F32)).astype(BF)


def params(mib=56, **more):
    return pltpu.CompilerParams(vmem_limit_bytes=mib * MIB, **more)


def whole(shape):
    rank = len(shape)
    return pl.BlockSpec(shape, lambda *_: (0,) * rank)


def call(kernel, ins, in_specs, outs, name, grid=(1,), scalars=(), deps=(), scratch=(), flops=0, keep=(), mib=56):
    n_scalars, n_in, n_extra = len(scalars), len(ins), len(keep) + len(deps)

    def body(*refs):
        kernel(*refs[: n_scalars + n_in], *refs[n_scalars + n_in + n_extra :])

    extra = [a for _, a in keep] + list(deps)
    first = n_scalars + n_in
    moved = sum(a.size * a.dtype.itemsize for a in ins) + sum(
        functools.reduce(lambda p, q: p * q, o[0]) * 2 for o in outs
    )
    return pl.pallas_call(
        body,
        grid_spec=pltpu.PrefetchScalarGridSpec(
            num_scalar_prefetch=n_scalars,
            grid=grid,
            in_specs=[*in_specs, *(pl.BlockSpec(memory_space=pl.ANY) for _ in extra)],
            out_specs=[o[2] for o in outs],
            scratch_shapes=list(scratch),
        ),
        out_shape=[jax.ShapeDtypeStruct(o[0], o[1]) for o in outs],
        input_output_aliases={first + k: at for k, (at, _) in enumerate(keep)},
        compiler_params=params(mib),
        cost_estimate=pl.CostEstimate(flops=flops, bytes_accessed=moved, transcendentals=0),
        name=name,
    )(*scalars, *ins, *extra)


def index_kernel(per, src_ref, pos_row_ref, pos_col_ref, req_ref):
    n = src_ref.shape[1]
    rows = src_ref[...]
    cols = rows.T
    src_row, loc_row = rows[0:1], rows[1:2]
    src_col = cols[:, 0:1]
    member = (src_col == iota((n, LANES), 1).astype(F32)).astype(F32)
    member_t = (src_row == iota((LANES, n), 0).astype(F32)).astype(F32)
    before = (iota((n, n), 1) < iota((n, n), 0)).astype(F32).astype(BF)
    before_t = (iota((n, n), 0) < iota((n, n), 1)).astype(F32).astype(BF)
    rank = jnp.sum(dot(before, member.astype(BF)) * member, axis=1, keepdims=True)
    rank_t = jnp.sum(dot(member_t.astype(BF), before_t) * member_t, axis=0, keepdims=True)
    place = (src_col * per + rank).astype(I32)
    pos_col_ref[...] = place
    pos_row_ref[...] = (src_row * per + rank_t).astype(I32)
    onehot = (place == iota((n, n), 1)).astype(F32).astype(BF)
    high = jnp.floor(loc_row * (1.0 / 32.0))
    low = loc_row - high * 32.0
    pair = jnp.where(iota((8, n), 0) == 0, high, low).astype(BF)
    found = dot(pair, onehot)
    req_ref[...] = (found[0:1] * 32.0 + found[1:2]).astype(I32)


def find_places(anchor, n, per):
    src = (anchor // n).astype(F32)
    loc = (anchor % n).astype(F32)
    rows = jnp.concatenate([src[None], loc[None], jnp.zeros((6, n), F32)])
    return pl.pallas_call(
        functools.partial(index_kernel, per),
        out_shape=(
            jax.ShapeDtypeStruct((1, n), I32),
            jax.ShapeDtypeStruct((n, 1), I32),
            jax.ShapeDtypeStruct((1, n), I32),
        ),
        compiler_params=params(),
        name="places",
    )(rows)


def pick_kernel(idx_ref, data_ref, out_ref, hot_ref):
    n = idx_ref.shape[1]

    @pl.when(pl.program_id(0) == 0)
    def _():
        col = jnp.broadcast_to(idx_ref[...].astype(F32), (8, n)).T[:, 0:1].astype(I32)
        hot_ref[...] = (col == iota((n, n), 1)).astype(F32).astype(BF)

    out_ref[...] = dot(hot_ref[...], data_ref[...]).astype(BF)


def put_kernel(idx_ref, data_ref, out_ref, hot_ref):
    n = idx_ref.shape[1]

    @pl.when(pl.program_id(0) == 0)
    def _():
        hot_ref[...] = (idx_ref[...] == iota((n, n), 0)).astype(F32).astype(BF)

    out_ref[...] = dot(hot_ref[...], data_ref[...]).astype(BF)


def put_add_kernel(idx_ref, data_ref, base_ref, out_ref, hot_ref):
    n = idx_ref.shape[1]

    @pl.when(pl.program_id(0) == 0)
    def _():
        hot_ref[...] = (idx_ref[...] == iota((n, n), 0)).astype(F32).astype(BF)

    out_ref[...] = (base_ref[...].astype(F32) + dot(hot_ref[...], data_ref[...])).astype(BF)


def move_rows(kernel, idx, *data, name, deps=()):
    n, width = data[0].shape
    tile = next((t for t in (384, 256) if width % t == 0), width)
    spec = pl.BlockSpec((n, tile), lambda i, *_: (0, i))
    return call(
        kernel,
        [idx, *data],
        [whole((1, n))] + [spec] * len(data),
        [((n, width), BF, spec)],
        name,
        grid=(width // tile,),
        deps=deps,
        scratch=[pltpu.VMEM((n, n), BF)],
        flops=2 * n * n * width,
    )[0]


def row_ends(ids_ref, lengths_ref):
    me = ids_ref[0]
    ends = [lengths_ref[me, 0]]
    for k in range(1, lengths_ref.shape[1]):
        ends.append(ends[-1] + lengths_ref[me, k])
    return ends


def seg_of(ends, place):
    seg = jnp.zeros(place.shape, I32)
    for end in ends:
        seg = seg + (place >= end).astype(I32)
    return jnp.where(place < 0, -1, seg)


def seg_scalar(ends, place):
    seg = jnp.int32(0)
    for end in ends:
        seg = seg + (place >= end).astype(I32)
    return jnp.where(place < 0, jnp.int32(-1), seg)


def softplus(v):
    e = jnp.exp(-jnp.abs(v))
    w = 1.0 + e
    one = w == 1.0
    log1p = jnp.where(one, e, jnp.log(w) * (e / jnp.where(one, 1.0, w - 1.0)))
    return jnp.maximum(v, 0.0) + log1p


def widen(parts, head_size, width):
    rows = parts[0].shape[0]
    spread = (iota((2 * LANES, width), 0) % LANES == iota((2 * LANES, width), 1) // head_size)
    spread = spread.astype(F32).astype(BF)
    stacked = jnp.concatenate([jnp.concatenate(split2(p), axis=1) for p in parts], axis=0)
    out = dot(stacked, spread)
    return [out[k * rows : (k + 1) * rows] for k in range(len(parts))]


def head_sums(v, head_size, split):
    rows, width = v.shape
    gather = (iota((width, LANES), 0) // head_size == iota((width, LANES), 1)).astype(F32).astype(BF)
    pieces = split(v)
    out = dot(jnp.concatenate(pieces, axis=0), gather)
    return sum(out[k * rows : (k + 1) * rows] for k in range(len(pieces)))


def fixed_sum(mask, v):
    out = dot(mask, jnp.concatenate(split3(v), axis=1))
    w = v.shape[1]
    return out[:, :w] + out[:, w : 2 * w] + out[:, 2 * w :]


def decays(ends, base, span, dt, rates):
    place = base + iota((span, 1), 0)
    seg_c = seg_of(ends, place)
    low = (iota((span, span), 0) >= iota((span, span), 1)).astype(F32).astype(BF)
    cum = fixed_sum(low, dt * rates)
    last = cum[span - 1 : span]
    seg_before = seg_scalar(ends, base - 1)
    seg_last = seg_scalar(ends, base + span - 1)
    head_decay = jnp.where(seg_c == seg_before, jnp.exp(cum), 0.0)
    tail_decay = jnp.where(seg_c == seg_last, jnp.exp(last - cum), 0.0)
    return cum, head_decay, tail_decay, seg_c, seg_last


def half_masks(group):
    lane = iota((1, LANES), 1)
    return [(lane // (LANES // group) == k).astype(F32) for k in range(group)]


def hand_out(send_ref, keep_ref, me, pieces):
    for j, piece in enumerate(pieces):
        place = me ^ j

        @pl.when(place % 2 == 1)
        def _(piece=piece, place=place):
            send_ref[place // 2, 0 : piece.shape[0]] = piece

        @pl.when(place % 2 == 0)
        def _(piece=piece, place=place):
            keep_ref[place // 2, 0 : piece.shape[0]] = piece


def fwd_kernel(
    sizes, first, ids_ref, lengths_ref, gotx_ref, pos_ref, gain_ref, wz_ref, wx_ref, wbc_ref, wdt_ref, vx_ref, vb_ref,
    vh_ref, wout_ref, *refs,
):
    head_size, shares = sizes
    if first:
        xtail_in, btail_in, state_in, *refs = refs
    (
        xd_ref, ht_ref, rin_ref, z_ref, xs_ref, px_ref, y_ref, bcv_ref, pbc_ref, dtr_ref, g_ref, stat_ref,
        state_out_ref, send_ref, keep_ref, xtail_ref, btail_ref, state,
        xext, bext,
    ) = refs
    span = pos_ref.shape[0]
    n = gotx_ref.shape[0]
    inner = wz_ref.shape[1]
    width = gotx_ref.shape[1]
    state_size = wbc_ref.shape[1] // 2
    taps = vb_ref.shape[0] - 1
    group = LANES // head_size
    step = pl.program_id(0)
    base = (first + step) * span
    ends = row_ends(ids_ref, lengths_ref)
    cxw_ref, cbw_ref = vx_ref, vb_ref
    bias_x, skip, ggain = (vx_ref[taps + k : taps + k + 1] for k in range(3))

    @pl.when(step == 0)
    def _():
        xext[0:8] = xtail_in[...] if first else jnp.zeros((8, inner), F32)
        bext[0:8] = btail_in[...] if first else jnp.zeros((8, 2 * state_size), F32)
        state[...] = state_in[...] if first else jnp.zeros_like(state)

    onehot = (pos_ref[...] == iota((span, n), 1)).astype(F32).astype(BF)
    x = dot(onehot, gotx_ref[...])
    xd_ref[...] = x.astype(BF)
    r_in = lax.rsqrt(jnp.sum(x * x, axis=1, keepdims=True) * (1.0 / width) + EPSILON)
    rin_ref[...] = r_in
    h = (x * r_in * gain_ref[...]).astype(BF)
    ht_ref[...] = h.T
    z = dot(h, wz_ref[...])
    z_ref[...] = z
    xs = dot(h, wx_ref[...])
    bc = dot(h, wbc_ref[...])
    dtr = dot(h, wdt_ref[...])
    dtr_ref[...] = dtr
    xs_ref[...] = xs.astype(BF)
    bcv_ref[...] = bc.astype(BF)

    place = base + iota((span, 1), 0)
    seg_here = seg_of(ends, place)
    xext[8 : 8 + span] = xs
    bext[8 : 8 + span] = bc
    px = bias_x + cxw_ref[taps - 1 : taps] * xs
    pbc = vb_ref[taps : taps + 1] + cbw_ref[taps - 1 : taps] * bc
    for k in range(1, taps):
        same = (seg_of(ends, place - k) == seg_here).astype(F32)
        px = px + cxw_ref[taps - 1 - k : taps - k] * (xext[8 - k : 8 - k + span] * same)
        pbc = pbc + cbw_ref[taps - 1 - k : taps - k] * (bext[8 - k : 8 - k + span] * same)
    xext[0:8] = xs[span - 8 :]
    bext[0:8] = bc[span - 8 :]
    xtail_ref[...] = xs[span - 8 :]
    btail_ref[...] = bc[span - 8 :]
    px_ref[...] = px
    pbc_ref[...] = pbc
    u = px * jax.nn.sigmoid(px)
    bcc = pbc * jax.nn.sigmoid(pbc)
    b_rows = bcc[:, :state_size].astype(BF)
    c_rows = bcc[:, state_size:].astype(BF)

    dt = softplus(dtr + vh_ref[0:1])
    cum, head_decay, tail_decay, seg_c, _ = decays(ends, base, span, dt, vh_ref[1:2])
    cum_t = cum.T
    dt_w, head_w, tail_w = widen([dt, head_decay, tail_decay], head_size, inner)
    udt = u * dt_w
    seg_r = seg_of(ends, base + iota((1, span), 1))
    counts = (seg_c == seg_r) & (iota((span, span), 0) >= iota((span, span), 1))
    never = jnp.where(counts, 0.0, NEVER)
    scores = dot_t(c_rows, b_rows)
    entering = state[...]
    state_out_ref[0] = entering
    masks = half_masks(group)
    pieces = []
    for tile in range(inner // LANES):
        lanes = slice(tile * LANES, (tile + 1) * LANES)
        block = udt[:, lanes]
        total = None
        for k in range(group):
            head = tile * group + k
            decay = jnp.exp(cum[:, head : head + 1] - cum_t[head : head + 1, :] + never)
            term = dot((decay * scores).astype(BF), (block * masks[k]).astype(BF))
            total = term if total is None else total + term
        pieces.append(total)
    y = jnp.concatenate(pieces, axis=1)
    y = y + dot(c_rows, entering.astype(BF)) * head_w
    y = y + skip * u
    y_ref[...] = y
    b_t = bcc[:, :state_size].T.astype(BF)
    state[...] = head_w[span - 1 : span] * entering + dot(b_t, (udt * tail_w).astype(BF))
    gated = y * (z * jax.nn.sigmoid(z))
    squares = jnp.sum(gated * gated, axis=1, keepdims=True)
    stat_ref[0] = jnp.broadcast_to(squares, (span, LANES)).T[0:8]
    g = (gated * ggain).astype(BF)
    g_ref[...] = g
    mix = dot(g, wout_ref[...]).astype(BF)
    cols = width // shares
    hand_out(send_ref, keep_ref, ids_ref[1], [mix[:, j * cols : (j + 1) * cols] for j in range(shares)])


def run_fwd(part, scalars, sizes, got_x, pos, vectors, weights, before, deps):
    head_size, shares = sizes
    n, width = got_x.shape
    gain, vx, vb, vh = vectors
    w_z, w_x, w_bc, w_dt, w_out = weights
    inner = w_z.shape[1]
    two = w_bc.shape[1]
    span = SPAN
    first, last = part
    steps = last - first
    blocks = n // span

    def rows(c):
        return pl.BlockSpec((span, c), lambda i, *_: (first + i, 0))

    def by_block(a, c):
        return pl.BlockSpec((1, a, c), lambda i, *_: (first + i, 0, 0))

    ops = [got_x, pos, gain, w_z, w_x, w_bc, w_dt, vx, vb, vh, w_out]
    specs = [whole(o.shape) for o in ops]
    specs[1] = rows(1)
    cols = width // shares
    part_spec = pl.BlockSpec((shares // 2, span, cols), lambda i, *_: (0, i, 0))
    outs = [
        ((n, width), BF, rows(width)),
        ((width, n), BF, pl.BlockSpec((width, span), lambda i, *_: (0, first + i))),
        ((n, 1), F32, rows(1)),
        ((n, inner), F32, rows(inner)),
        ((n, inner), BF, rows(inner)),
        ((n, inner), F32, rows(inner)),
        ((n, inner), F32, rows(inner)),
        ((n, two), BF, rows(two)),
        ((n, two), F32, rows(two)),
        ((n, LANES), F32, rows(LANES)),
        ((n, inner), BF, rows(inner)),
        ((blocks, 8, span), F32, by_block(8, span)),
        ((blocks, two // 2, inner), F32, by_block(two // 2, inner)),
        ((shares // 2, steps * span, cols), BF, part_spec),
        ((shares // 2, steps * span, cols), BF, part_spec),
        ((8, inner), F32, whole((8, inner))),
        ((8, two), F32, whole((8, two))),
        ((two // 2, inner), F32, whole((two // 2, inner))),
    ]
    keep = []
    if before is not None:
        carry = list(before[15:18])
        ops += carry
        specs += [whole(o.shape) for o in carry]
        keep = list(enumerate(before[:13]))
    return call(
        functools.partial(fwd_kernel, sizes, first), ops, specs, outs, f"forward_{first}", grid=(steps,),
        scalars=scalars, deps=deps, keep=keep, flops=2 * steps * span * width * 5 * inner,
        scratch=[pltpu.VMEM((span + 8, inner), F32), pltpu.VMEM((span + 8, two), F32)],
    )


def dots_kernel(ids_ref, lengths_ref, pos_ref, dyn_ref, g_ref, stat_ref, out_ref, stat_out_ref):
    span = pos_ref.shape[0]
    n = dyn_ref.shape[0]
    base = pl.program_id(0) * span
    full = row_ends(ids_ref, lengths_ref)[-1]
    onehot = (pos_ref[...] == iota((span, n), 1)) & (base + iota((span, 1), 0) < full)
    dyn = dot(onehot.astype(F32).astype(BF), dyn_ref[...])
    out_ref[...] = dyn.astype(BF)
    inner_dot = jnp.sum(dyn * g_ref[...].astype(F32), axis=1, keepdims=True)
    as_row = jnp.broadcast_to(inner_dot, (span, LANES)).T[0:8]
    stat_out_ref[0] = jnp.where(iota((8, span), 0) == 0, stat_ref[0], as_row)


def run_dots(scalars, pos, got_dyn, g, stat, deps):
    n, inner = got_dyn.shape
    span = SPAN
    rows = pl.BlockSpec((span, inner), lambda i, *_: (i, 0))
    stats = pl.BlockSpec((1, 8, span), lambda i, *_: (i, 0, 0))
    return call(
        dots_kernel, [pos, got_dyn, g, stat],
        [pl.BlockSpec((span, 1), lambda i, *_: (i, 0)), whole((n, inner)), rows, stats],
        [((n, inner), BF, rows), (stat.shape, F32, stats)], "row_dots", grid=(n // span,), scalars=scalars, deps=deps,
        flops=2 * n * n * inner,
    )


def bwd_kernel(
    sizes, last, blocks, ids_ref, lengths_ref, stat_ref, dyn_ref, z_ref, xs_ref, px_ref, y_ref, bcv_ref, pbc_ref,
    dtr_ref, xd_ref, rin_ref, state_ref, gain_ref, wz_ref, wx_ref, wbc_ref, wdt_ref, vx_ref, vb_ref, vh_ref, *refs,
):
    head_size, shares = sizes
    newest = last == blocks
    if not newest:
        before, refs = refs[:8], refs[8:]
    (
        cols_ref, send_ref, keep_ref, *carry, xext, bext, extra,
    ) = refs
    xhead_ref, bhead_ref, dstate, across, accx_ref, accb_ref, acch_ref, accd_ref = carry
    span, inner = z_ref.shape
    width = xd_ref.shape[1]
    two = pbc_ref.shape[1]
    early = cols_ref.shape[1] - 2 * inner
    state_size = two // 2
    taps = vb_ref.shape[0] - 1
    group = LANES // head_size
    units = inner * shares
    step = pl.program_id(0)
    base = (last - 1 - step) * span
    ends = row_ends(ids_ref, lengths_ref)
    tensor = ids_ref[1]
    cxw_ref, cbw_ref = vx_ref, vb_ref
    skip, ggain = vx_ref[taps + 1 : taps + 2], vx_ref[taps + 2 : taps + 3]

    @pl.when(step == 0)
    def _():
        for k, ref in enumerate(carry):
            ref[...] = jnp.zeros_like(ref) if newest else before[k][...]
        extra[...] = jnp.zeros_like(extra)

    xext[span : span + 8] = xhead_ref[...]
    bext[span : span + 8] = bhead_ref[...]

    def add_row(ref, row, value):
        ref[row : row + 1] += jnp.sum(value, axis=0, keepdims=True)

    place = base + iota((span, 1), 0)
    stat_cols = stat_ref[0].T
    r_g = lax.rsqrt(stat_cols[:, 0:1] * (1.0 / units) + EPSILON)
    row_dot = stat_cols[:, 1:2] * (1.0 / units)
    z = z_ref[...]
    y = y_ref[...]
    dyn = dyn_ref[...].astype(F32)
    sig_z = jax.nn.sigmoid(z)
    silu_z = z * sig_z
    gated = y * silu_z
    normed = gated * r_g
    d_gated = r_g * (dyn * ggain) - normed * (r_g * r_g * row_dot)
    d_y = d_gated * silu_z
    dz = (d_gated * y * (sig_z * (1.0 + z * (1.0 - sig_z)))).astype(BF)
    cols_ref[:, early : early + inner] = dz
    add_row(accx_ref, taps + 2, dyn * normed)

    px = px_ref[...]
    sig_x = jax.nn.sigmoid(px)
    u = px * sig_x
    pbc = pbc_ref[...]
    sig_bc = jax.nn.sigmoid(pbc)
    bcc = pbc * sig_bc
    b_rows = bcc[:, :state_size].astype(BF)
    c_rows = bcc[:, state_size:].astype(BF)
    add_row(accx_ref, taps + 1, u * d_y)

    pre = dtr_ref[...] + vh_ref[0:1]
    dt = softplus(pre)
    rates = vh_ref[1:2]
    cum, head_decay, tail_decay, seg_c, seg_last = decays(ends, base, span, dt, rates)
    cum_t = cum.T
    dt_w, head_w, tail_w = widen([dt, head_decay, tail_decay], head_size, inner)
    udt = u * dt_w
    seg_r = seg_of(ends, base + iota((1, span), 1))
    counts = (seg_c == seg_r) & (iota((span, span), 1) >= iota((span, span), 0))
    never = jnp.where(counts, 0.0, NEVER)
    scores = dot_t(b_rows, c_rows)
    d_scores = jnp.zeros((span, span), F32)
    masks = half_masks(group)
    pieces = []
    for tile in range(inner // LANES):
        lanes = slice(tile * LANES, (tile + 1) * LANES)
        udt_block = udt[:, lanes]
        dy_block = d_y[:, lanes]
        dy_low = dy_block.astype(BF)
        total = None
        for k in range(group):
            head = tile * group + k
            decay = jnp.exp(cum_t[head : head + 1, :] - cum[:, head : head + 1] + never)
            d_scores = d_scores + decay * dot_t((udt_block * masks[k]).astype(BF), dy_low)
            term = dot((decay * scores).astype(BF), (dy_block * masks[k]).astype(BF))
            total = term if total is None else total + term
        pieces.append(total)
    in_block = jnp.concatenate(pieces, axis=1)
    d_state = dstate[...]
    d_state_low = d_state.astype(BF)
    entering = state_ref[0]
    entering_low = entering.astype(BF)
    at_end = dot(b_rows, d_state_low)
    at_start = dot(c_rows, entering_low)
    d_udt = in_block + at_end * tail_w
    from_start = (d_y * head_w).astype(BF)
    to_end = (udt * tail_w).astype(BF)
    d_c = dot(d_scores.T.astype(BF), b_rows) + dot_t(from_start, entering_low)
    d_b = dot(d_scores.astype(BF), c_rows) + dot_t(to_end, d_state_low)
    y_block = y - skip * u - at_start * head_w
    balance = d_y.astype(BF).astype(F32) * y_block - udt.astype(BF).astype(F32) * in_block
    balance = balance + from_start.astype(F32) * at_start - to_end.astype(F32) * at_end
    v_part = head_sums(u * d_udt, head_size, split2)
    mask_low = counts.astype(F32).astype(BF)
    d_la = fixed_sum(mask_low, head_sums(balance, head_size, split3))
    d_la = d_la + jnp.where(seg_c == seg_last, across[0:1], 0.0)
    d_dt = v_part + rates * d_la
    d_pre = d_dt * jax.nn.sigmoid(pre)
    add_row(acch_ref, 0, d_la * dt * rates)
    add_row(acch_ref, 1, d_pre)

    c_t = bcc[:, state_size:].T.astype(BF)
    d_enter = dot(c_t, from_start) + head_w[span - 1 : span] * d_state
    dstate[...] = d_enter
    crossing = jnp.sum(d_enter.astype(BF).astype(F32) * entering, axis=0, keepdims=True)
    across[...] = head_sums(jnp.broadcast_to(crossing, (8, inner)), head_size, split3)

    d_u = skip * d_y + dt_w * d_udt
    d_px = d_u * (sig_x * (1.0 + px * (1.0 - sig_x)))
    d_pbc = jnp.concatenate([d_b, d_c], axis=1) * (sig_bc * (1.0 + pbc * (1.0 - sig_bc)))
    xext[0:span] = d_px
    bext[0:span] = d_pbc
    seg_here = seg_of(ends, place)
    xs = xs_ref[...].astype(F32)
    bcv = bcv_ref[...].astype(F32)
    d_xs = cxw_ref[taps - 1 : taps] * d_px
    d_bc = cbw_ref[taps - 1 : taps] * d_pbc
    add_row(accx_ref, taps, d_px)
    add_row(accb_ref, taps, d_pbc)
    add_row(accx_ref, taps - 1, d_px * xs)
    add_row(accb_ref, taps - 1, d_pbc * bcv)
    for k in range(1, taps):
        later = place + k
        same = ((seg_of(ends, later) == seg_here) & (later < blocks * span)).astype(F32)
        tap = taps - 1 - k
        xk = xext[k : k + span] * same
        bk = bext[k : k + span] * same
        d_xs = d_xs + cxw_ref[tap : tap + 1] * xk
        d_bc = d_bc + cbw_ref[tap : tap + 1] * bk
        add_row(accx_ref, tap, xk * xs)
        add_row(accb_ref, tap, bk * bcv)
    xhead_ref[...] = d_px[0:8]
    bhead_ref[...] = d_pbc[0:8]
    dx_low = d_xs.astype(BF)
    dbc_low = d_bc.astype(BF)
    ddt_low = d_pre.astype(BF)
    cols_ref[:, 0:two] = dbc_low
    cols_ref[:, two : two + LANES] = ddt_low
    cols_ref[:, early + inner : early + 2 * inner] = dx_low
    for at in range(two + LANES, early, LANES):
        cols_ref[:, at : at + LANES] = jnp.zeros((span, LANES), BF)
    back = dot_t(dz, wz_ref[...]) + dot_t(dx_low, wx_ref[...])
    back = back + dot_t(ddt_low, wdt_ref[...]) + dot_t(dbc_low, wbc_ref[...])
    x_hat = xd_ref[...].astype(F32) * rin_ref[...]
    shared = back * x_hat
    add_row(accd_ref, 0, shared)
    inner_dot = jnp.sum(shared * gain_ref[...], axis=1, keepdims=True)
    low = back.astype(BF)
    cols = width // shares
    row = jnp.broadcast_to(inner_dot, (span, LANES)).T[0:1]
    for k in range(span // LANES):
        extra[k : k + 1] = row[:, k * LANES : (k + 1) * LANES]
    hand_out(send_ref, keep_ref, tensor, [low[:, j * cols : (j + 1) * cols] for j in range(shares)])
    more = extra[...].astype(BF)
    for part in range(shares // 2):
        send_ref[part, span : span + EXTRA, 0:LANES] = more
        keep_ref[part, span : span + EXTRA, 0:LANES] = more


def run_bwd(part, scalars, sizes, stat, dyn, kept, vectors, weights, before, deps):
    head_size, shares = sizes
    z, xs, px, y, bcv, pbc, dtr, xd, rin, states = kept
    w_z, w_x, w_bc, w_dt = weights
    n, inner = z.shape
    width = xd.shape[1]
    two = pbc.shape[1]
    span = SPAN
    first, last = part
    steps = last - first
    blocks = n // span
    cols = width // shares

    def rows(c):
        return pl.BlockSpec((span, c), lambda i, *_: (last - 1 - i, 0))

    def by_block(a, c):
        return pl.BlockSpec((1, a, c), lambda i, *_: (last - 1 - i, 0, 0))

    ops = [stat, dyn, z, xs, px, y, bcv, pbc, dtr, xd, rin, states]
    specs = [by_block(8, span), *(rows(o.shape[1]) for o in ops[1:11]), by_block(two // 2, inner)]
    fixed = [vectors[0], w_z, w_x, w_bc, w_dt, *vectors[1:]]
    part_spec = pl.BlockSpec((shares // 2, span + EXTRA, cols), lambda i, *_: (0, steps - 1 - i, 0))
    wide = -(-(2 * inner + two + LANES) // (2 * LANES)) * (2 * LANES)
    sums = [(8, inner), (8, two), (two // 2, inner), (8, LANES), (8, inner), (8, two), (8, LANES), (8, width)]
    outs = [
        ((n, wide), BF, rows(wide)),
        ((shares // 2, steps * (span + EXTRA), cols), BF, part_spec),
        ((shares // 2, steps * (span + EXTRA), cols), BF, part_spec),
        *((c, F32, whole(c)) for c in sums),
    ]
    keep = []
    if before is not None:
        fixed += before[3:]
        keep = list(enumerate(before[:1]))
    return call(
        functools.partial(bwd_kernel, sizes, last, blocks), ops + fixed, specs + [whole(o.shape) for o in fixed], outs,
        f"backward_{first}", grid=(steps,), scalars=scalars, deps=deps, keep=keep,
        flops=2 * steps * span * width * 6 * inner,
        scratch=[pltpu.VMEM((span + 8, inner), F32), pltpu.VMEM((span + 8, two), F32), pltpu.VMEM((EXTRA, LANES), F32)],
    )


def outer_kernel(groups, ids_ref, left_ref, right_ref, send_ref, keep_ref):
    each = groups // pl.num_programs(0)
    rows = left_ref.shape[0] // each
    low = dot(left_ref[...], right_ref[...]).astype(BF)
    at = pl.program_id(0) * each
    for i in range(each):
        place = ids_ref[0] ^ (at + i)

        @pl.when(place % 2 == 1)
        def _(i=i, place=place):
            send_ref[place // 2] = low[i * rows : (i + 1) * rows]

        @pl.when(place % 2 == 0)
        def _(i=i, place=place):
            keep_ref[place // 2] = low[i * rows : (i + 1) * rows]


def outer(ids, groups, left_t, right, first, count, deps=()):
    width, n = left_t.shape
    steps = 4
    rows = width // groups
    out = ((groups // 2, rows, count), BF, whole((groups // 2, rows, count)))
    return call(
        functools.partial(outer_kernel, groups), [left_t, right],
        [pl.BlockSpec((width // steps, n), lambda i, *_: (i, 0)), pl.BlockSpec((n, count), lambda *_: (0, first // count))],
        [out, out], "outer",
        grid=(steps,), scalars=[ids], deps=deps, flops=2 * n * width * count,
    )


def put_yn_kernel(units, ids_ref, lengths_ref, pos_ref, stat_ref, data_ref, out_ref, hot_ref, scale_ref):
    n = pos_ref.shape[1]
    blocks, _, span = stat_ref.shape

    @pl.when(pl.program_id(0) == 0)
    def _():
        hot_ref[...] = (pos_ref[...] == iota((n, n), 0)).astype(F32).astype(BF)
        full = row_ends(ids_ref, lengths_ref)[-1]
        for k in range(blocks):
            squares = stat_ref[k].T[:, 0:1]
            valid = k * span + iota((span, 1), 0) < full
            scale = lax.rsqrt(squares * (1.0 / units) + EPSILON)
            scale_ref[k * span : (k + 1) * span] = jnp.where(valid, scale, 0.0)

    yn = (data_ref[...].astype(F32) * scale_ref[...]).astype(BF)
    out_ref[...] = dot(hot_ref[...], yn).astype(BF)


def put_yn(scalars, units, pos, stat, g, deps):
    n, width = g.shape
    tile = next((t for t in (384, 256) if width % t == 0), width)
    spec = pl.BlockSpec((n, tile), lambda i, *_: (0, i))
    return call(
        functools.partial(put_yn_kernel, units), [pos, stat, g], [whole(pos.shape), whole(stat.shape), spec],
        [((n, width), BF, spec)], "put_yn", grid=(width // tile,), scalars=scalars, deps=deps,
        scratch=[pltpu.VMEM((n, n), BF), pltpu.VMEM((n, 1), F32)], flops=2 * n * n * width,
    )[0]


def add_up(refs, counts):
    pieces, at = [], 0
    for count in counts:
        total = refs[at][0].astype(F32)
        for ref in refs[at + 1 : at + count]:
            total = total + ref[0].astype(F32)
        pieces.append(total)
        at += count
    return jnp.concatenate(pieces, axis=0)


def send_out_kernel(units, counts, ids_ref, lengths_ref, pos_ref, stat_ref, x_ref, *refs):
    *terms, out_ref, sq_ref = refs
    n = pos_ref.shape[1]
    blocks, _, span = stat_ref.shape
    mix = add_up(terms, counts)
    squares = jnp.concatenate([stat_ref[k].T[:, 0:1] for k in range(blocks)], axis=0)
    valid = (iota((n, 1), 0) < row_ends(ids_ref, lengths_ref)[-1]).astype(F32)
    mix = mix * (lax.rsqrt(squares * (1.0 / units) + EPSILON) * valid)
    x = x_ref[...].astype(F32)
    out = (x + mix).astype(BF)
    full = out.astype(F32)
    onehot = (pos_ref[...] == iota((n, n), 0)).astype(F32).astype(BF)
    out_ref[...] = dot(onehot, out).astype(BF)
    sq_ref[...] = jnp.zeros_like(sq_ref)
    for k, v in enumerate((x * x * valid, mix * mix, full * full * valid)):
        sq_ref[k : k + 1] = jnp.sum(v, axis=0, keepdims=True)


def send_dx_kernel(width, span, counts, pos_ref, x_ref, rin_ref, gain_ref, *refs):
    *terms, out_ref = refs
    n = pos_ref.shape[1]
    total = add_up(terms, counts)
    each = span + EXTRA
    d_h, dots = [], []
    for k in range(n // span):
        d_h.append(total[k * each : k * each + span])
        rows = total[k * each + span : k * each + span + 8, 0:LANES].T
        dots += [rows[:, i : i + 1] for i in range(span // LANES)]
    d_h, dots = jnp.concatenate(d_h, axis=0), jnp.concatenate(dots, axis=0)
    r_in = rin_ref[...]
    x_hat = x_ref[...].astype(F32) * r_in
    dx = (r_in * (d_h * gain_ref[...] - x_hat * (dots * (1.0 / width)))).astype(BF)
    onehot = (pos_ref[...] == iota((n, n), 0)).astype(F32).astype(BF)
    out_ref[...] = dot(onehot, dx).astype(BF)


def term_ops(groups_of_terms):
    ops = [t for terms in groups_of_terms for t in terms]
    specs = [pl.BlockSpec((1,) + o.shape[1:], lambda *_: (0, 0, 0)) for o in ops]
    return ops, specs, [len(terms) for terms in groups_of_terms]


def swap(v, axis, bit):
    size = lax.axis_size(axis)
    return lax.ppermute(v, axis, [(i, i ^ (1 << bit)) for i in range(size)])


def bits_of(axis):
    return lax.axis_size(axis).bit_length() - 1


class Halving:
    def __init__(self, send, keep, axis, order):
        self.axis, self.order = axis, order
        self.left = list(range(len(order) - 1, 0, -1))
        shape = (2,) * len(self.left) + keep.shape[1:]
        self.terms = [keep.reshape(shape)]
        self.sent = send.reshape(shape)
        self.got = None
        self.flat = [keep]
        self.at = 0

    def launch(self):
        if self.sent is not None:
            self.got = swap(self.sent, self.axis, self.order[self.at])
            self.sent = None
        return self

    def take(self):
        got, self.got = self.got, None
        self.terms.append(got)
        self.flat.append(got.reshape((-1,) + got.shape[len(self.left) :]))
        self.at += 1
        return self

    def advance(self):
        if self.left:
            dim = self.left.index(self.order[self.at])
            self.left.pop(dim)
            odd = [lax.index_in_dim(t, 1, dim, keepdims=False).astype(F32) for t in self.terms]
            self.sent = sum(odd[1:], odd[0]).astype(BF)
            self.terms = [lax.index_in_dim(t, 0, dim, keepdims=False) for t in self.terms]
        return self

    def land(self):
        return self if self.got is None else self.take().advance()

    def split(self, at, order):
        other = copy.copy(self)
        other.left, other.order = list(self.left), order
        other.terms = [t[..., at:] for t in self.terms]
        self.terms = [t[..., :at] for t in self.terms]
        return other

    def finish(self):
        while self.sent is not None or self.got is not None:
            self.launch().land()
        return self

    def total(self):
        self.finish()
        wide = [t.astype(F32) for t in self.terms]
        return sum(wide[1:], wide[0])


def fence(halvings, *values):
    held = [(h.sent, h.got) for h in halvings]
    flat, tree = jax.tree.flatten((held, values))
    held, values = tree.unflatten(lax.optimization_barrier(flat))
    for h, (sent, got) in zip(halvings, held, strict=True):
        h.sent, h.got = sent, got
    return values


def exchange(v, axis):
    groups = lax.axis_size(axis)
    rows = v.shape[0]
    parts = v.reshape((groups, rows // groups) + v.shape[1:])
    return lax.all_to_all(parts, axis, split_axis=0, concat_axis=0, tiled=True).reshape(v.shape)


def sum_at_once(v, axis):
    size = lax.axis_size(axis)
    others = [lax.ppermute(v, axis, [(i, i ^ k) for i in range(size)]) for k in range(1, size)]
    return sum((o.astype(F32) for o in others), v.astype(F32))


def pad_lanes(v):
    return jnp.pad(v, [(0, 0)] * (v.ndim - 1) + [(0, LANES - v.shape[-1])])


def local(
    stream, out_grad, seq_lengths, anchor, norm_gain, w_z, w_x, w_bc, w_dt, conv_x_w, conv_x_b, conv_bc_w,
    conv_bc_b, dt_bias, a_log, d_skip, gated_gain, w_out,
):
    groups = lax.axis_size("dp")
    shares = lax.axis_size("tensor")
    me = lax.axis_index("dp")
    tensor = lax.axis_index("tensor")
    n, width = stream.shape
    per = n // groups
    cols = width // shares
    first_col = tensor * cols
    inner = w_z.shape[1]
    heads = w_dt.shape[1]
    head_size = inner // heads
    two = w_bc.shape[1]
    taps = conv_x_w.shape[0]
    sizes = (head_size, shares)
    units = inner * shares
    ids = jnp.stack([me, tensor]).astype(I32)
    scalars = [ids, seq_lengths]
    tensor_order = list(range(bits_of("tensor")))
    dp_bits = bits_of("dp")
    order_a = list(range(dp_bits))
    order_b = order_a[:1] + order_a[1:][::-1]

    pos_row, pos_col, requests = find_places(anchor, n, per)
    wanted = lax.all_to_all(
        requests.reshape(groups, per), "dp", split_axis=0, concat_axis=0, tiled=True
    ).reshape(1, n)
    got_x = exchange(move_rows(pick_kernel, wanted, stream, name="pick_x"), "dp")
    gain = norm_gain[None]
    vx = jnp.concatenate([conv_x_w, conv_x_b[None], jnp.repeat(d_skip, head_size)[None], gated_gain[None]])
    vb = jnp.concatenate([conv_bc_w, conv_bc_b[None]])
    vh = pad_lanes(jnp.stack([dt_bias, -jnp.exp(a_log)]))
    w_dt_pad = pad_lanes(w_dt)
    dy_t = out_grad.T
    gain_cols = lax.dynamic_slice_in_dim(norm_gain, first_col, cols, 0)[None]
    dy_cols = lax.dynamic_slice_in_dim(out_grad, first_col, cols, 1)
    d_yn_src = jnp.einsum("td,id->ti", out_grad, w_out, preferred_element_type=F32).astype(BF)
    dyn_send = move_rows(
        pick_kernel, wanted, d_yn_src, name="pick_dyn", deps=[gain, vx, vb, vh, w_dt_pad, dy_t, gain_cols, dy_cols]
    )
    got_dyn = exchange(dyn_send, "dp")

    vectors = (gain, vx, vb, vh)
    first, second = FORWARD
    weights = (w_z, w_x, w_bc, w_dt_pad)
    got = run_fwd(first, scalars, sizes, got_x, pos_col, vectors, (*weights, w_out), None, [dyn_send])
    mix_1 = Halving(got[13], got[14], "tensor", tensor_order).launch()
    got = run_fwd(second, scalars, sizes, got_x, pos_col, vectors, (*weights, w_out), got, [])
    mix_2 = Halving(got[13], got[14], "tensor", tensor_order)
    (xd, h_t, rin, z, xs, px, y, bcv, pbc, dtr, g, stat, states) = got[:13]
    x_cols = lax.dynamic_slice_in_dim(xd, first_col, cols, 1)
    stat, x_cols = fence([mix_1], stat, x_cols)
    mix_1.land()
    dyn, stat = run_dots(scalars, pos_col, got_dyn, g, stat, [])
    stat = sum_at_once(stat, "tensor")
    (stat,) = fence([mix_1, mix_2], stat)

    kept = (z, xs, px, y, bcv, pbc, dtr, xd, rin, states)
    yn_send = put_yn(scalars, units, pos_row, stat, g, [])
    yn_back = exchange(yn_send, "dp")
    mix_1.launch()
    mix_2.launch()
    got = run_bwd(BACKWARD[0], scalars, sizes, stat, dyn, kept, vectors, weights, None, [yn_send])
    back_1 = Halving(got[1], got[2], "tensor", tensor_order)
    yn_back, carry = fence([mix_1, mix_2, back_1], yn_back, got[3:])
    got = [*got[:3], *carry]
    mix_1.land()
    mix_2.land()
    back_1.launch()
    mix_1.launch()
    mix_2.launch()
    yn_src = move_rows(put_kernel, wanted, yn_back, name="place_yn")
    h_out = Halving(*outer(ids, groups, dy_t, yn_src, 0, inner), "dp", order_b)
    got = run_bwd(BACKWARD[1], scalars, sizes, stat, dyn, kept, vectors, weights, got, [h_out.sent])
    h_out.launch().land()
    back_2 = Halving(got[1], got[2], "tensor", tensor_order)
    grad_cols, tail = got[0], got[7:]
    grad_cols, tail, x_cols = fence([mix_1, mix_2, back_1, back_2, h_out], grad_cols, tail, x_cols)
    acc_x, acc_b, acc_h, acc_d = tail

    mix_1.land().finish()
    mix_2.land().finish()
    back_1.land()
    back_2.launch()
    back_1.launch()
    h_out.launch()
    half = grad_cols.shape[1] // 2
    h_a = Halving(*outer(ids, groups, h_t, grad_cols, 0, 2 * half), "dp", order_a)
    (x_cols,) = fence([back_1, back_2, h_out, h_a], x_cols)

    back_2.land().launch()
    back_1.land().finish()
    h_a.launch()
    ops, specs, counts = term_ops([mix_1.flat, mix_2.flat])
    ops = [pos_row, stat, x_cols, *ops]
    out_send, squares = call(
        functools.partial(send_out_kernel, units, counts), ops, [*(whole(o.shape) for o in ops[:3]), *specs],
        [((n, cols), BF, whole((n, cols))), ((8, cols), F32, whole((8, cols)))], "send_out", scalars=scalars,
        flops=2 * n * n * cols,
    )
    flat = [acc_x, acc_h, acc_b[: taps + 1], acc_d[0], jnp.sum(squares, axis=1)]
    flat = [f.reshape(-1) for f in flat]
    lens = [f.shape[0] for f in flat]
    small = jnp.concatenate(flat).astype(BF)
    small = jnp.pad(small, (0, -sum(lens) % (16 * cols))).reshape(1, -1, cols)
    small = jnp.broadcast_to(small, (groups,) + small.shape[1:])
    sent = jnp.concatenate([out_send.reshape(groups, per, cols), small], axis=1)
    out_back = lax.all_to_all(sent, "dp", split_axis=0, concat_axis=0, tiled=True)
    (x_cols,) = fence([back_2, h_a], x_cols)

    back_2.land().finish()
    h_a.take()
    h_b = h_a.split(half, order_b)
    h_a.advance().launch()
    h_b.advance().launch()
    h_out.land().launch()
    back_ops, back_specs, back_counts = term_ops([back_2.flat, back_1.flat])
    ops = [pos_row, x_cols, rin, gain_cols]
    dx_send = call(
        functools.partial(send_dx_kernel, width, SPAN, back_counts), [*ops, *back_ops],
        [*(whole(o.shape) for o in ops), *back_specs],
        [((n, cols), BF, whole((n, cols)))], "send_dx", flops=2 * n * n * cols,
    )[0]
    dx_send, out_back = fence([], dx_send, out_back)

    dx_back = exchange(dx_send, "dp")
    out_rows = out_back[:, :per].reshape(n, cols)
    out_final = move_rows(put_kernel, wanted, out_rows, name="place_out")
    small = jnp.sum(out_back[:, per:].astype(F32), axis=0).reshape(-1)
    out_final, small, dy_cols = fence([h_a, h_b, h_out], out_final, small, dy_cols)

    h_a.land().launch()
    h_b.land().launch()
    h_out.land()
    dx_final = move_rows(put_add_kernel, wanted, dx_back, dy_cols, name="place_dx")
    (dx_final,) = fence([h_a, h_b], dx_final)

    g_out = h_out.total()
    g_a = h_a.total()
    g_b = h_b.total()
    early = 2 * half - 2 * inner
    g_dt = g_a[:, two : two + heads]
    g_z = jnp.concatenate([g_a[:, early:], g_b[:, : early + inner - half]], axis=1)
    g_x = g_b[:, early + inner - half :]

    own = lens[0] + lens[1]
    s_x = small[: lens[0]].reshape(acc_x.shape)
    s_h = small[lens[0] : own].reshape(acc_h.shape)
    both = small[own : sum(lens)]
    both = jnp.pad(both, (0, -both.shape[0] % (8 * two))).reshape(-1, two)
    both = sum_at_once(jnp.concatenate([g_a[:, :two], both]).astype(BF), "tensor")
    g_bc = both[: g_a.shape[0]]
    both = both[g_a.shape[0] :].reshape(-1)
    s_b = both[: lens[2]].reshape(taps + 1, two)
    s_d = both[lens[2] : lens[2] + lens[3]]
    s_sq = both[lens[2] + lens[3] : lens[2] + lens[3] + 3]
    g_gain = lax.dynamic_slice_in_dim(s_d, first_col, cols, 0)
    rms = jnp.sqrt(s_sq / (jnp.sum(seq_lengths).astype(F32) * width))
    g_skip = jnp.sum(s_x[taps + 1].reshape(heads, head_size), axis=1)
    return (
        out_final, dx_final, g_gain, g_z, g_x, g_bc, g_dt, s_x[:taps], s_x[taps], s_b[:taps], s_b[taps],
        s_h[1, :heads], s_h[0, :heads], g_skip, s_x[taps + 2], g_out.T, rms,
    )


def solution(mesh):
    in_specs = (
        P("dp", None), P("dp", None), P(), P("dp"), P(), P(None, "tensor"), P(None, "tensor"), P(),
        P(None, "tensor"), P(None, "tensor"), P("tensor"), P(), P(), P("tensor"), P("tensor"), P("tensor"),
        P("tensor"), P("tensor", None),
    )
    out_specs = (
        P("dp", "tensor"), P("dp", "tensor"), P("tensor"), P("dp", "tensor"), P("dp", "tensor"), P("dp", None),
        P("dp", "tensor"), P(None, "tensor"), P("tensor"), P(), P(), P("tensor"), P("tensor"), P("tensor"),
        P("tensor"), P("tensor", "dp"), P(),
    )
    return jax.shard_map(local, mesh=mesh, in_specs=in_specs, out_specs=out_specs, check_vma=False)
```

```python
import copy
import functools

import jax
import jax.numpy as jnp
from jax import lax
from jax.experimental import pallas as pl
from jax.experimental.pallas import tpu as pltpu
from jax.sharding import PartitionSpec as P

SPAN = 256
EPSILON = 1e-05
LANES = 128
NEVER = -1e30
BF = jnp.bfloat16
F32 = jnp.float32
I32 = jnp.int32
MIB = 1 << 20
EXTRA = 16
FORWARD = ((0, 2), (2, 4))
BACKWARD = ((2, 4), (0, 2))


def dot(a, b):
    return jnp.dot(a, b, preferred_element_type=F32)


def dot_t(a, b):
    return lax.dot_general(a, b, (((1,), (1,)), ((), ())), preferred_element_type=F32)


def iota(shape, dim):
    return lax.broadcasted_iota(I32, shape, dim)


def split2(v):
    hi = v.astype(BF)
    return hi, (v - hi.astype(F32)).astype(BF)


def split3(v):
    hi = v.astype(BF)
    rest = v - hi.astype(F32)
    mid = rest.astype(BF)
    return hi, mid, (rest - mid.astype(F32)).astype(BF)


def params(mib=56, **more):
    return pltpu.CompilerParams(vmem_limit_bytes=mib * MIB, **more)


def whole(shape):
    rank = len(shape)
    return pl.BlockSpec(shape, lambda *_: (0,) * rank)


def call(kernel, ins, in_specs, outs, name, grid=(1,), scalars=(), deps=(), scratch=(), flops=0, keep=(), mib=56):
    n_scalars, n_in, n_extra = len(scalars), len(ins), len(keep) + len(deps)

    def body(*refs):
        kernel(*refs[: n_scalars + n_in], *refs[n_scalars + n_in + n_extra :])

    extra = [a for _, a in keep] + list(deps)
    first = n_scalars + n_in
    moved = sum(a.size * a.dtype.itemsize for a in ins) + sum(
        functools.reduce(lambda p, q: p * q, o[0]) * 2 for o in outs
    )
    return pl.pallas_call(
        body,
        grid_spec=pltpu.PrefetchScalarGridSpec(
            num_scalar_prefetch=n_scalars,
            grid=grid,
            in_specs=[*in_specs, *(pl.BlockSpec(memory_space=pl.ANY) for _ in extra)],
            out_specs=[o[2] for o in outs],
            scratch_shapes=list(scratch),
        ),
        out_shape=[jax.ShapeDtypeStruct(o[0], o[1]) for o in outs],
        input_output_aliases={first + k: at for k, (at, _) in enumerate(keep)},
        compiler_params=params(mib),
        cost_estimate=pl.CostEstimate(flops=flops, bytes_accessed=moved, transcendentals=0),
        name=name,
    )(*scalars, *ins, *extra)


def index_kernel(per, src_ref, pos_row_ref, pos_col_ref, req_ref):
    n = src_ref.shape[1]
    rows = src_ref[...]
    cols = rows.T
    src_row, loc_row = rows[0:1], rows[1:2]
    src_col = cols[:, 0:1]
    member = (src_col == iota((n, LANES), 1).astype(F32)).astype(F32)
    member_t = (src_row == iota((LANES, n), 0).astype(F32)).astype(F32)
    before = (iota((n, n), 1) < iota((n, n), 0)).astype(F32).astype(BF)
    before_t = (iota((n, n), 0) < iota((n, n), 1)).astype(F32).astype(BF)
    rank = jnp.sum(dot(before, member.astype(BF)) * member, axis=1, keepdims=True)
    rank_t = jnp.sum(dot(member_t.astype(BF), before_t) * member_t, axis=0, keepdims=True)
    place = (src_col * per + rank).astype(I32)
    pos_col_ref[...] = place
    pos_row_ref[...] = (src_row * per + rank_t).astype(I32)
    onehot = (place == iota((n, n), 1)).astype(F32).astype(BF)
    high = jnp.floor(loc_row * (1.0 / 32.0))
    low = loc_row - high * 32.0
    pair = jnp.where(iota((8, n), 0) == 0, high, low).astype(BF)
    found = dot(pair, onehot)
    req_ref[...] = (found[0:1] * 32.0 + found[1:2]).astype(I32)


def find_places(anchor, n, per):
    src = (anchor // n).astype(F32)
    loc = (anchor % n).astype(F32)
    rows = jnp.concatenate([src[None], loc[None], jnp.zeros((6, n), F32)])
    return pl.pallas_call(
        functools.partial(index_kernel, per),
        out_shape=(
            jax.ShapeDtypeStruct((1, n), I32),
            jax.ShapeDtypeStruct((n, 1), I32),
            jax.ShapeDtypeStruct((1, n), I32),
        ),
        compiler_params=params(),
        name="places",
    )(rows)


def pick_kernel(idx_ref, data_ref, out_ref, hot_ref):
    n = idx_ref.shape[1]

    @pl.when(pl.program_id(0) == 0)
    def _():
        col = jnp.broadcast_to(idx_ref[...].astype(F32), (8, n)).T[:, 0:1].astype(I32)
        hot_ref[...] = (col == iota((n, n), 1)).astype(F32).astype(BF)

    out_ref[...] = dot(hot_ref[...], data_ref[...]).astype(BF)


def put_kernel(idx_ref, data_ref, out_ref, hot_ref):
    n = idx_ref.shape[1]

    @pl.when(pl.program_id(0) == 0)
    def _():
        hot_ref[...] = (idx_ref[...] == iota((n, n), 0)).astype(F32).astype(BF)

    out_ref[...] = dot(hot_ref[...], data_ref[...]).astype(BF)


def put_add_kernel(idx_ref, data_ref, base_ref, out_ref, hot_ref):
    n = idx_ref.shape[1]

    @pl.when(pl.program_id(0) == 0)
    def _():
        hot_ref[...] = (idx_ref[...] == iota((n, n), 0)).astype(F32).astype(BF)

    out_ref[...] = (base_ref[...].astype(F32) + dot(hot_ref[...], data_ref[...])).astype(BF)


def move_rows(kernel, idx, *data, name, deps=()):
    n, width = data[0].shape
    tile = next((t for t in (768, 384, 256) if width % t == 0), width)
    spec = pl.BlockSpec((n, tile), lambda i, *_: (0, i))
    return call(
        kernel,
        [idx, *data],
        [whole((1, n))] + [spec] * len(data),
        [((n, width), BF, spec)],
        name,
        grid=(width // tile,),
        deps=deps,
        scratch=[pltpu.VMEM((n, n), BF)],
        flops=2 * n * n * width,
    )[0]


def row_ends(ids_ref, lengths_ref):
    me = ids_ref[0]
    ends = [lengths_ref[me, 0]]
    for k in range(1, lengths_ref.shape[1]):
        ends.append(ends[-1] + lengths_ref[me, k])
    return ends


def seg_of(ends, place):
    seg = jnp.zeros(place.shape, I32)
    for end in ends:
        seg = seg + (place >= end).astype(I32)
    return jnp.where(place < 0, -1, seg)


def seg_scalar(ends, place):
    seg = jnp.int32(0)
    for end in ends:
        seg = seg + (place >= end).astype(I32)
    return jnp.where(place < 0, jnp.int32(-1), seg)


def softplus(v):
    e = jnp.exp(-jnp.abs(v))
    w = 1.0 + e
    one = w == 1.0
    log1p = jnp.where(one, e, jnp.log(w) * (e / jnp.where(one, 1.0, w - 1.0)))
    return jnp.maximum(v, 0.0) + log1p


def widen(parts, head_size, width):
    rows = parts[0].shape[0]
    spread = (iota((2 * LANES, width), 0) % LANES == iota((2 * LANES, width), 1) // head_size)
    spread = spread.astype(F32).astype(BF)
    stacked = jnp.concatenate([jnp.concatenate(split2(p), axis=1) for p in parts], axis=0)
    out = dot(stacked, spread)
    return [out[k * rows : (k + 1) * rows] for k in range(len(parts))]


def head_sums(v, head_size, split):
    rows, width = v.shape
    gather = (iota((width, LANES), 0) // head_size == iota((width, LANES), 1)).astype(F32).astype(BF)
    pieces = split(v)
    out = dot(jnp.concatenate(pieces, axis=0), gather)
    return sum(out[k * rows : (k + 1) * rows] for k in range(len(pieces)))


def fixed_sum(mask, v):
    out = dot(mask, jnp.concatenate(split3(v), axis=1))
    w = v.shape[1]
    return out[:, :w] + out[:, w : 2 * w] + out[:, 2 * w :]


def decays(ends, base, span, dt, rates):
    place = base + iota((span, 1), 0)
    seg_c = seg_of(ends, place)
    low = (iota((span, span), 0) >= iota((span, span), 1)).astype(F32).astype(BF)
    cum = fixed_sum(low, dt * rates)
    last = cum[span - 1 : span]
    seg_before = seg_scalar(ends, base - 1)
    seg_last = seg_scalar(ends, base + span - 1)
    head_decay = jnp.where(seg_c == seg_before, jnp.exp(cum), 0.0)
    tail_decay = jnp.where(seg_c == seg_last, jnp.exp(last - cum), 0.0)
    return cum, head_decay, tail_decay, seg_c, seg_last


def half_masks(group):
    lane = iota((1, LANES), 1)
    return [(lane // (LANES // group) == k).astype(F32) for k in range(group)]


def hand_out(send_ref, keep_ref, me, pieces):
    for j, piece in enumerate(pieces):
        place = me ^ j

        @pl.when(place % 2 == 1)
        def _(piece=piece, place=place):
            send_ref[place // 2, 0 : piece.shape[0]] = piece

        @pl.when(place % 2 == 0)
        def _(piece=piece, place=place):
            keep_ref[place // 2, 0 : piece.shape[0]] = piece


def fwd_kernel(
    sizes, first, ids_ref, lengths_ref, gotx_ref, pos_ref, gain_ref, vx_ref, vb_ref, vh_ref,
    wz_src, wx_src, wbc_src, wdt_src, wout_src, *refs,
):
    head_size, shares = sizes
    if first:
        xtail_in, btail_in, state_in, *refs = refs
    (
        xd_ref, ht_ref, rin_ref, z_ref, xs_ref, px_ref, y_ref, bcv_ref, pbc_ref, dtr_ref, g_ref, stat_ref,
        state_out_ref, send_ref, keep_ref, xtail_ref, btail_ref, state,
        xext, bext, wz_ref, wx_ref, wbc_ref, wdt_ref, wout_ref, sems,
    ) = refs
    sources = (wz_src, wx_src, wbc_src, wdt_src, wout_src)
    held = (wz_ref, wx_ref, wbc_ref, wdt_ref, wout_ref)
    copies = [pltpu.make_async_copy(a, b, sems.at[k]) for k, (a, b) in enumerate(zip(sources, held, strict=True))]
    span = pos_ref.shape[0]
    n = gotx_ref.shape[0]
    inner = wz_src.shape[1]
    width = gotx_ref.shape[1]
    state_size = wbc_src.shape[1] // 2
    taps = vb_ref.shape[0] - 1
    group = LANES // head_size
    step = pl.program_id(0)
    base = (first + step) * span
    ends = row_ends(ids_ref, lengths_ref)
    cxw_ref, cbw_ref = vx_ref, vb_ref
    bias_x, skip, ggain = (vx_ref[taps + k : taps + k + 1] for k in range(3))

    @pl.when(step == 0)
    def _():
        for one in copies:
            one.start()
        xext[0:8] = xtail_in[...] if first else jnp.zeros((8, inner), F32)
        bext[0:8] = btail_in[...] if first else jnp.zeros((8, 2 * state_size), F32)
        state[...] = state_in[...] if first else jnp.zeros_like(state)

    onehot = (pos_ref[...] == iota((span, n), 1)).astype(F32).astype(BF)
    x = dot(onehot, gotx_ref[...])
    xd_ref[...] = x.astype(BF)
    r_in = lax.rsqrt(jnp.sum(x * x, axis=1, keepdims=True) * (1.0 / width) + EPSILON)
    rin_ref[...] = r_in
    h = (x * r_in * gain_ref[...]).astype(BF)
    ht_ref[...] = h.T

    @pl.when(step == 0)
    def _():
        for one in copies[:4]:
            one.wait()

    z = dot(h, wz_ref[...])
    z_ref[...] = z
    xs = dot(h, wx_ref[...])
    bc = dot(h, wbc_ref[...])
    dtr = dot(h, wdt_ref[...])
    dtr_ref[...] = dtr
    xs_ref[...] = xs.astype(BF)
    bcv_ref[...] = bc.astype(BF)

    place = base + iota((span, 1), 0)
    seg_here = seg_of(ends, place)
    xext[8 : 8 + span] = xs
    bext[8 : 8 + span] = bc
    px = bias_x + cxw_ref[taps - 1 : taps] * xs
    pbc = vb_ref[taps : taps + 1] + cbw_ref[taps - 1 : taps] * bc
    for k in range(1, taps):
        same = (seg_of(ends, place - k) == seg_here).astype(F32)
        px = px + cxw_ref[taps - 1 - k : taps - k] * (xext[8 - k : 8 - k + span] * same)
        pbc = pbc + cbw_ref[taps - 1 - k : taps - k] * (bext[8 - k : 8 - k + span] * same)
    xext[0:8] = xs[span - 8 :]
    bext[0:8] = bc[span - 8 :]
    xtail_ref[...] = xs[span - 8 :]
    btail_ref[...] = bc[span - 8 :]
    px_ref[...] = px
    pbc_ref[...] = pbc
    u = px * jax.nn.sigmoid(px)
    bcc = pbc * jax.nn.sigmoid(pbc)
    b_rows = bcc[:, :state_size].astype(BF)
    c_rows = bcc[:, state_size:].astype(BF)

    dt = softplus(dtr + vh_ref[0:1])
    cum, head_decay, tail_decay, seg_c, _ = decays(ends, base, span, dt, vh_ref[1:2])
    cum_t = cum.T
    dt_w, head_w, tail_w = widen([dt, head_decay, tail_decay], head_size, inner)
    udt = u * dt_w
    seg_r = seg_of(ends, base + iota((1, span), 1))
    counts = (seg_c == seg_r) & (iota((span, span), 0) >= iota((span, span), 1))
    never = jnp.where(counts, 0.0, NEVER)
    scores = dot_t(c_rows, b_rows)
    entering = state[...]
    state_out_ref[0] = entering
    masks = half_masks(group)
    pieces = []
    for tile in range(inner // LANES):
        lanes = slice(tile * LANES, (tile + 1) * LANES)
        block = udt[:, lanes]
        total = None
        for k in range(group):
            head = tile * group + k
            decay = jnp.exp(cum[:, head : head + 1] - cum_t[head : head + 1, :] + never)
            term = dot((decay * scores).astype(BF), (block * masks[k]).astype(BF))
            total = term if total is None else total + term
        pieces.append(total)
    y = jnp.concatenate(pieces, axis=1)
    y = y + dot(c_rows, entering.astype(BF)) * head_w
    y = y + skip * u
    y_ref[...] = y
    b_t = bcc[:, :state_size].T.astype(BF)
    state[...] = head_w[span - 1 : span] * entering + dot(b_t, (udt * tail_w).astype(BF))
    gated = y * (z * jax.nn.sigmoid(z))
    squares = jnp.sum(gated * gated, axis=1, keepdims=True)
    stat_ref[0] = jnp.broadcast_to(squares, (span, LANES)).T[0:8]
    g = (gated * ggain).astype(BF)
    g_ref[...] = g

    @pl.when(step == 0)
    def _():
        copies[4].wait()

    mix = dot(g, wout_ref[...]).astype(BF)
    cols = width // shares
    hand_out(send_ref, keep_ref, ids_ref[1], [mix[:, j * cols : (j + 1) * cols] for j in range(shares)])


def run_fwd(part, scalars, sizes, got_x, pos, vectors, weights, before, deps):
    head_size, shares = sizes
    n, width = got_x.shape
    gain, vx, vb, vh = vectors
    w_z, w_x, w_bc, w_dt, w_out = weights
    inner = w_z.shape[1]
    two = w_bc.shape[1]
    span = SPAN
    first, last = part
    steps = last - first
    blocks = n // span

    def rows(c):
        return pl.BlockSpec((span, c), lambda i, *_: (first + i, 0))

    def by_block(a, c):
        return pl.BlockSpec((1, a, c), lambda i, *_: (first + i, 0, 0))

    held = [w_z, w_x, w_bc, w_dt, w_out]
    ops = [got_x, pos, gain, vx, vb, vh]
    specs = [whole(o.shape) for o in ops]
    specs[1] = rows(1)
    ops += held
    specs += [pl.BlockSpec(memory_space=pl.ANY)] * len(held)
    cols = width // shares
    part_spec = pl.BlockSpec((shares // 2, span, cols), lambda i, *_: (0, i, 0))
    outs = [
        ((n, width), BF, rows(width)),
        ((width, n), BF, pl.BlockSpec((width, span), lambda i, *_: (0, first + i))),
        ((n, 1), F32, rows(1)),
        ((n, inner), F32, rows(inner)),
        ((n, inner), BF, rows(inner)),
        ((n, inner), F32, rows(inner)),
        ((n, inner), F32, rows(inner)),
        ((n, two), BF, rows(two)),
        ((n, two), F32, rows(two)),
        ((n, LANES), F32, rows(LANES)),
        ((n, inner), BF, rows(inner)),
        ((blocks, 8, span), F32, by_block(8, span)),
        ((blocks, two // 2, inner), F32, by_block(two // 2, inner)),
        ((shares // 2, steps * span, cols), BF, part_spec),
        ((shares // 2, steps * span, cols), BF, part_spec),
        ((8, inner), F32, whole((8, inner))),
        ((8, two), F32, whole((8, two))),
        ((two // 2, inner), F32, whole((two // 2, inner))),
    ]
    keep = []
    if before is not None:
        carry = list(before[15:18])
        ops += carry
        specs += [whole(o.shape) for o in carry]
        keep = list(enumerate(before[:13]))
    return call(
        functools.partial(fwd_kernel, sizes, first), ops, specs, outs, f"forward_{first}", grid=(steps,),
        scalars=scalars, deps=deps, keep=keep, flops=2 * steps * span * width * 5 * inner,
        scratch=[
            pltpu.VMEM((span + 8, inner), F32), pltpu.VMEM((span + 8, two), F32),
            *(pltpu.VMEM(w.shape, w.dtype) for w in held), pltpu.SemaphoreType.DMA((len(held),)),
        ],
    )


def dots_kernel(ids_ref, lengths_ref, pos_ref, dyn_ref, g_ref, stat_ref, out_ref, stat_out_ref):
    rows = pos_ref.shape[0]
    n = dyn_ref.shape[0]
    blocks, _, span = stat_ref.shape
    base = pl.program_id(0) * rows
    full = row_ends(ids_ref, lengths_ref)[-1]
    onehot = (pos_ref[...] == iota((rows, n), 1)) & (base + iota((rows, 1), 0) < full)
    dyn = dot(onehot.astype(F32).astype(BF), dyn_ref[...])
    out_ref[...] = dyn.astype(BF)
    inner_dot = jnp.sum(dyn * g_ref[...].astype(F32), axis=1, keepdims=True)
    as_row = jnp.broadcast_to(inner_dot, (rows, LANES)).T[0:8]
    for k in range(blocks):
        own = as_row[:, k * span : (k + 1) * span]
        stat_out_ref[k] = jnp.where(iota((8, span), 0) == 0, stat_ref[k], own)


def run_dots(scalars, pos, got_dyn, g, stat, deps):
    n, inner = got_dyn.shape
    span = 2 * SPAN
    rows = pl.BlockSpec((span, inner), lambda i, *_: (i, 0))
    stats = pl.BlockSpec((2, 8, SPAN), lambda i, *_: (i, 0, 0))
    return call(
        dots_kernel, [pos, got_dyn, g, stat],
        [pl.BlockSpec((span, 1), lambda i, *_: (i, 0)), whole((n, inner)), rows, stats],
        [((n, inner), BF, rows), (stat.shape, F32, stats)], "row_dots", grid=(n // span,), scalars=scalars, deps=deps,
        flops=2 * n * n * inner,
    )


def bwd_kernel(
    sizes, last, blocks, ids_ref, lengths_ref, stat_ref, dyn_ref, z_ref, xs_ref, px_ref, y_ref, bcv_ref, pbc_ref,
    dtr_ref, xd_ref, rin_ref, state_ref, gain_ref, wz_ref, wx_ref, wbc_ref, wdt_ref, vx_ref, vb_ref, vh_ref, *refs,
):
    head_size, shares = sizes
    newest = last == blocks
    if not newest:
        before, refs = refs[:8], refs[8:]
    (
        cols_ref, send_ref, keep_ref, *carry, xext, bext, extra,
    ) = refs
    xhead_ref, bhead_ref, dstate, across, accx_ref, accb_ref, acch_ref, accd_ref = carry
    span, inner = z_ref.shape
    width = xd_ref.shape[1]
    two = pbc_ref.shape[1]
    early = cols_ref.shape[1] - 2 * inner
    state_size = two // 2
    taps = vb_ref.shape[0] - 1
    group = LANES // head_size
    units = inner * shares
    step = pl.program_id(0)
    base = (last - 1 - step) * span
    ends = row_ends(ids_ref, lengths_ref)
    tensor = ids_ref[1]
    cxw_ref, cbw_ref = vx_ref, vb_ref
    skip, ggain = vx_ref[taps + 1 : taps + 2], vx_ref[taps + 2 : taps + 3]

    @pl.when(step == 0)
    def _():
        for k, ref in enumerate(carry):
            ref[...] = jnp.zeros_like(ref) if newest else before[k][...]
        extra[...] = jnp.zeros_like(extra)

    xext[span : span + 8] = xhead_ref[...]
    bext[span : span + 8] = bhead_ref[...]

    def add_row(ref, row, value):
        ref[row : row + 1] += jnp.sum(value, axis=0, keepdims=True)

    place = base + iota((span, 1), 0)
    stat_cols = stat_ref[0].T
    r_g = lax.rsqrt(stat_cols[:, 0:1] * (1.0 / units) + EPSILON)
    row_dot = stat_cols[:, 1:2] * (1.0 / units)
    z = z_ref[...]
    y = y_ref[...]
    dyn = dyn_ref[...].astype(F32)
    sig_z = jax.nn.sigmoid(z)
    silu_z = z * sig_z
    gated = y * silu_z
    normed = gated * r_g
    d_gated = r_g * (dyn * ggain) - normed * (r_g * r_g * row_dot)
    d_y = d_gated * silu_z
    dz = (d_gated * y * (sig_z * (1.0 + z * (1.0 - sig_z)))).astype(BF)
    cols_ref[:, early : early + inner] = dz
    add_row(accx_ref, taps + 2, dyn * normed)

    px = px_ref[...]
    sig_x = jax.nn.sigmoid(px)
    u = px * sig_x
    pbc = pbc_ref[...]
    sig_bc = jax.nn.sigmoid(pbc)
    bcc = pbc * sig_bc
    b_rows = bcc[:, :state_size].astype(BF)
    c_rows = bcc[:, state_size:].astype(BF)
    add_row(accx_ref, taps + 1, u * d_y)

    pre = dtr_ref[...] + vh_ref[0:1]
    dt = softplus(pre)
    rates = vh_ref[1:2]
    cum, head_decay, tail_decay, seg_c, seg_last = decays(ends, base, span, dt, rates)
    cum_t = cum.T
    dt_w, head_w, tail_w = widen([dt, head_decay, tail_decay], head_size, inner)
    udt = u * dt_w
    seg_r = seg_of(ends, base + iota((1, span), 1))
    counts = (seg_c == seg_r) & (iota((span, span), 1) >= iota((span, span), 0))
    never = jnp.where(counts, 0.0, NEVER)
    scores = dot_t(b_rows, c_rows)
    d_scores = jnp.zeros((span, span), F32)
    masks = half_masks(group)
    pieces = []
    for tile in range(inner // LANES):
        lanes = slice(tile * LANES, (tile + 1) * LANES)
        udt_block = udt[:, lanes]
        dy_block = d_y[:, lanes]
        dy_low = dy_block.astype(BF)
        total = None
        for k in range(group):
            head = tile * group + k
            decay = jnp.exp(cum_t[head : head + 1, :] - cum[:, head : head + 1] + never)
            d_scores = d_scores + decay * dot_t((udt_block * masks[k]).astype(BF), dy_low)
            term = dot((decay * scores).astype(BF), (dy_block * masks[k]).astype(BF))
            total = term if total is None else total + term
        pieces.append(total)
    in_block = jnp.concatenate(pieces, axis=1)
    d_state = dstate[...]
    d_state_low = d_state.astype(BF)
    entering = state_ref[0]
    entering_low = entering.astype(BF)
    at_end = dot(b_rows, d_state_low)
    at_start = dot(c_rows, entering_low)
    d_udt = in_block + at_end * tail_w
    from_start = (d_y * head_w).astype(BF)
    to_end = (udt * tail_w).astype(BF)
    d_c = dot(d_scores.T.astype(BF), b_rows) + dot_t(from_start, entering_low)
    d_b = dot(d_scores.astype(BF), c_rows) + dot_t(to_end, d_state_low)
    y_block = y - skip * u - at_start * head_w
    balance = d_y.astype(BF).astype(F32) * y_block - udt.astype(BF).astype(F32) * in_block
    balance = balance + from_start.astype(F32) * at_start - to_end.astype(F32) * at_end
    v_part = head_sums(u * d_udt, head_size, split2)
    mask_low = counts.astype(F32).astype(BF)
    d_la = fixed_sum(mask_low, head_sums(balance, head_size, split3))
    d_la = d_la + jnp.where(seg_c == seg_last, across[0:1], 0.0)
    d_dt = v_part + rates * d_la
    d_pre = d_dt * jax.nn.sigmoid(pre)
    add_row(acch_ref, 0, d_la * dt * rates)
    add_row(acch_ref, 1, d_pre)

    c_t = bcc[:, state_size:].T.astype(BF)
    d_enter = dot(c_t, from_start) + head_w[span - 1 : span] * d_state
    dstate[...] = d_enter
    crossing = jnp.sum(d_enter.astype(BF).astype(F32) * entering, axis=0, keepdims=True)
    across[...] = head_sums(jnp.broadcast_to(crossing, (8, inner)), head_size, split3)

    d_u = skip * d_y + dt_w * d_udt
    d_px = d_u * (sig_x * (1.0 + px * (1.0 - sig_x)))
    d_pbc = jnp.concatenate([d_b, d_c], axis=1) * (sig_bc * (1.0 + pbc * (1.0 - sig_bc)))
    xext[0:span] = d_px
    bext[0:span] = d_pbc
    seg_here = seg_of(ends, place)
    xs = xs_ref[...].astype(F32)
    bcv = bcv_ref[...].astype(F32)
    d_xs = cxw_ref[taps - 1 : taps] * d_px
    d_bc = cbw_ref[taps - 1 : taps] * d_pbc
    add_row(accx_ref, taps, d_px)
    add_row(accb_ref, taps, d_pbc)
    add_row(accx_ref, taps - 1, d_px * xs)
    add_row(accb_ref, taps - 1, d_pbc * bcv)
    for k in range(1, taps):
        later = place + k
        same = ((seg_of(ends, later) == seg_here) & (later < blocks * span)).astype(F32)
        tap = taps - 1 - k
        xk = xext[k : k + span] * same
        bk = bext[k : k + span] * same
        d_xs = d_xs + cxw_ref[tap : tap + 1] * xk
        d_bc = d_bc + cbw_ref[tap : tap + 1] * bk
        add_row(accx_ref, tap, xk * xs)
        add_row(accb_ref, tap, bk * bcv)
    xhead_ref[...] = d_px[0:8]
    bhead_ref[...] = d_pbc[0:8]
    dx_low = d_xs.astype(BF)
    dbc_low = d_bc.astype(BF)
    ddt_low = d_pre.astype(BF)
    cols_ref[:, 0:two] = dbc_low
    cols_ref[:, two : two + LANES] = ddt_low
    cols_ref[:, early + inner : early + 2 * inner] = dx_low
    for at in range(two + LANES, early, LANES):
        cols_ref[:, at : at + LANES] = jnp.zeros((span, LANES), BF)
    back = dot_t(dz, wz_ref[...]) + dot_t(dx_low, wx_ref[...])
    back = back + dot_t(ddt_low, wdt_ref[...]) + dot_t(dbc_low, wbc_ref[...])
    x_hat = xd_ref[...].astype(F32) * rin_ref[...]
    shared = back * x_hat
    add_row(accd_ref, 0, shared)
    inner_dot = jnp.sum(shared * gain_ref[...], axis=1, keepdims=True)
    low = back.astype(BF)
    cols = width // shares
    row = jnp.broadcast_to(inner_dot, (span, LANES)).T[0:1]
    for k in range(span // LANES):
        extra[k : k + 1] = row[:, k * LANES : (k + 1) * LANES]
    hand_out(send_ref, keep_ref, tensor, [low[:, j * cols : (j + 1) * cols] for j in range(shares)])
    more = extra[...].astype(BF)
    for part in range(shares // 2):
        send_ref[part, span : span + EXTRA, 0:LANES] = more
        keep_ref[part, span : span + EXTRA, 0:LANES] = more


def run_bwd(part, scalars, sizes, stat, dyn, kept, vectors, weights, before, deps):
    head_size, shares = sizes
    z, xs, px, y, bcv, pbc, dtr, xd, rin, states = kept
    w_z, w_x, w_bc, w_dt = weights
    n, inner = z.shape
    width = xd.shape[1]
    two = pbc.shape[1]
    span = SPAN
    first, last = part
    steps = last - first
    blocks = n // span
    cols = width // shares

    def rows(c):
        return pl.BlockSpec((span, c), lambda i, *_: (last - 1 - i, 0))

    def by_block(a, c):
        return pl.BlockSpec((1, a, c), lambda i, *_: (last - 1 - i, 0, 0))

    ops = [stat, dyn, z, xs, px, y, bcv, pbc, dtr, xd, rin, states]
    specs = [by_block(8, span), *(rows(o.shape[1]) for o in ops[1:11]), by_block(two // 2, inner)]
    fixed = [vectors[0], w_z, w_x, w_bc, w_dt, *vectors[1:]]
    part_spec = pl.BlockSpec((shares // 2, span + EXTRA, cols), lambda i, *_: (0, steps - 1 - i, 0))
    wide = -(-(2 * inner + two + LANES) // (2 * LANES)) * (2 * LANES)
    sums = [(8, inner), (8, two), (two // 2, inner), (8, LANES), (8, inner), (8, two), (8, LANES), (8, width)]
    outs = [
        ((n, wide), BF, rows(wide)),
        ((shares // 2, steps * (span + EXTRA), cols), BF, part_spec),
        ((shares // 2, steps * (span + EXTRA), cols), BF, part_spec),
        *((c, F32, whole(c)) for c in sums),
    ]
    keep = []
    if before is not None:
        fixed += before[3:]
        keep = list(enumerate(before[:1]))
    return call(
        functools.partial(bwd_kernel, sizes, last, blocks), ops + fixed, specs + [whole(o.shape) for o in fixed], outs,
        f"backward_{first}", grid=(steps,), scalars=scalars, deps=deps, keep=keep,
        flops=2 * steps * span * width * 6 * inner,
        scratch=[pltpu.VMEM((span + 8, inner), F32), pltpu.VMEM((span + 8, two), F32), pltpu.VMEM((EXTRA, LANES), F32)],
    )


def outer_kernel(groups, ids_ref, left_ref, right_ref, send_ref, keep_ref):
    each = groups // pl.num_programs(0)
    rows = left_ref.shape[0] // each
    low = dot(left_ref[...], right_ref[...]).astype(BF)
    at = pl.program_id(0) * each
    for i in range(each):
        place = ids_ref[0] ^ (at + i)

        @pl.when(place % 2 == 1)
        def _(i=i, place=place):
            send_ref[place // 2] = low[i * rows : (i + 1) * rows]

        @pl.when(place % 2 == 0)
        def _(i=i, place=place):
            keep_ref[place // 2] = low[i * rows : (i + 1) * rows]


def outer(ids, groups, left_t, right, first, count, deps=()):
    width, n = left_t.shape
    steps = 4
    rows = width // groups
    out = ((groups // 2, rows, count), BF, whole((groups // 2, rows, count)))
    return call(
        functools.partial(outer_kernel, groups), [left_t, right],
        [pl.BlockSpec((width // steps, n), lambda i, *_: (i, 0)), pl.BlockSpec((n, count), lambda *_: (0, first // count))],
        [out, out], "outer",
        grid=(steps,), scalars=[ids], deps=deps, flops=2 * n * width * count,
    )


def put_yn_kernel(units, ids_ref, lengths_ref, pos_ref, stat_ref, data_ref, out_ref, hot_ref, scale_ref):
    n = pos_ref.shape[1]
    blocks, _, span = stat_ref.shape

    @pl.when(pl.program_id(0) == 0)
    def _():
        hot_ref[...] = (pos_ref[...] == iota((n, n), 0)).astype(F32).astype(BF)
        full = row_ends(ids_ref, lengths_ref)[-1]
        for k in range(blocks):
            squares = stat_ref[k].T[:, 0:1]
            valid = k * span + iota((span, 1), 0) < full
            scale = lax.rsqrt(squares * (1.0 / units) + EPSILON)
            scale_ref[k * span : (k + 1) * span] = jnp.where(valid, scale, 0.0)

    yn = (data_ref[...].astype(F32) * scale_ref[...]).astype(BF)
    out_ref[...] = dot(hot_ref[...], yn).astype(BF)


def put_yn(scalars, units, pos, stat, g, deps):
    n, width = g.shape
    tile = next((t for t in (384, 256) if width % t == 0), width)
    spec = pl.BlockSpec((n, tile), lambda i, *_: (0, i))
    return call(
        functools.partial(put_yn_kernel, units), [pos, stat, g], [whole(pos.shape), whole(stat.shape), spec],
        [((n, width), BF, spec)], "put_yn", grid=(width // tile,), scalars=scalars, deps=deps,
        scratch=[pltpu.VMEM((n, n), BF), pltpu.VMEM((n, 1), F32)], flops=2 * n * n * width,
    )[0]


def add_up(refs, counts):
    pieces, at = [], 0
    for count in counts:
        total = refs[at][0].astype(F32)
        for ref in refs[at + 1 : at + count]:
            total = total + ref[0].astype(F32)
        pieces.append(total)
        at += count
    return jnp.concatenate(pieces, axis=0)


def send_out_kernel(units, counts, ids_ref, lengths_ref, pos_ref, stat_ref, x_ref, *refs):
    *terms, out_ref, sq_ref = refs
    n = pos_ref.shape[1]
    blocks, _, span = stat_ref.shape
    mix = add_up(terms, counts)
    squares = jnp.concatenate([stat_ref[k].T[:, 0:1] for k in range(blocks)], axis=0)
    valid = (iota((n, 1), 0) < row_ends(ids_ref, lengths_ref)[-1]).astype(F32)
    mix = mix * (lax.rsqrt(squares * (1.0 / units) + EPSILON) * valid)
    x = x_ref[...].astype(F32)
    out = (x + mix).astype(BF)
    full = out.astype(F32)
    onehot = (pos_ref[...] == iota((n, n), 0)).astype(F32).astype(BF)
    out_ref[...] = dot(onehot, out).astype(BF)
    sq_ref[...] = jnp.zeros_like(sq_ref)
    for k, v in enumerate((x * x * valid, mix * mix, full * full * valid)):
        sq_ref[k : k + 1] = jnp.sum(v, axis=0, keepdims=True)


def send_dx_kernel(width, span, counts, pos_ref, x_ref, rin_ref, gain_ref, *refs):
    *terms, out_ref = refs
    n = pos_ref.shape[1]
    total = add_up(terms, counts)
    each = span + EXTRA
    d_h, dots = [], []
    for k in range(n // span):
        d_h.append(total[k * each : k * each + span])
        rows = total[k * each + span : k * each + span + 8, 0:LANES].T
        dots += [rows[:, i : i + 1] for i in range(span // LANES)]
    d_h, dots = jnp.concatenate(d_h, axis=0), jnp.concatenate(dots, axis=0)
    r_in = rin_ref[...]
    x_hat = x_ref[...].astype(F32) * r_in
    dx = (r_in * (d_h * gain_ref[...] - x_hat * (dots * (1.0 / width)))).astype(BF)
    onehot = (pos_ref[...] == iota((n, n), 0)).astype(F32).astype(BF)
    out_ref[...] = dot(onehot, dx).astype(BF)


def term_ops(groups_of_terms):
    ops = [t for terms in groups_of_terms for t in terms]
    specs = [pl.BlockSpec((1,) + o.shape[1:], lambda *_: (0, 0, 0)) for o in ops]
    return ops, specs, [len(terms) for terms in groups_of_terms]


def swap(v, axis, bit):
    size = lax.axis_size(axis)
    return lax.ppermute(v, axis, [(i, i ^ (1 << bit)) for i in range(size)])


def bits_of(axis):
    return lax.axis_size(axis).bit_length() - 1


class Halving:
    def __init__(self, send, keep, axis, order):
        self.axis, self.order = axis, order
        self.left = list(range(len(order) - 1, 0, -1))
        shape = (2,) * len(self.left) + keep.shape[1:]
        self.terms = [keep.reshape(shape)]
        self.sent = send.reshape(shape)
        self.got = None
        self.flat = [keep]
        self.at = 0

    def launch(self):
        if self.sent is not None:
            self.got = swap(self.sent, self.axis, self.order[self.at])
            self.sent = None
        return self

    def take(self):
        got, self.got = self.got, None
        self.terms.append(got)
        self.flat.append(got.reshape((-1,) + got.shape[len(self.left) :]))
        self.at += 1
        return self

    def advance(self):
        if self.left:
            dim = self.left.index(self.order[self.at])
            self.left.pop(dim)
            odd = [lax.index_in_dim(t, 1, dim, keepdims=False).astype(F32) for t in self.terms]
            self.sent = sum(odd[1:], odd[0]).astype(BF)
            self.terms = [lax.index_in_dim(t, 0, dim, keepdims=False) for t in self.terms]
        return self

    def land(self):
        return self if self.got is None else self.take().advance()

    def split(self, at, order):
        other = copy.copy(self)
        other.left, other.order = list(self.left), order
        other.terms = [t[..., at:] for t in self.terms]
        self.terms = [t[..., :at] for t in self.terms]
        return other

    def finish(self):
        while self.sent is not None or self.got is not None:
            self.launch().land()
        return self

    def total(self):
        self.finish()
        wide = [t.astype(F32) for t in self.terms]
        return sum(wide[1:], wide[0])


def fence(halvings, *values):
    held = [(h.sent, h.got) for h in halvings]
    flat, tree = jax.tree.flatten((held, values))
    held, values = tree.unflatten(lax.optimization_barrier(flat))
    for h, (sent, got) in zip(halvings, held, strict=True):
        h.sent, h.got = sent, got
    return values


def exchange(v, axis):
    groups = lax.axis_size(axis)
    rows = v.shape[0]
    parts = v.reshape((groups, rows // groups) + v.shape[1:])
    return lax.all_to_all(parts, axis, split_axis=0, concat_axis=0, tiled=True).reshape(v.shape)


def sum_at_once(v, axis):
    size = lax.axis_size(axis)
    others = [lax.ppermute(v, axis, [(i, i ^ k) for i in range(size)]) for k in range(1, size)]
    return sum((o.astype(F32) for o in others), v.astype(F32))


def pad_lanes(v):
    return jnp.pad(v, [(0, 0)] * (v.ndim - 1) + [(0, LANES - v.shape[-1])])


def local(
    stream, out_grad, seq_lengths, anchor, norm_gain, w_z, w_x, w_bc, w_dt, conv_x_w, conv_x_b, conv_bc_w,
    conv_bc_b, dt_bias, a_log, d_skip, gated_gain, w_out,
):
    groups = lax.axis_size("dp")
    shares = lax.axis_size("tensor")
    me = lax.axis_index("dp")
    tensor = lax.axis_index("tensor")
    n, width = stream.shape
    per = n // groups
    cols = width // shares
    first_col = tensor * cols
    inner = w_z.shape[1]
    heads = w_dt.shape[1]
    head_size = inner // heads
    two = w_bc.shape[1]
    taps = conv_x_w.shape[0]
    sizes = (head_size, shares)
    units = inner * shares
    ids = jnp.stack([me, tensor]).astype(I32)
    scalars = [ids, seq_lengths]
    tensor_order = list(range(bits_of("tensor")))
    dp_bits = bits_of("dp")
    order_a = list(range(dp_bits))
    order_b = order_a[:1] + order_a[1:][::-1]

    pos_row, pos_col, requests = find_places(anchor, n, per)
    wanted = lax.all_to_all(
        requests.reshape(groups, per), "dp", split_axis=0, concat_axis=0, tiled=True
    ).reshape(1, n)
    rows = stream.at[wanted.reshape(n)].get(mode="promise_in_bounds", unique_indices=True)
    got_x = exchange(rows, "dp")
    gain = norm_gain[None]
    vx = jnp.concatenate([conv_x_w, conv_x_b[None], jnp.repeat(d_skip, head_size)[None], gated_gain[None]])
    vb = jnp.concatenate([conv_bc_w, conv_bc_b[None]])
    vh = pad_lanes(jnp.stack([dt_bias, -jnp.exp(a_log)]))
    w_dt_pad = pad_lanes(w_dt)
    dy_t = out_grad.T
    gain_cols = lax.dynamic_slice_in_dim(norm_gain, first_col, cols, 0)[None]
    dy_cols = lax.dynamic_slice_in_dim(out_grad, first_col, cols, 1)
    d_yn_src = jnp.einsum("td,id->ti", out_grad, w_out, preferred_element_type=F32).astype(BF)
    dyn_send = move_rows(
        pick_kernel, wanted, d_yn_src, name="pick_dyn", deps=[gain, vx, vb, vh, w_dt_pad, dy_t, gain_cols, dy_cols]
    )
    got_dyn = exchange(dyn_send, "dp")

    vectors = (gain, vx, vb, vh)
    first, second = FORWARD
    weights = (w_z, w_x, w_bc, w_dt_pad)
    got = run_fwd(first, scalars, sizes, got_x, pos_col, vectors, (*weights, w_out), None, [dyn_send])
    mix_1 = Halving(got[13], got[14], "tensor", tensor_order).launch()
    got = run_fwd(second, scalars, sizes, got_x, pos_col, vectors, (*weights, w_out), got, [])
    mix_2 = Halving(got[13], got[14], "tensor", tensor_order)
    (xd, h_t, rin, z, xs, px, y, bcv, pbc, dtr, g, stat, states) = got[:13]
    (stat,) = fence([mix_1], stat)
    dyn, stat = run_dots(scalars, pos_col, got_dyn, g, stat, [])
    (stat,) = fence([mix_1], stat)
    mix_1.land()
    stat = sum_at_once(stat, "tensor")
    (stat,) = fence([mix_1, mix_2], stat)

    kept = (z, xs, px, y, bcv, pbc, dtr, xd, rin, states)
    yn_send = put_yn(scalars, units, pos_row, stat, g, [])
    yn_back = exchange(yn_send, "dp")
    mix_1.launch()
    mix_2.launch()
    got = run_bwd(BACKWARD[0], scalars, sizes, stat, dyn, kept, vectors, weights, None, [yn_send])
    back_1 = Halving(got[1], got[2], "tensor", tensor_order)
    yn_back, carry = fence([mix_1, mix_2, back_1], yn_back, got[3:])
    got = [*got[:3], *carry]
    mix_1.land()
    mix_2.land()
    back_1.launch()
    mix_1.launch()
    mix_2.launch()
    yn_src = move_rows(put_kernel, wanted, yn_back, name="place_yn")
    h_out = Halving(*outer(ids, groups, dy_t, yn_src, 0, inner), "dp", order_b)
    got = run_bwd(BACKWARD[1], scalars, sizes, stat, dyn, kept, vectors, weights, got, [h_out.sent])
    h_out.launch().land()
    back_2 = Halving(got[1], got[2], "tensor", tensor_order)
    grad_cols, tail = got[0], got[7:]
    grad_cols, tail, xd = fence([mix_1, mix_2, back_1, back_2, h_out], grad_cols, tail, xd)
    acc_x, acc_b, acc_h, acc_d = tail

    mix_1.land().finish()
    mix_2.land().finish()
    back_1.land()
    back_2.launch()
    back_1.launch()
    h_out.launch()
    half = grad_cols.shape[1] // 2
    x_cols = lax.dynamic_slice_in_dim(xd, first_col, cols, 1)
    h_a = Halving(*outer(ids, groups, h_t, grad_cols, 0, 2 * half), "dp", order_a)
    (x_cols,) = fence([back_1, back_2, h_out, h_a], x_cols)

    back_2.land().launch()
    back_1.land().finish()
    h_a.launch()
    ops, specs, counts = term_ops([mix_1.flat, mix_2.flat])
    ops = [pos_row, stat, x_cols, *ops]
    out_send, squares = call(
        functools.partial(send_out_kernel, units, counts), ops, [*(whole(o.shape) for o in ops[:3]), *specs],
        [((n, cols), BF, whole((n, cols))), ((8, cols), F32, whole((8, cols)))], "send_out", scalars=scalars,
        flops=2 * n * n * cols,
    )
    flat = [acc_x, acc_h, acc_b[: taps + 1], acc_d[0], jnp.sum(squares, axis=1)]
    flat = [f.reshape(-1) for f in flat]
    lens = [f.shape[0] for f in flat]
    small = jnp.concatenate(flat).astype(BF)
    small = jnp.pad(small, (0, -sum(lens) % (16 * cols))).reshape(1, -1, cols)
    small = jnp.broadcast_to(small, (groups,) + small.shape[1:])
    sent = jnp.concatenate([out_send.reshape(groups, per, cols), small], axis=1)
    out_back = lax.all_to_all(sent, "dp", split_axis=0, concat_axis=0, tiled=True)
    (x_cols,) = fence([back_2, h_a], x_cols)

    back_2.land().finish()
    h_a.take()
    h_b = h_a.split(half, order_b)
    h_a.advance().launch()
    h_b.advance().launch()
    h_out.land().launch()
    back_ops, back_specs, back_counts = term_ops([back_2.flat, back_1.flat])
    ops = [pos_row, x_cols, rin, gain_cols]
    dx_send = call(
        functools.partial(send_dx_kernel, width, SPAN, back_counts), [*ops, *back_ops],
        [*(whole(o.shape) for o in ops), *back_specs],
        [((n, cols), BF, whole((n, cols)))], "send_dx", flops=2 * n * n * cols,
    )[0]
    dx_send, out_back = fence([], dx_send, out_back)

    dx_back = exchange(dx_send, "dp")
    out_rows = out_back[:, :per].reshape(n, cols)
    out_final = move_rows(put_kernel, wanted, out_rows, name="place_out")
    small = jnp.sum(out_back[:, per:].astype(F32), axis=0).reshape(-1)
    out_final, small, dy_cols = fence([h_a, h_b, h_out], out_final, small, dy_cols)

    h_a.land().launch()
    h_b.land().launch()
    h_out.land()
    dx_final = move_rows(put_add_kernel, wanted, dx_back, dy_cols, name="place_dx")
    (dx_final,) = fence([h_a, h_b], dx_final)

    g_out = h_out.total()
    g_a = h_a.total()
    g_b = h_b.total()
    early = 2 * half - 2 * inner
    g_dt = g_a[:, two : two + heads]
    g_z = jnp.concatenate([g_a[:, early:], g_b[:, : early + inner - half]], axis=1)
    g_x = g_b[:, early + inner - half :]

    own = lens[0] + lens[1]
    s_x = small[: lens[0]].reshape(acc_x.shape)
    s_h = small[lens[0] : own].reshape(acc_h.shape)
    both = small[own : sum(lens)]
    both = jnp.pad(both, (0, -both.shape[0] % (8 * two))).reshape(-1, two)
    both = sum_at_once(jnp.concatenate([g_a[:, :two], both]).astype(BF), "tensor")
    g_bc = both[: g_a.shape[0]]
    both = both[g_a.shape[0] :].reshape(-1)
    s_b = both[: lens[2]].reshape(taps + 1, two)
    s_d = both[lens[2] : lens[2] + lens[3]]
    s_sq = both[lens[2] + lens[3] : lens[2] + lens[3] + 3]
    g_gain = lax.dynamic_slice_in_dim(s_d, first_col, cols, 0)
    rms = jnp.sqrt(s_sq / (jnp.sum(seq_lengths).astype(F32) * width))
    g_skip = jnp.sum(s_x[taps + 1].reshape(heads, head_size), axis=1)
    return (
        out_final, dx_final, g_gain, g_z, g_x, g_bc, g_dt, s_x[:taps], s_x[taps], s_b[:taps], s_b[taps],
        s_h[1, :heads], s_h[0, :heads], g_skip, s_x[taps + 2], g_out.T, rms,
    )


def solution(mesh):
    in_specs = (
        P("dp", None), P("dp", None), P(), P("dp"), P(), P(None, "tensor"), P(None, "tensor"), P(),
        P(None, "tensor"), P(None, "tensor"), P("tensor"), P(), P(), P("tensor"), P("tensor"), P("tensor"),
        P("tensor"), P("tensor", None),
    )
    out_specs = (
        P("dp", "tensor"), P("dp", "tensor"), P("tensor"), P("dp", "tensor"), P("dp", "tensor"), P("dp", None),
        P("dp", "tensor"), P(None, "tensor"), P("tensor"), P(), P(), P("tensor"), P("tensor"), P("tensor"),
        P("tensor"), P("tensor", "dp"), P(),
    )
    return jax.shard_map(local, mesh=mesh, in_specs=in_specs, out_specs=out_specs, check_vma=False)
```

```python
import copy
import functools

import jax
import jax.numpy as jnp
from jax import lax
from jax.experimental import pallas as pl
from jax.experimental.pallas import tpu as pltpu
from jax.sharding import PartitionSpec as P

SPAN = 256
EPSILON = 1e-05
LANES = 128
NEVER = -1e30
BF = jnp.bfloat16
F32 = jnp.float32
I32 = jnp.int32
MIB = 1 << 20
EXTRA = 16
FORWARD = ((0, 2), (2, 4))
BACKWARD = ((2, 4), (0, 2))


def dot(a, b):
    return jnp.dot(a, b, preferred_element_type=F32)


def dot_t(a, b):
    return lax.dot_general(a, b, (((1,), (1,)), ((), ())), preferred_element_type=F32)


def iota(shape, dim):
    return lax.broadcasted_iota(I32, shape, dim)


def split2(v):
    hi = v.astype(BF)
    return hi, (v - hi.astype(F32)).astype(BF)


def split3(v):
    hi = v.astype(BF)
    rest = v - hi.astype(F32)
    mid = rest.astype(BF)
    return hi, mid, (rest - mid.astype(F32)).astype(BF)


def params(mib=56, **more):
    return pltpu.CompilerParams(vmem_limit_bytes=mib * MIB, **more)


def whole(shape):
    rank = len(shape)
    return pl.BlockSpec(shape, lambda *_: (0,) * rank)


def call(kernel, ins, in_specs, outs, name, grid=(1,), scalars=(), deps=(), scratch=(), flops=0, keep=(), mib=56):
    n_scalars, n_in, n_extra = len(scalars), len(ins), len(keep) + len(deps)

    def body(*refs):
        kernel(*refs[: n_scalars + n_in], *refs[n_scalars + n_in + n_extra :])

    extra = [a for _, a in keep] + list(deps)
    first = n_scalars + n_in
    moved = sum(a.size * a.dtype.itemsize for a in ins) + sum(
        functools.reduce(lambda p, q: p * q, o[0]) * 2 for o in outs
    )
    return pl.pallas_call(
        body,
        grid_spec=pltpu.PrefetchScalarGridSpec(
            num_scalar_prefetch=n_scalars,
            grid=grid,
            in_specs=[*in_specs, *(pl.BlockSpec(memory_space=pl.ANY) for _ in extra)],
            out_specs=[o[2] for o in outs],
            scratch_shapes=list(scratch),
        ),
        out_shape=[jax.ShapeDtypeStruct(o[0], o[1]) for o in outs],
        input_output_aliases={first + k: at for k, (at, _) in enumerate(keep)},
        compiler_params=params(mib),
        cost_estimate=pl.CostEstimate(flops=flops, bytes_accessed=moved, transcendentals=0),
        name=name,
    )(*scalars, *ins, *extra)


def index_kernel(per, src_ref, pos_row_ref, pos_col_ref, req_ref):
    n = src_ref.shape[1]
    rows = src_ref[...]
    cols = rows.T
    src_row, loc_row = rows[0:1], rows[1:2]
    src_col = cols[:, 0:1]
    member = (src_col == iota((n, LANES), 1).astype(F32)).astype(F32)
    member_t = (src_row == iota((LANES, n), 0).astype(F32)).astype(F32)
    before = (iota((n, n), 1) < iota((n, n), 0)).astype(F32).astype(BF)
    before_t = (iota((n, n), 0) < iota((n, n), 1)).astype(F32).astype(BF)
    rank = jnp.sum(dot(before, member.astype(BF)) * member, axis=1, keepdims=True)
    rank_t = jnp.sum(dot(member_t.astype(BF), before_t) * member_t, axis=0, keepdims=True)
    place = (src_col * per + rank).astype(I32)
    pos_col_ref[...] = place
    pos_row_ref[...] = (src_row * per + rank_t).astype(I32)
    onehot = (place == iota((n, n), 1)).astype(F32).astype(BF)
    high = jnp.floor(loc_row * (1.0 / 32.0))
    low = loc_row - high * 32.0
    pair = jnp.where(iota((8, n), 0) == 0, high, low).astype(BF)
    found = dot(pair, onehot)
    req_ref[...] = (found[0:1] * 32.0 + found[1:2]).astype(I32)


def find_places(anchor, n, per):
    src = (anchor // n).astype(F32)
    loc = (anchor % n).astype(F32)
    rows = jnp.concatenate([src[None], loc[None], jnp.zeros((6, n), F32)])
    return pl.pallas_call(
        functools.partial(index_kernel, per),
        out_shape=(
            jax.ShapeDtypeStruct((1, n), I32),
            jax.ShapeDtypeStruct((n, 1), I32),
            jax.ShapeDtypeStruct((1, n), I32),
        ),
        compiler_params=params(),
        name="places",
    )(rows)


def pick_kernel(idx_ref, data_ref, out_ref, hot_ref):
    n = idx_ref.shape[1]

    @pl.when(pl.program_id(0) == 0)
    def _():
        col = jnp.broadcast_to(idx_ref[...].astype(F32), (8, n)).T[:, 0:1].astype(I32)
        hot_ref[...] = (col == iota((n, n), 1)).astype(F32).astype(BF)

    out_ref[...] = dot(hot_ref[...], data_ref[...]).astype(BF)


def put_kernel(idx_ref, data_ref, out_ref, hot_ref):
    n = idx_ref.shape[1]

    @pl.when(pl.program_id(0) == 0)
    def _():
        hot_ref[...] = (idx_ref[...] == iota((n, n), 0)).astype(F32).astype(BF)

    out_ref[...] = dot(hot_ref[...], data_ref[...]).astype(BF)


def put_add_kernel(idx_ref, data_ref, base_ref, out_ref, hot_ref):
    n = idx_ref.shape[1]

    @pl.when(pl.program_id(0) == 0)
    def _():
        hot_ref[...] = (idx_ref[...] == iota((n, n), 0)).astype(F32).astype(BF)

    out_ref[...] = (base_ref[...].astype(F32) + dot(hot_ref[...], data_ref[...])).astype(BF)


def move_rows(kernel, idx, *data, name, deps=()):
    n, width = data[0].shape
    tile = next((t for t in (768, 384, 256) if width % t == 0), width)
    spec = pl.BlockSpec((n, tile), lambda i, *_: (0, i))
    return call(
        kernel,
        [idx, *data],
        [whole((1, n))] + [spec] * len(data),
        [((n, width), BF, spec)],
        name,
        grid=(width // tile,),
        deps=deps,
        scratch=[pltpu.VMEM((n, n), BF)],
        flops=2 * n * n * width,
    )[0]


def row_ends(ids_ref, lengths_ref):
    me = ids_ref[0]
    ends = [lengths_ref[me, 0]]
    for k in range(1, lengths_ref.shape[1]):
        ends.append(ends[-1] + lengths_ref[me, k])
    return ends


def seg_of(ends, place):
    seg = jnp.zeros(place.shape, I32)
    for end in ends:
        seg = seg + (place >= end).astype(I32)
    return jnp.where(place < 0, -1, seg)


def seg_scalar(ends, place):
    seg = jnp.int32(0)
    for end in ends:
        seg = seg + (place >= end).astype(I32)
    return jnp.where(place < 0, jnp.int32(-1), seg)


def softplus(v):
    e = jnp.exp(-jnp.abs(v))
    w = 1.0 + e
    one = w == 1.0
    log1p = jnp.where(one, e, jnp.log(w) * (e / jnp.where(one, 1.0, w - 1.0)))
    return jnp.maximum(v, 0.0) + log1p


def widen(parts, head_size, width):
    rows = parts[0].shape[0]
    spread = (iota((2 * LANES, width), 0) % LANES == iota((2 * LANES, width), 1) // head_size)
    spread = spread.astype(F32).astype(BF)
    stacked = jnp.concatenate([jnp.concatenate(split2(p), axis=1) for p in parts], axis=0)
    out = dot(stacked, spread)
    return [out[k * rows : (k + 1) * rows] for k in range(len(parts))]


def head_sums(v, head_size, split):
    rows, width = v.shape
    gather = (iota((width, LANES), 0) // head_size == iota((width, LANES), 1)).astype(F32).astype(BF)
    pieces = split(v)
    out = dot(jnp.concatenate(pieces, axis=0), gather)
    return sum(out[k * rows : (k + 1) * rows] for k in range(len(pieces)))


def fixed_sum(mask, v):
    out = dot(mask, jnp.concatenate(split3(v), axis=1))
    w = v.shape[1]
    return out[:, :w] + out[:, w : 2 * w] + out[:, 2 * w :]


def decays(ends, base, span, dt, rates):
    place = base + iota((span, 1), 0)
    seg_c = seg_of(ends, place)
    low = (iota((span, span), 0) >= iota((span, span), 1)).astype(F32).astype(BF)
    cum = fixed_sum(low, dt * rates)
    last = cum[span - 1 : span]
    seg_before = seg_scalar(ends, base - 1)
    seg_last = seg_scalar(ends, base + span - 1)
    head_decay = jnp.where(seg_c == seg_before, jnp.exp(cum), 0.0)
    tail_decay = jnp.where(seg_c == seg_last, jnp.exp(last - cum), 0.0)
    return cum, head_decay, tail_decay, seg_c, seg_last


def half_masks(group):
    lane = iota((1, LANES), 1)
    return [(lane // (LANES // group) == k).astype(F32) for k in range(group)]


def hand_out(send_ref, keep_ref, me, pieces):
    for j, piece in enumerate(pieces):
        place = me ^ j

        @pl.when(place % 2 == 1)
        def _(piece=piece, place=place):
            send_ref[place // 2, 0 : piece.shape[0]] = piece

        @pl.when(place % 2 == 0)
        def _(piece=piece, place=place):
            keep_ref[place // 2, 0 : piece.shape[0]] = piece


def fwd_kernel(
    sizes, first, ids_ref, lengths_ref, gotx_ref, pos_ref, gain_ref, vx_ref, vb_ref, vh_ref,
    wz_src, wx_src, wbc_src, wdt_src, wout_src, *refs,
):
    head_size, shares = sizes
    if first:
        xtail_in, btail_in, state_in, *refs = refs
    (
        xd_ref, ht_ref, rin_ref, z_ref, xs_ref, px_ref, y_ref, bcv_ref, pbc_ref, dtr_ref, g_ref, stat_ref,
        state_out_ref, send_ref, keep_ref, xtail_ref, btail_ref, state,
        xext, bext, wz_ref, wx_ref, wbc_ref, wdt_ref, wout_ref, sems,
    ) = refs
    sources = (wz_src, wx_src, wbc_src, wdt_src, wout_src)
    held = (wz_ref, wx_ref, wbc_ref, wdt_ref, wout_ref)
    copies = [pltpu.make_async_copy(a, b, sems.at[k]) for k, (a, b) in enumerate(zip(sources, held, strict=True))]
    span = pos_ref.shape[0]
    n = gotx_ref.shape[0]
    inner = wz_src.shape[1]
    width = gotx_ref.shape[1]
    state_size = wbc_src.shape[1] // 2
    taps = vb_ref.shape[0] - 1
    group = LANES // head_size
    step = pl.program_id(0)
    base = (first + step) * span
    ends = row_ends(ids_ref, lengths_ref)
    cxw_ref, cbw_ref = vx_ref, vb_ref
    bias_x, skip, ggain = (vx_ref[taps + k : taps + k + 1] for k in range(3))

    @pl.when(step == 0)
    def _():
        for one in copies:
            one.start()
        xext[0:8] = xtail_in[...] if first else jnp.zeros((8, inner), F32)
        bext[0:8] = btail_in[...] if first else jnp.zeros((8, 2 * state_size), F32)
        state[...] = state_in[...] if first else jnp.zeros_like(state)

    onehot = (pos_ref[...] == iota((span, n), 1)).astype(F32).astype(BF)
    x = dot(onehot, gotx_ref[...])
    xd_ref[...] = x.astype(BF)
    r_in = lax.rsqrt(jnp.sum(x * x, axis=1, keepdims=True) * (1.0 / width) + EPSILON)
    rin_ref[...] = r_in
    h = (x * r_in * gain_ref[...]).astype(BF)
    ht_ref[...] = h.T

    @pl.when(step == 0)
    def _():
        for one in copies[:4]:
            one.wait()

    z = dot(h, wz_ref[...])
    z_ref[...] = z
    xs = dot(h, wx_ref[...])
    bc = dot(h, wbc_ref[...])
    dtr = dot(h, wdt_ref[...])
    dtr_ref[...] = dtr
    xs_ref[...] = xs.astype(BF)
    bcv_ref[...] = bc.astype(BF)

    place = base + iota((span, 1), 0)
    seg_here = seg_of(ends, place)
    xext[8 : 8 + span] = xs
    bext[8 : 8 + span] = bc
    px = bias_x + cxw_ref[taps - 1 : taps] * xs
    pbc = vb_ref[taps : taps + 1] + cbw_ref[taps - 1 : taps] * bc
    for k in range(1, taps):
        same = (seg_of(ends, place - k) == seg_here).astype(F32)
        px = px + cxw_ref[taps - 1 - k : taps - k] * (xext[8 - k : 8 - k + span] * same)
        pbc = pbc + cbw_ref[taps - 1 - k : taps - k] * (bext[8 - k : 8 - k + span] * same)
    xext[0:8] = xs[span - 8 :]
    bext[0:8] = bc[span - 8 :]
    xtail_ref[...] = xs[span - 8 :]
    btail_ref[...] = bc[span - 8 :]
    px_ref[...] = px
    pbc_ref[...] = pbc
    u = px * jax.nn.sigmoid(px)
    bcc = pbc * jax.nn.sigmoid(pbc)
    b_rows = bcc[:, :state_size].astype(BF)
    c_rows = bcc[:, state_size:].astype(BF)

    dt = softplus(dtr + vh_ref[0:1])
    cum, head_decay, tail_decay, seg_c, _ = decays(ends, base, span, dt, vh_ref[1:2])
    cum_t = cum.T
    dt_w, head_w, tail_w = widen([dt, head_decay, tail_decay], head_size, inner)
    udt = u * dt_w
    seg_r = seg_of(ends, base + iota((1, span), 1))
    counts = (seg_c == seg_r) & (iota((span, span), 0) >= iota((span, span), 1))
    never = jnp.where(counts, 0.0, NEVER)
    scores = dot_t(c_rows, b_rows)
    entering = state[...]
    state_out_ref[0] = entering
    masks = half_masks(group)
    pieces = []
    for tile in range(inner // LANES):
        lanes = slice(tile * LANES, (tile + 1) * LANES)
        block = udt[:, lanes]
        total = None
        for k in range(group):
            head = tile * group + k
            decay = jnp.exp(cum[:, head : head + 1] - cum_t[head : head + 1, :] + never)
            term = dot((decay * scores).astype(BF), (block * masks[k]).astype(BF))
            total = term if total is None else total + term
        pieces.append(total)
    y = jnp.concatenate(pieces, axis=1)
    y = y + dot(c_rows, entering.astype(BF)) * head_w
    y = y + skip * u
    y_ref[...] = y
    b_t = bcc[:, :state_size].T.astype(BF)
    state[...] = head_w[span - 1 : span] * entering + dot(b_t, (udt * tail_w).astype(BF))
    gated = y * (z * jax.nn.sigmoid(z))
    squares = jnp.sum(gated * gated, axis=1, keepdims=True)
    stat_ref[0] = jnp.broadcast_to(squares, (span, LANES)).T[0:8]
    g = (gated * ggain).astype(BF)
    g_ref[...] = g

    @pl.when(step == 0)
    def _():
        copies[4].wait()

    mix = dot(g, wout_ref[...]).astype(BF)
    cols = width // shares
    hand_out(send_ref, keep_ref, ids_ref[1], [mix[:, j * cols : (j + 1) * cols] for j in range(shares)])


def run_fwd(part, scalars, sizes, got_x, pos, vectors, weights, before, deps):
    head_size, shares = sizes
    n, width = got_x.shape
    gain, vx, vb, vh = vectors
    w_z, w_x, w_bc, w_dt, w_out = weights
    inner = w_z.shape[1]
    two = w_bc.shape[1]
    span = SPAN
    first, last = part
    steps = last - first
    blocks = n // span

    def rows(c):
        return pl.BlockSpec((span, c), lambda i, *_: (first + i, 0))

    def by_block(a, c):
        return pl.BlockSpec((1, a, c), lambda i, *_: (first + i, 0, 0))

    held = [w_z, w_x, w_bc, w_dt, w_out]
    ops = [got_x, pos, gain, vx, vb, vh]
    specs = [whole(o.shape) for o in ops]
    specs[1] = rows(1)
    ops += held
    specs += [pl.BlockSpec(memory_space=pl.ANY)] * len(held)
    cols = width // shares
    part_spec = pl.BlockSpec((shares // 2, span, cols), lambda i, *_: (0, i, 0))
    outs = [
        ((n, width), BF, rows(width)),
        ((width, n), BF, pl.BlockSpec((width, span), lambda i, *_: (0, first + i))),
        ((n, 1), F32, rows(1)),
        ((n, inner), F32, rows(inner)),
        ((n, inner), BF, rows(inner)),
        ((n, inner), F32, rows(inner)),
        ((n, inner), F32, rows(inner)),
        ((n, two), BF, rows(two)),
        ((n, two), F32, rows(two)),
        ((n, LANES), F32, rows(LANES)),
        ((n, inner), BF, rows(inner)),
        ((blocks, 8, span), F32, by_block(8, span)),
        ((blocks, two // 2, inner), F32, by_block(two // 2, inner)),
        ((shares // 2, steps * span, cols), BF, part_spec),
        ((shares // 2, steps * span, cols), BF, part_spec),
        ((8, inner), F32, whole((8, inner))),
        ((8, two), F32, whole((8, two))),
        ((two // 2, inner), F32, whole((two // 2, inner))),
    ]
    keep = []
    if before is not None:
        carry = list(before[15:18])
        ops += carry
        specs += [whole(o.shape) for o in carry]
        keep = list(enumerate(before[:13]))
    return call(
        functools.partial(fwd_kernel, sizes, first), ops, specs, outs, f"forward_{first}", grid=(steps,),
        scalars=scalars, deps=deps, keep=keep, flops=2 * steps * span * width * 5 * inner,
        scratch=[
            pltpu.VMEM((span + 8, inner), F32), pltpu.VMEM((span + 8, two), F32),
            *(pltpu.VMEM(w.shape, w.dtype) for w in held), pltpu.SemaphoreType.DMA((len(held),)),
        ],
    )


def dots_kernel(ids_ref, lengths_ref, pos_ref, dyn_ref, g_ref, stat_ref, out_ref, stat_out_ref):
    rows = pos_ref.shape[0]
    n = dyn_ref.shape[0]
    blocks, _, span = stat_ref.shape
    base = pl.program_id(0) * rows
    full = row_ends(ids_ref, lengths_ref)[-1]
    onehot = (pos_ref[...] == iota((rows, n), 1)) & (base + iota((rows, 1), 0) < full)
    dyn = dot(onehot.astype(F32).astype(BF), dyn_ref[...])
    out_ref[...] = dyn.astype(BF)
    inner_dot = jnp.sum(dyn * g_ref[...].astype(F32), axis=1, keepdims=True)
    as_row = jnp.broadcast_to(inner_dot, (rows, LANES)).T[0:8]
    for k in range(blocks):
        own = as_row[:, k * span : (k + 1) * span]
        stat_out_ref[k] = jnp.where(iota((8, span), 0) == 0, stat_ref[k], own)


def run_dots(scalars, pos, got_dyn, g, stat, deps):
    n, inner = got_dyn.shape
    span = 2 * SPAN
    rows = pl.BlockSpec((span, inner), lambda i, *_: (i, 0))
    stats = pl.BlockSpec((2, 8, SPAN), lambda i, *_: (i, 0, 0))
    return call(
        dots_kernel, [pos, got_dyn, g, stat],
        [pl.BlockSpec((span, 1), lambda i, *_: (i, 0)), whole((n, inner)), rows, stats],
        [((n, inner), BF, rows), (stat.shape, F32, stats)], "row_dots", grid=(n // span,), scalars=scalars, deps=deps,
        flops=2 * n * n * inner,
    )


def bwd_kernel(
    sizes, last, blocks, ids_ref, lengths_ref, stat_ref, dyn_ref, z_ref, xs_ref, px_ref, y_ref, bcv_ref, pbc_ref,
    dtr_ref, xd_ref, rin_ref, state_ref, gain_ref, wz_ref, wx_ref, wbc_ref, wdt_ref, vx_ref, vb_ref, vh_ref, *refs,
):
    head_size, shares = sizes
    newest = last == blocks
    if not newest:
        before, refs = refs[:8], refs[8:]
    (
        cols_ref, send_ref, keep_ref, *carry, xext, bext, extra,
    ) = refs
    xhead_ref, bhead_ref, dstate, across, accx_ref, accb_ref, acch_ref, accd_ref = carry
    span, inner = z_ref.shape
    width = xd_ref.shape[1]
    two = pbc_ref.shape[1]
    early = cols_ref.shape[1] - 2 * inner
    state_size = two // 2
    taps = vb_ref.shape[0] - 1
    group = LANES // head_size
    units = inner * shares
    step = pl.program_id(0)
    base = (last - 1 - step) * span
    ends = row_ends(ids_ref, lengths_ref)
    tensor = ids_ref[1]
    cxw_ref, cbw_ref = vx_ref, vb_ref
    skip, ggain = vx_ref[taps + 1 : taps + 2], vx_ref[taps + 2 : taps + 3]

    @pl.when(step == 0)
    def _():
        for k, ref in enumerate(carry):
            ref[...] = jnp.zeros_like(ref) if newest else before[k][...]
        extra[...] = jnp.zeros_like(extra)

    xext[span : span + 8] = xhead_ref[...]
    bext[span : span + 8] = bhead_ref[...]

    def add_row(ref, row, value):
        ref[row : row + 1] += jnp.sum(value, axis=0, keepdims=True)

    place = base + iota((span, 1), 0)
    stat_cols = stat_ref[0].T
    r_g = lax.rsqrt(stat_cols[:, 0:1] * (1.0 / units) + EPSILON)
    row_dot = stat_cols[:, 1:2] * (1.0 / units)
    z = z_ref[...]
    y = y_ref[...]
    dyn = dyn_ref[...].astype(F32)
    sig_z = jax.nn.sigmoid(z)
    silu_z = z * sig_z
    gated = y * silu_z
    normed = gated * r_g
    d_gated = r_g * (dyn * ggain) - normed * (r_g * r_g * row_dot)
    d_y = d_gated * silu_z
    dz = (d_gated * y * (sig_z * (1.0 + z * (1.0 - sig_z)))).astype(BF)
    cols_ref[:, early : early + inner] = dz
    add_row(accx_ref, taps + 2, dyn * normed)

    px = px_ref[...]
    sig_x = jax.nn.sigmoid(px)
    u = px * sig_x
    pbc = pbc_ref[...]
    sig_bc = jax.nn.sigmoid(pbc)
    bcc = pbc * sig_bc
    b_rows = bcc[:, :state_size].astype(BF)
    c_rows = bcc[:, state_size:].astype(BF)
    add_row(accx_ref, taps + 1, u * d_y)

    pre = dtr_ref[...] + vh_ref[0:1]
    dt = softplus(pre)
    rates = vh_ref[1:2]
    cum, head_decay, tail_decay, seg_c, seg_last = decays(ends, base, span, dt, rates)
    cum_t = cum.T
    dt_w, head_w, tail_w = widen([dt, head_decay, tail_decay], head_size, inner)
    udt = u * dt_w
    seg_r = seg_of(ends, base + iota((1, span), 1))
    counts = (seg_c == seg_r) & (iota((span, span), 1) >= iota((span, span), 0))
    never = jnp.where(counts, 0.0, NEVER)
    scores = dot_t(b_rows, c_rows)
    d_scores = jnp.zeros((span, span), F32)
    masks = half_masks(group)
    pieces = []
    for tile in range(inner // LANES):
        lanes = slice(tile * LANES, (tile + 1) * LANES)
        udt_block = udt[:, lanes]
        dy_block = d_y[:, lanes]
        dy_low = dy_block.astype(BF)
        total = None
        for k in range(group):
            head = tile * group + k
            decay = jnp.exp(cum_t[head : head + 1, :] - cum[:, head : head + 1] + never)
            d_scores = d_scores + decay * dot_t((udt_block * masks[k]).astype(BF), dy_low)
            term = dot((decay * scores).astype(BF), (dy_block * masks[k]).astype(BF))
            total = term if total is None else total + term
        pieces.append(total)
    in_block = jnp.concatenate(pieces, axis=1)
    d_state = dstate[...]
    d_state_low = d_state.astype(BF)
    entering = state_ref[0]
    entering_low = entering.astype(BF)
    at_end = dot(b_rows, d_state_low)
    at_start = dot(c_rows, entering_low)
    d_udt = in_block + at_end * tail_w
    from_start = (d_y * head_w).astype(BF)
    to_end = (udt * tail_w).astype(BF)
    d_c = dot(d_scores.T.astype(BF), b_rows) + dot_t(from_start, entering_low)
    d_b = dot(d_scores.astype(BF), c_rows) + dot_t(to_end, d_state_low)
    y_block = y - skip * u - at_start * head_w
    balance = d_y.astype(BF).astype(F32) * y_block - udt.astype(BF).astype(F32) * in_block
    balance = balance + from_start.astype(F32) * at_start - to_end.astype(F32) * at_end
    v_part = head_sums(u * d_udt, head_size, split2)
    mask_low = counts.astype(F32).astype(BF)
    d_la = fixed_sum(mask_low, head_sums(balance, head_size, split3))
    d_la = d_la + jnp.where(seg_c == seg_last, across[0:1], 0.0)
    d_dt = v_part + rates * d_la
    d_pre = d_dt * jax.nn.sigmoid(pre)
    add_row(acch_ref, 0, d_la * dt * rates)
    add_row(acch_ref, 1, d_pre)

    c_t = bcc[:, state_size:].T.astype(BF)
    d_enter = dot(c_t, from_start) + head_w[span - 1 : span] * d_state
    dstate[...] = d_enter
    crossing = jnp.sum(d_enter.astype(BF).astype(F32) * entering, axis=0, keepdims=True)
    across[...] = head_sums(jnp.broadcast_to(crossing, (8, inner)), head_size, split3)

    d_u = skip * d_y + dt_w * d_udt
    d_px = d_u * (sig_x * (1.0 + px * (1.0 - sig_x)))
    d_pbc = jnp.concatenate([d_b, d_c], axis=1) * (sig_bc * (1.0 + pbc * (1.0 - sig_bc)))
    xext[0:span] = d_px
    bext[0:span] = d_pbc
    seg_here = seg_of(ends, place)
    xs = xs_ref[...].astype(F32)
    bcv = bcv_ref[...].astype(F32)
    d_xs = cxw_ref[taps - 1 : taps] * d_px
    d_bc = cbw_ref[taps - 1 : taps] * d_pbc
    add_row(accx_ref, taps, d_px)
    add_row(accb_ref, taps, d_pbc)
    add_row(accx_ref, taps - 1, d_px * xs)
    add_row(accb_ref, taps - 1, d_pbc * bcv)
    for k in range(1, taps):
        later = place + k
        same = ((seg_of(ends, later) == seg_here) & (later < blocks * span)).astype(F32)
        tap = taps - 1 - k
        xk = xext[k : k + span] * same
        bk = bext[k : k + span] * same
        d_xs = d_xs + cxw_ref[tap : tap + 1] * xk
        d_bc = d_bc + cbw_ref[tap : tap + 1] * bk
        add_row(accx_ref, tap, xk * xs)
        add_row(accb_ref, tap, bk * bcv)
    xhead_ref[...] = d_px[0:8]
    bhead_ref[...] = d_pbc[0:8]
    dx_low = d_xs.astype(BF)
    dbc_low = d_bc.astype(BF)
    ddt_low = d_pre.astype(BF)
    cols_ref[:, 0:two] = dbc_low
    cols_ref[:, two : two + LANES] = ddt_low
    cols_ref[:, early + inner : early + 2 * inner] = dx_low
    for at in range(two + LANES, early, LANES):
        cols_ref[:, at : at + LANES] = jnp.zeros((span, LANES), BF)
    back = dot_t(dz, wz_ref[...]) + dot_t(dx_low, wx_ref[...])
    back = back + dot_t(ddt_low, wdt_ref[...]) + dot_t(dbc_low, wbc_ref[...])
    x_hat = xd_ref[...].astype(F32) * rin_ref[...]
    shared = back * x_hat
    add_row(accd_ref, 0, shared)
    inner_dot = jnp.sum(shared * gain_ref[...], axis=1, keepdims=True)
    low = back.astype(BF)
    cols = width // shares
    row = jnp.broadcast_to(inner_dot, (span, LANES)).T[0:1]
    for k in range(span // LANES):
        extra[k : k + 1] = row[:, k * LANES : (k + 1) * LANES]
    hand_out(send_ref, keep_ref, tensor, [low[:, j * cols : (j + 1) * cols] for j in range(shares)])
    more = extra[...].astype(BF)
    for part in range(shares // 2):
        send_ref[part, span : span + EXTRA, 0:LANES] = more
        keep_ref[part, span : span + EXTRA, 0:LANES] = more


def run_bwd(part, scalars, sizes, stat, dyn, kept, vectors, weights, before, deps):
    head_size, shares = sizes
    z, xs, px, y, bcv, pbc, dtr, xd, rin, states = kept
    w_z, w_x, w_bc, w_dt = weights
    n, inner = z.shape
    width = xd.shape[1]
    two = pbc.shape[1]
    span = SPAN
    first, last = part
    steps = last - first
    blocks = n // span
    cols = width // shares

    def rows(c):
        return pl.BlockSpec((span, c), lambda i, *_: (last - 1 - i, 0))

    def by_block(a, c):
        return pl.BlockSpec((1, a, c), lambda i, *_: (last - 1 - i, 0, 0))

    ops = [stat, dyn, z, xs, px, y, bcv, pbc, dtr, xd, rin, states]
    specs = [by_block(8, span), *(rows(o.shape[1]) for o in ops[1:11]), by_block(two // 2, inner)]
    fixed = [vectors[0], w_z, w_x, w_bc, w_dt, *vectors[1:]]
    part_spec = pl.BlockSpec((shares // 2, span + EXTRA, cols), lambda i, *_: (0, steps - 1 - i, 0))
    wide = -(-(2 * inner + two + LANES) // (2 * LANES)) * (2 * LANES)
    sums = [(8, inner), (8, two), (two // 2, inner), (8, LANES), (8, inner), (8, two), (8, LANES), (8, width)]
    outs = [
        ((n, wide), BF, rows(wide)),
        ((shares // 2, steps * (span + EXTRA), cols), BF, part_spec),
        ((shares // 2, steps * (span + EXTRA), cols), BF, part_spec),
        *((c, F32, whole(c)) for c in sums),
    ]
    keep = []
    if before is not None:
        fixed += before[3:]
        keep = list(enumerate(before[:1]))
    return call(
        functools.partial(bwd_kernel, sizes, last, blocks), ops + fixed, specs + [whole(o.shape) for o in fixed], outs,
        f"backward_{first}", grid=(steps,), scalars=scalars, deps=deps, keep=keep,
        flops=2 * steps * span * width * 6 * inner,
        scratch=[pltpu.VMEM((span + 8, inner), F32), pltpu.VMEM((span + 8, two), F32), pltpu.VMEM((EXTRA, LANES), F32)],
    )


def outer_kernel(groups, ids_ref, left_ref, right_ref, send_ref, keep_ref):
    each = groups // pl.num_programs(0)
    rows = left_ref.shape[0] // each
    low = dot(left_ref[...], right_ref[...]).astype(BF)
    at = pl.program_id(0) * each
    for i in range(each):
        place = ids_ref[0] ^ (at + i)

        @pl.when(place % 2 == 1)
        def _(i=i, place=place):
            send_ref[place // 2] = low[i * rows : (i + 1) * rows]

        @pl.when(place % 2 == 0)
        def _(i=i, place=place):
            keep_ref[place // 2] = low[i * rows : (i + 1) * rows]


def outer(ids, groups, left_t, right, first, count, deps=()):
    width, n = left_t.shape
    steps = 4
    rows = width // groups
    out = ((groups // 2, rows, count), BF, whole((groups // 2, rows, count)))
    return call(
        functools.partial(outer_kernel, groups), [left_t, right],
        [pl.BlockSpec((width // steps, n), lambda i, *_: (i, 0)), pl.BlockSpec((n, count), lambda *_: (0, first // count))],
        [out, out], "outer",
        grid=(steps,), scalars=[ids], deps=deps, flops=2 * n * width * count,
    )


def put_yn_kernel(units, ids_ref, lengths_ref, pos_ref, stat_ref, data_ref, out_ref, hot_ref, scale_ref):
    n = pos_ref.shape[1]
    blocks, _, span = stat_ref.shape

    @pl.when(pl.program_id(0) == 0)
    def _():
        hot_ref[...] = (pos_ref[...] == iota((n, n), 0)).astype(F32).astype(BF)
        full = row_ends(ids_ref, lengths_ref)[-1]
        for k in range(blocks):
            squares = stat_ref[k].T[:, 0:1]
            valid = k * span + iota((span, 1), 0) < full
            scale = lax.rsqrt(squares * (1.0 / units) + EPSILON)
            scale_ref[k * span : (k + 1) * span] = jnp.where(valid, scale, 0.0)

    yn = (data_ref[...].astype(F32) * scale_ref[...]).astype(BF)
    out_ref[...] = dot(hot_ref[...], yn).astype(BF)


def put_yn(scalars, units, pos, stat, g, deps):
    n, width = g.shape
    tile = next((t for t in (768, 384, 256) if width % t == 0), width)
    spec = pl.BlockSpec((n, tile), lambda i, *_: (0, i))
    return call(
        functools.partial(put_yn_kernel, units), [pos, stat, g], [whole(pos.shape), whole(stat.shape), spec],
        [((n, width), BF, spec)], "put_yn", grid=(width // tile,), scalars=scalars, deps=deps,
        scratch=[pltpu.VMEM((n, n), BF), pltpu.VMEM((n, 1), F32)], flops=2 * n * n * width,
    )[0]


def add_up(refs, counts):
    pieces, at = [], 0
    for count in counts:
        total = refs[at][0].astype(F32)
        for ref in refs[at + 1 : at + count]:
            total = total + ref[0].astype(F32)
        pieces.append(total)
        at += count
    return jnp.concatenate(pieces, axis=0)


def send_out_kernel(units, counts, ids_ref, lengths_ref, pos_ref, stat_ref, x_ref, *refs):
    *terms, out_ref, sq_ref = refs
    n = pos_ref.shape[1]
    blocks, _, span = stat_ref.shape
    mix = add_up(terms, counts)
    squares = jnp.concatenate([stat_ref[k].T[:, 0:1] for k in range(blocks)], axis=0)
    valid = (iota((n, 1), 0) < row_ends(ids_ref, lengths_ref)[-1]).astype(F32)
    mix = mix * (lax.rsqrt(squares * (1.0 / units) + EPSILON) * valid)
    x = x_ref[...].astype(F32)
    out = (x + mix).astype(BF)
    full = out.astype(F32)
    onehot = (pos_ref[...] == iota((n, n), 0)).astype(F32).astype(BF)
    out_ref[...] = dot(onehot, out).astype(BF)
    sq_ref[...] = jnp.zeros_like(sq_ref)
    for k, v in enumerate((x * x * valid, mix * mix, full * full * valid)):
        sq_ref[k : k + 1] = jnp.sum(v, axis=0, keepdims=True)


def send_dx_kernel(width, span, counts, pos_ref, x_ref, rin_ref, gain_ref, *refs):
    *terms, out_ref = refs
    n = pos_ref.shape[1]
    total = add_up(terms, counts)
    each = span + EXTRA
    d_h, dots = [], []
    for k in range(n // span):
        d_h.append(total[k * each : k * each + span])
        rows = total[k * each + span : k * each + span + 8, 0:LANES].T
        dots += [rows[:, i : i + 1] for i in range(span // LANES)]
    d_h, dots = jnp.concatenate(d_h, axis=0), jnp.concatenate(dots, axis=0)
    r_in = rin_ref[...]
    x_hat = x_ref[...].astype(F32) * r_in
    dx = (r_in * (d_h * gain_ref[...] - x_hat * (dots * (1.0 / width)))).astype(BF)
    onehot = (pos_ref[...] == iota((n, n), 0)).astype(F32).astype(BF)
    out_ref[...] = dot(onehot, dx).astype(BF)


def term_ops(groups_of_terms):
    ops = [t for terms in groups_of_terms for t in terms]
    specs = [pl.BlockSpec((1,) + o.shape[1:], lambda *_: (0, 0, 0)) for o in ops]
    return ops, specs, [len(terms) for terms in groups_of_terms]


def swap(v, axis, bit):
    size = lax.axis_size(axis)
    return lax.ppermute(v, axis, [(i, i ^ (1 << bit)) for i in range(size)])


def bits_of(axis):
    return lax.axis_size(axis).bit_length() - 1


class Halving:
    def __init__(self, send, keep, axis, order):
        self.axis, self.order = axis, order
        self.left = list(range(len(order) - 1, 0, -1))
        shape = (2,) * len(self.left) + keep.shape[1:]
        self.terms = [keep.reshape(shape)]
        self.sent = send.reshape(shape)
        self.got = None
        self.flat = [keep]
        self.at = 0

    def launch(self):
        if self.sent is not None:
            self.got = swap(self.sent, self.axis, self.order[self.at])
            self.sent = None
        return self

    def take(self):
        got, self.got = self.got, None
        self.terms.append(got)
        self.flat.append(got.reshape((-1,) + got.shape[len(self.left) :]))
        self.at += 1
        return self

    def advance(self):
        if self.left:
            dim = self.left.index(self.order[self.at])
            self.left.pop(dim)
            odd = [lax.index_in_dim(t, 1, dim, keepdims=False).astype(F32) for t in self.terms]
            self.sent = sum(odd[1:], odd[0]).astype(BF)
            self.terms = [lax.index_in_dim(t, 0, dim, keepdims=False) for t in self.terms]
        return self

    def land(self):
        return self if self.got is None else self.take().advance()

    def split(self, at, order):
        other = copy.copy(self)
        other.left, other.order = list(self.left), order
        other.terms = [t[..., at:] for t in self.terms]
        self.terms = [t[..., :at] for t in self.terms]
        return other

    def finish(self):
        while self.sent is not None or self.got is not None:
            self.launch().land()
        return self

    def total(self):
        self.finish()
        wide = [t.astype(F32) for t in self.terms]
        return sum(wide[1:], wide[0])


def fence(halvings, *values):
    held = [(h.sent, h.got) for h in halvings]
    flat, tree = jax.tree.flatten((held, values))
    held, values = tree.unflatten(lax.optimization_barrier(flat))
    for h, (sent, got) in zip(halvings, held, strict=True):
        h.sent, h.got = sent, got
    return values


def exchange(v, axis):
    groups = lax.axis_size(axis)
    rows = v.shape[0]
    parts = v.reshape((groups, rows // groups) + v.shape[1:])
    return lax.all_to_all(parts, axis, split_axis=0, concat_axis=0, tiled=True).reshape(v.shape)


def sum_at_once(v, axis):
    size = lax.axis_size(axis)
    others = [lax.ppermute(v, axis, [(i, i ^ k) for i in range(size)]) for k in range(1, size)]
    return sum((o.astype(F32) for o in others), v.astype(F32))


def pad_lanes(v):
    return jnp.pad(v, [(0, 0)] * (v.ndim - 1) + [(0, LANES - v.shape[-1])])


def local(
    stream, out_grad, seq_lengths, anchor, norm_gain, w_z, w_x, w_bc, w_dt, conv_x_w, conv_x_b, conv_bc_w,
    conv_bc_b, dt_bias, a_log, d_skip, gated_gain, w_out,
):
    groups = lax.axis_size("dp")
    shares = lax.axis_size("tensor")
    me = lax.axis_index("dp")
    tensor = lax.axis_index("tensor")
    n, width = stream.shape
    per = n // groups
    cols = width // shares
    first_col = tensor * cols
    inner = w_z.shape[1]
    heads = w_dt.shape[1]
    head_size = inner // heads
    two = w_bc.shape[1]
    taps = conv_x_w.shape[0]
    sizes = (head_size, shares)
    units = inner * shares
    ids = jnp.stack([me, tensor]).astype(I32)
    scalars = [ids, seq_lengths]
    tensor_order = list(range(bits_of("tensor")))
    dp_bits = bits_of("dp")
    order_a = list(range(dp_bits))
    order_b = order_a[:1] + order_a[1:][::-1]

    pos_row, pos_col, requests = find_places(anchor, n, per)
    wanted = lax.all_to_all(
        requests.reshape(groups, per), "dp", split_axis=0, concat_axis=0, tiled=True
    ).reshape(1, n)
    rows = stream.at[wanted.reshape(n)].get(mode="promise_in_bounds", unique_indices=True)
    got_x = exchange(rows, "dp")
    gain = norm_gain[None]
    vx = jnp.concatenate([conv_x_w, conv_x_b[None], jnp.repeat(d_skip, head_size)[None], gated_gain[None]])
    vb = jnp.concatenate([conv_bc_w, conv_bc_b[None]])
    vh = pad_lanes(jnp.stack([dt_bias, -jnp.exp(a_log)]))
    w_dt_pad = pad_lanes(w_dt)
    dy_t = out_grad.T
    gain_cols = lax.dynamic_slice_in_dim(norm_gain, first_col, cols, 0)[None]
    dy_cols = lax.dynamic_slice_in_dim(out_grad, first_col, cols, 1)
    d_yn_src = jnp.einsum("td,id->ti", out_grad, w_out, preferred_element_type=F32).astype(BF)
    dyn_send = move_rows(
        pick_kernel, wanted, d_yn_src, name="pick_dyn", deps=[gain, vx, vb, vh, w_dt_pad, dy_t, gain_cols, dy_cols]
    )
    got_dyn = exchange(dyn_send, "dp")

    vectors = (gain, vx, vb, vh)
    first, second = FORWARD
    weights = (w_z, w_x, w_bc, w_dt_pad)
    got = run_fwd(first, scalars, sizes, got_x, pos_col, vectors, (*weights, w_out), None, [dyn_send])
    mix_1 = Halving(got[13], got[14], "tensor", tensor_order).launch()
    got = run_fwd(second, scalars, sizes, got_x, pos_col, vectors, (*weights, w_out), got, [])
    mix_2 = Halving(got[13], got[14], "tensor", tensor_order)
    (xd, h_t, rin, z, xs, px, y, bcv, pbc, dtr, g, stat, states) = got[:13]
    (stat,) = fence([mix_1], stat)
    dyn, stat = run_dots(scalars, pos_col, got_dyn, g, stat, [])
    (stat,) = fence([mix_1], stat)
    mix_1.land()
    stat = sum_at_once(stat, "tensor")
    (stat,) = fence([mix_1, mix_2], stat)

    kept = (z, xs, px, y, bcv, pbc, dtr, xd, rin, states)
    yn_send = put_yn(scalars, units, pos_row, stat, g, [])
    yn_back = exchange(yn_send, "dp")
    mix_1.launch()
    mix_2.launch()
    got = run_bwd(BACKWARD[0], scalars, sizes, stat, dyn, kept, vectors, weights, None, [yn_send])
    back_1 = Halving(got[1], got[2], "tensor", tensor_order)
    yn_back, carry = fence([mix_1, mix_2, back_1], yn_back, got[3:])
    got = [*got[:3], *carry]
    mix_1.land()
    mix_2.land()
    back_1.launch()
    mix_1.launch()
    mix_2.launch()
    yn_src = move_rows(put_kernel, wanted, yn_back, name="place_yn")
    h_out = Halving(*outer(ids, groups, dy_t, yn_src, 0, inner), "dp", order_b)
    got = run_bwd(BACKWARD[1], scalars, sizes, stat, dyn, kept, vectors, weights, got, [h_out.sent])
    h_out.launch().land()
    back_2 = Halving(got[1], got[2], "tensor", tensor_order)
    grad_cols, tail = got[0], got[7:]
    grad_cols, tail, xd = fence([mix_1, mix_2, back_1, back_2, h_out], grad_cols, tail, xd)
    acc_x, acc_b, acc_h, acc_d = tail

    mix_1.land().finish()
    mix_2.land().finish()
    back_1.land()
    back_2.launch()
    back_1.launch()
    h_out.launch()
    half = grad_cols.shape[1] // 2
    x_cols = lax.dynamic_slice_in_dim(xd, first_col, cols, 1)
    h_a = Halving(*outer(ids, groups, h_t, grad_cols, 0, 2 * half), "dp", order_a)
    (x_cols,) = fence([back_1, back_2, h_out, h_a], x_cols)

    back_2.land().launch()
    back_1.land().finish()
    h_a.launch()
    ops, specs, counts = term_ops([mix_1.flat, mix_2.flat])
    ops = [pos_row, stat, x_cols, *ops]
    out_send, squares = call(
        functools.partial(send_out_kernel, units, counts), ops, [*(whole(o.shape) for o in ops[:3]), *specs],
        [((n, cols), BF, whole((n, cols))), ((8, cols), F32, whole((8, cols)))], "send_out", scalars=scalars,
        flops=2 * n * n * cols,
    )
    flat = [acc_x, acc_h, acc_b[: taps + 1], acc_d[0], jnp.sum(squares, axis=1)]
    flat = [f.reshape(-1) for f in flat]
    lens = [f.shape[0] for f in flat]
    small = jnp.concatenate(flat).astype(BF)
    small = jnp.pad(small, (0, -sum(lens) % (16 * cols))).reshape(1, -1, cols)
    small = jnp.broadcast_to(small, (groups,) + small.shape[1:])
    sent = jnp.concatenate([out_send.reshape(groups, per, cols), small], axis=1)
    out_back = lax.all_to_all(sent, "dp", split_axis=0, concat_axis=0, tiled=True)
    (x_cols,) = fence([back_2, h_a], x_cols)

    back_2.land().finish()
    h_a.take()
    h_b = h_a.split(half, order_b)
    h_a.advance().launch()
    h_b.advance().launch()
    h_out.land().launch()
    back_ops, back_specs, back_counts = term_ops([back_2.flat, back_1.flat])
    ops = [pos_row, x_cols, rin, gain_cols]
    dx_send = call(
        functools.partial(send_dx_kernel, width, SPAN, back_counts), [*ops, *back_ops],
        [*(whole(o.shape) for o in ops), *back_specs],
        [((n, cols), BF, whole((n, cols)))], "send_dx", flops=2 * n * n * cols,
    )[0]
    dx_send, out_back = fence([], dx_send, out_back)

    dx_back = exchange(dx_send, "dp")
    out_rows = out_back[:, :per].reshape(n, cols)
    out_final = move_rows(put_kernel, wanted, out_rows, name="place_out")
    small = jnp.sum(out_back[:, per:].astype(F32), axis=0).reshape(-1)
    out_final, small, dy_cols = fence([h_a, h_b, h_out], out_final, small, dy_cols)

    h_a.land().launch()
    h_b.land().launch()
    h_out.land()
    dx_final = move_rows(put_add_kernel, wanted, dx_back, dy_cols, name="place_dx")
    (dx_final,) = fence([h_a, h_b], dx_final)

    g_out = h_out.total()
    g_a = h_a.total()
    g_b = h_b.total()
    early = 2 * half - 2 * inner
    g_dt = g_a[:, two : two + heads]
    g_z = jnp.concatenate([g_a[:, early:], g_b[:, : early + inner - half]], axis=1)
    g_x = g_b[:, early + inner - half :]

    own = lens[0] + lens[1]
    s_x = small[: lens[0]].reshape(acc_x.shape)
    s_h = small[lens[0] : own].reshape(acc_h.shape)
    both = small[own : sum(lens)]
    both = jnp.pad(both, (0, -both.shape[0] % (8 * two))).reshape(-1, two)
    both = sum_at_once(jnp.concatenate([g_a[:, :two], both]).astype(BF), "tensor")
    g_bc = both[: g_a.shape[0]]
    both = both[g_a.shape[0] :].reshape(-1)
    s_b = both[: lens[2]].reshape(taps + 1, two)
    s_d = both[lens[2] : lens[2] + lens[3]]
    s_sq = both[lens[2] + lens[3] : lens[2] + lens[3] + 3]
    g_gain = lax.dynamic_slice_in_dim(s_d, first_col, cols, 0)
    rms = jnp.sqrt(s_sq / (jnp.sum(seq_lengths).astype(F32) * width))
    g_skip = jnp.sum(s_x[taps + 1].reshape(heads, head_size), axis=1)
    return (
        out_final, dx_final, g_gain, g_z, g_x, g_bc, g_dt, s_x[:taps], s_x[taps], s_b[:taps], s_b[taps],
        s_h[1, :heads], s_h[0, :heads], g_skip, s_x[taps + 2], g_out.T, rms,
    )


def solution(mesh):
    in_specs = (
        P("dp", None), P("dp", None), P(), P("dp"), P(), P(None, "tensor"), P(None, "tensor"), P(),
        P(None, "tensor"), P(None, "tensor"), P("tensor"), P(), P(), P("tensor"), P("tensor"), P("tensor"),
        P("tensor"), P("tensor", None),
    )
    out_specs = (
        P("dp", "tensor"), P("dp", "tensor"), P("tensor"), P("dp", "tensor"), P("dp", "tensor"), P("dp", None),
        P("dp", "tensor"), P(None, "tensor"), P("tensor"), P(), P(), P("tensor"), P("tensor"), P("tensor"),
        P("tensor"), P("tensor", "dp"), P(),
    )
    return jax.shard_map(local, mesh=mesh, in_specs=in_specs, out_specs=out_specs, check_vma=False)
```
